32 devices in a mesh: ctx: 8 (over y, x, core), seq: 4 (over z).
Axes of the slice: x: 2, y: 2, z: 4, core: 2. Of those that a mesh axis runs over, the one named last changes fastest.
Arguments:
- layer_input: bfloat16 [16, 2208, 256], P('ctx', 'seq'), may hold values from -6 to 6
- gene_kept: int32 [16, 2208], P('ctx'), may hold values 0 or 1
- attn_gain: bfloat16 [256], replicated, may hold values from 0.5 to 1.5
- attn_shift: bfloat16 [256], replicated, may hold values from -1.5 to 1.5
- w_query: bfloat16 [256, 256], replicated, may hold values from -0.5 to 0.5
- w_key: bfloat16 [256, 256], replicated, may hold values from -0.5 to 0.5
- w_value: bfloat16 [256, 256], replicated, may hold values from -0.375 to 0.375
- w_out: bfloat16 [256, 256], replicated, may hold values from -2 to 2
- out_bias: bfloat16 [256], replicated, may hold values from -1.5 to 1.5
- mlp_gain: bfloat16 [256], replicated, may hold values from 0.5 to 1.5
- mlp_shift: bfloat16 [256], replicated, may hold values from -1.5 to 1.5
- w_up: bfloat16 [256, 1024], replicated, may hold values from -0.375 to 0.375
- up_bias: bfloat16 [1024], replicated, may hold values from -2.5 to 2.5
- w_down: bfloat16 [1024, 256], replicated, may hold values from -0.25 to 0.25
- down_bias: bfloat16 [256], replicated, may hold values from -1.5 to 1.5
- cotangent: float32 [16, 2208, 256], P('ctx', 'seq'), may hold values from -16 to 16
Outputs:
- block_output: bfloat16 [16, 2208, 256], P('ctx', 'seq')
- input_grad: float32 [16, 2208, 256], P('ctx', 'seq')
- grad_attn_gain: float32 [256], replicated
- grad_attn_shift: float32 [256], replicated
- grad_w_query: float32 [256, 256], replicated
- grad_w_key: float32 [256, 256], replicated
- grad_w_value: float32 [256, 256], replicated
- grad_w_out: float32 [256, 256], replicated
- grad_out_bias: float32 [256], replicated
- grad_mlp_gain: float32 [256], replicated
- grad_mlp_shift: float32 [256], replicated
- grad_w_up: float32 [256, 1024], replicated
- grad_up_bias: float32 [1024], replicated
- grad_w_down: float32 [1024, 256], replicated
- grad_down_bias: float32 [256], replicated
The draws below stay inside these ranges and needn't reach their ends.
All inputs are finite; a program needn't handle non-finite values. No bound on the sum of `gene_kept` on one device may be relied on, other than what follows from the above.
Results may differ from the reference program's by a relative error of at most 0.014.
The reference program's roundings to bfloat16 on the way count: a program that leaves them out, or rounds other values in their place, can miss the bound.
Values may be sent and summed in bfloat16 or wider, within the bound.
A program may use at most 128 MiB of HBM per device.

```python
import math
import jax
import jax.numpy as jnp
from jax import lax

D = 256
FF = 1024
HEADS = 4
CLS = 8
LEN = 2208
CONTEXTS = 16


def draw_cotangent(key, part):
    key = jax.random.fold_in(key, 7)
    key_field, key_level = jax.random.split(key, 2)
    field = jax.random.truncated_normal(key_field, -4.0, 4.0, (CONTEXTS, LEN, D), jnp.float32)
    levels = jnp.exp(jax.random.uniform(key_level, (CONTEXTS, 1, 1), jnp.float32, math.log(0.3), math.log(3.0)))
    return jnp.clip(field * levels, -16.0, 16.0)


def plant(drawn, key, smallest, top_value):
    place = [jax.random.randint(jax.random.fold_in(key, axis), (), 0, length) for axis, length in enumerate(drawn.shape)]
    widest = drawn.shape.index(max(drawn.shape))
    next_to = place[:widest] + [(place[widest] + 1) % drawn.shape[widest]] + place[widest + 1:]
    return drawn.at[tuple(place)].set(smallest).at[tuple(next_to)].set(top_value)


def block_scale(stream_key, shape, pieces, smallest, high):
    def one(dim, parts):
        draws = jax.random.uniform(jax.random.fold_in(jax.random.fold_in(stream_key, 6), dim), (parts,), jnp.float32, smallest / len(pieces), high / len(pieces))
        return jnp.repeat(jnp.exp(draws), shape[dim] // parts).reshape((-1,) + (1,) * (len(shape) - dim - 1))

    factor_of = one(*pieces[0])
    for cut in pieces[1:]:
        factor_of = factor_of * one(*cut)
    return factor_of


def scatter_about(rng, dims, scale, most, cuts=(), held_as=jnp.bfloat16):
    array = jax.random.normal(rng, dims, jnp.float32) * scale
    if len(cuts) > 0:
        array = block_scale(rng, dims, cuts, -0.22, 0.18) * array
    return jnp.clip(array, min=-most, max=most).astype(held_as)


def setup_inputs(seed: int = 0) -> dict:
    keys = jax.random.split(jax.random.key(seed), 17)
    return {
        "layer_input": scatter_about(keys[0], (CONTEXTS, LEN, D), 1.0, 6.0, ((0, 8), (1, 4))),
        "gene_kept": plant((jax.random.randint(keys[1], (CONTEXTS, LEN), 0, 4) < 3).astype(jnp.int32), jax.random.fold_in(keys[1], 1), 0, 1),
        "attn_gain": jnp.clip(1.0 + 0.1 * jax.random.normal(keys[2], (D,), jnp.float32), 0.5, 1.5).astype(jnp.bfloat16),
        "attn_shift": scatter_about(keys[3], (D,), 0.3, 1.5),
        "w_query": scatter_about(keys[4], (D, D), (D // 2) ** -0.5, 0.5),
        "w_key": scatter_about(keys[5], (D, D), (D // 2) ** -0.5, 0.5),
        "w_value": scatter_about(keys[6], (D, D), D ** -0.5, 0.375),
        "w_out": scatter_about(keys[7], (D, D), (D // 32) ** -0.5, 2.0),
        "out_bias": scatter_about(keys[8], (D,), 0.3, 1.5),
        "mlp_gain": jnp.clip(1.0 + 0.1 * jax.random.normal(keys[9], (D,), jnp.float32), 0.5, 1.5).astype(jnp.bfloat16),
        "mlp_shift": scatter_about(keys[10], (D,), 0.3, 1.5),
        "w_up": scatter_about(keys[11], (D, FF), D ** -0.5, 0.375),
        "up_bias": scatter_about(keys[12], (FF,), 0.5, 2.5),
        "w_down": scatter_about(keys[13], (FF, D), (FF // 2) ** -0.5, 0.25),
        "down_bias": scatter_about(keys[14], (D,), 0.3, 1.5),
        "cotangent": draw_cotangent(jax.random.fold_in(keys[16], 71), 0),
    }


@jax.custom_vjp
def low(v):
    return lax.optimization_barrier(v.astype(jnp.bfloat16)).astype(jnp.float32)

@jax.custom_vjp
def low_back(v):
    return v

def low_keep(v):
    return (low(v), None)

def low_pass(kept, grad):
    return (grad,)

def back_keep(v):
    return (v, None)

def back_low(kept, grad):
    return (low(grad),)
low.defvjp(low_keep, low_pass)
low_back.defvjp(back_keep, back_low)

def both_ways(values_in):
    return low_back(low(values_in))

def matmul(left_side, right_side):
    return jnp.dot(left_side, right_side, precision=lax.Precision.HIGHEST)

def layer_norm(rows_in, gain_vec, shift_vec):
    average = lax.optimization_barrier(jnp.mean(rows_in, axis=-1, keepdims=True))
    centred = rows_in - average
    spread = lax.optimization_barrier(jnp.mean(centred * centred, axis=-1, keepdims=True))
    return centred * lax.rsqrt(spread + 1e-05) * gain_vec + shift_vec

def one_context(inputs, kept_row, weight_set):
    attn_gain, attn_shift, w_query, w_key, w_value, w_out, out_bias, mlp_gain, mlp_shift, w_up, up_bias, w_down, down_bias = weight_set
    head_dim = D // HEADS
    score_scale = 1.0 / math.sqrt(head_dim)
    normed = low(layer_norm(inputs, attn_gain, attn_shift))
    query_rows = both_ways(matmul(normed, w_query)).reshape(LEN, HEADS, head_dim)
    key_rows = both_ways(matmul(normed, w_key)).reshape(LEN, HEADS, head_dim)
    value_rows = both_ways(matmul(normed, w_value)).reshape(LEN, HEADS, head_dim)
    scores = low_back(jnp.einsum('qhd,khd->hqk', query_rows, key_rows, precision=lax.Precision.HIGHEST) * score_scale)
    usable = (kept_row == 1) | (jnp.arange(LEN) < CLS)
    scores = jnp.where(usable[None, None, :], scores, -1000000000.0)
    probs = low(jax.nn.softmax(scores, axis=-1))
    attended = both_ways(jnp.einsum('hqk,khd->qhd', probs, value_rows, precision=lax.Precision.HIGHEST).reshape(LEN, D))
    branch = low_back(matmul(attended, w_out) + out_bias)
    middle = inputs + branch
    normed_two = low(layer_norm(middle, mlp_gain, mlp_shift))
    hidden = low_back(matmul(normed_two, w_up) + up_bias)
    activated = low(jax.nn.gelu(hidden, approximate=False))
    return middle + low_back(matmul(activated, w_down) + down_bias)

def reference(layer_input, gene_kept, attn_gain, attn_shift, w_query, w_key, w_value, w_out, out_bias, mlp_gain, mlp_shift, w_up, up_bias, w_down, down_bias, cotangent):
    weight_set = tuple((weight_arg.astype(jnp.float32) for weight_arg in (attn_gain, attn_shift, w_query, w_key, w_value, w_out, out_bias, mlp_gain, mlp_shift, w_up, up_bias, w_down, down_bias)))
    step_fn = jax.checkpoint(one_context)

    def forward(inputs, weights_in):
        return lax.map(lambda operand_pair: step_fn(operand_pair[0], operand_pair[1], weights_in), (inputs, gene_kept))
    result, pullback = jax.vjp(forward, layer_input.astype(jnp.float32), weight_set)
    input_grad, weight_grads = pullback(cotangent.astype(jnp.float32))
    grad_attn_gain, grad_attn_shift, grad_w_query, grad_w_key, grad_w_value, grad_w_out, grad_out_bias, grad_mlp_gain, grad_mlp_shift, grad_w_up, grad_up_bias, grad_w_down, grad_down_bias = weight_grads
    return (result.astype(jnp.bfloat16), input_grad, grad_attn_gain, grad_attn_shift, grad_w_query, grad_w_key, grad_w_value, grad_w_out, grad_out_bias, grad_mlp_gain, grad_mlp_shift, grad_w_up, grad_up_bias, grad_w_down, grad_down_bias)
```

```python
import math
from functools import partial

import jax
import jax.numpy as jnp
from jax import lax
from jax.experimental import pallas as pl
from jax.experimental.pallas import tpu as pltpu
from jax.sharding import PartitionSpec as P

bf16 = jnp.bfloat16
f32 = jnp.float32
HEADS = 4
CLS = 8
TILE = 256
MASKED = -8.0e9
NN = (((1,), (0,)), ((), ()))
NT = (((1,), (1,)), ((), ()))
TN = (((0,), (0,)), ((), ()))
TT = (((0,), (1,)), ((), ()))
MESH = pl.DeviceIdType.MESH


def mm(a, b, dims=NN):
    return lax.dot_general(a, b, dims, preferred_element_type=f32)


def norm_parts(z):
    average = jnp.mean(z, axis=-1, keepdims=True)
    centred = z - average
    spread = jnp.mean(centred * centred, axis=-1, keepdims=True)
    rstd = lax.rsqrt(spread + 1e-05)
    return centred * rstd, rstd


def norm_back(f, n, rstd):
    mean_f = jnp.mean(f, axis=-1, keepdims=True)
    mean_fn = jnp.mean(f * n, axis=-1, keepdims=True)
    return rstd * (f - mean_f - n * mean_fn)


def normal_parts(u):
    bell = jnp.exp2(u * u * (-0.5 * math.log2(math.e)))
    t = 1.0 / (1.0 + (0.3275911 / math.sqrt(2.0)) * jnp.abs(u))
    poly = 1.061405429 * t - 1.453152027
    poly = poly * t + 1.421413741
    poly = poly * t - 0.284496736
    poly = (poly * t + 0.254829592) * t
    tail = 0.5 * poly * bell
    return jnp.where(u < 0, tail, 1.0 - tail), bell * (1.0 / math.sqrt(2.0 * math.pi))


def colsum(z):
    return jnp.sum(z, axis=0, keepdims=True)


def layer_kernel(
    x_ref, keep_ref, cot_ref,
    ag_ref, as_ref, wq_ref, wk_ref, wv_ref, wo_ref, ob_ref,
    mg_ref, ms_ref, wu_ref, ub_ref, wd_ref, db_ref,
    out_ref, dmid_ref, esib_ref, eown_ref, grads_ref, small_ref,
    n_ref, qaug, kaug, vaug, kt, vtaug, prob, s_ref, ot_ref, rl_ref,
    att_t, att, nt_ref, act_ref, gh_ref, gml_ref, gaug, gatt_t, dk_ref, dv_ref,
):
    rows, width = x_ref.shape
    own = rows // 2
    hd = width // HEADS
    pairs = HEADS // 2
    pw = 2 * hd
    head_cols = qaug.shape[2] // 2
    cols = 2 * head_cols
    tiles = cols // TILE
    scale = 1.0 / math.sqrt(hd)
    expo = scale * math.log2(math.e)
    ff = wu_ref.shape[1]
    chunk = own // 3

    gain = ag_ref[...].astype(f32)
    shift = as_ref[...].astype(f32)

    def norm_rows(i, carry):
        at = pl.ds(pl.multiple_of(i * chunk, 16), chunk)
        n, _ = norm_parts(x_ref[at, :].astype(f32))
        low = (n * gain + shift).astype(bf16)
        n_ref[at, :] = low
        k = mm(low, wk_ref[...]).astype(bf16)
        v = mm(low, wv_ref[...]).astype(bf16)
        for p in range(pairs):
            kaug[p, at, 0:pw] = k[:, p * pw:(p + 1) * pw]
            vaug[p, at, 0:pw] = v[:, p * pw:(p + 1) * pw]
        return carry

    lax.fori_loop(0, rows // chunk, norm_rows, 0)
    lane = lax.broadcasted_iota(jnp.int32, (rows, pw), 1)
    bias = jnp.where(lane == 0, keep_ref[...], 0.0).astype(bf16)
    ones = jnp.where(lane < 2, 1.0, 0.0).astype(bf16)
    for p in range(pairs):
        kaug[p, :, pw:2 * pw] = bias
        vaug[p, :, pw:2 * pw] = ones
    sub = lax.broadcasted_iota(jnp.int32, (16, rows), 0)
    kt[...] = mm(wk_ref[...], n_ref[...], TT).astype(bf16)
    vt = mm(wv_ref[...], n_ref[...], TT).astype(bf16)
    for p in range(pairs):
        vtaug[p, 0:pw, :] = vt[p * pw:(p + 1) * pw, :]
        vtaug[p, pw:pw + 16, :] = jnp.where(sub == 0, 1.0, 0.0).astype(bf16)
    qt = mm(wq_ref[...], n_ref[0:own, :], TT).astype(bf16)
    qaug[...] = jnp.zeros_like(qaug)
    gaug[...] = jnp.zeros_like(gaug)
    sub = lax.broadcasted_iota(jnp.int32, (16, cols), 0)
    for p in range(pairs):
        for h in range(2):
            qaug[p, h * hd:(h + 1) * hd, h * head_cols:h * head_cols + own] = qt[p * pw + h * hd:p * pw + (h + 1) * hd, :]
        qaug[p, pw:pw + 16, :] = jnp.where(sub == 0, 1.0, 0.0).astype(bf16)

    def forward(i, carry):
        p = i // tiles
        at = pl.ds(pl.multiple_of((i % tiles) * TILE, TILE), TILE)
        s_ref[...] = mm(kaug[p], qaug[p, :, at])
        top = jnp.max(s_ref[...], axis=0, keepdims=True)
        prob[p, :, at] = jnp.exp2((s_ref[...] - top) * expo).astype(bf16)
        o = mm(vtaug[p], prob[p, :, at])
        rl = 1.0 / o[pw:pw + 1]
        ot_ref[p, :, at] = o[0:pw] * rl
        rl_ref[p, :, at] = rl
        return carry

    lax.fori_loop(0, pairs * tiles, forward, 0)
    for p in range(pairs):
        for h in range(2):
            att_t[p * pw + h * hd:p * pw + (h + 1) * hd, :] = ot_ref[
                p, h * hd:(h + 1) * hd, h * head_cols:h * head_cols + own
            ].astype(bf16)
    att[...] = jnp.transpose(att_t[...])

    gain2 = mg_ref[...].astype(f32)
    shift2 = ms_ref[...].astype(f32)
    out_bias = ob_ref[...].astype(f32)
    up_bias = ub_ref[...].astype(f32)
    down_bias = db_ref[...].astype(f32)

    def mlp(i, carry):
        g_up, g_down, g_out, g_gain, g_shift = carry
        at = pl.ds(pl.multiple_of(i * chunk, 16), chunk)
        middle = x_ref[at, :].astype(f32) + (mm(att[at, :], wo_ref[...]) + out_bias)
        n, rstd = norm_parts(middle)
        low = (n * gain2 + shift2).astype(bf16)
        nt_ref[at, :] = low
        hidden = mm(low, wu_ref[...]) + up_bias
        dist, dens = normal_parts(hidden)
        act = (hidden * dist).astype(bf16)
        act_ref[at, :] = act
        out_ref[at, :] = (middle + (mm(act, wd_ref[...]) + down_bias)).astype(bf16)
        cot = cot_ref[at, :]
        gh = ((dist + hidden * dens) * mm(cot, wd_ref[...], NT)).astype(bf16)
        gh_ref[at, :] = gh
        e = mm(gh, wu_ref[...], NT)
        back = norm_back(e * gain2, n, rstd)
        dmid_ref[at, :] = back
        cot = cot.astype(f32)
        gml = (cot + back).astype(bf16)
        gml_ref[at, :] = gml
        return (
            g_up + colsum(gh.astype(f32)), g_down + colsum(cot), g_out + colsum(gml.astype(f32)),
            g_gain + colsum(e * n), g_shift + colsum(e),
        )

    zero = jnp.zeros((1, width), f32)
    sums = lax.fori_loop(0, 3, mlp, (jnp.zeros((1, ff), f32), zero, zero, zero, zero))
    small_ref[0:1, :] = sums[1]
    small_ref[1:2, :] = sums[2]
    small_ref[2:3, :] = sums[3]
    small_ref[3:4, :] = sums[4]
    for j in range(ff // width):
        small_ref[4 + j:5 + j, :] = sums[0][:, j * width:(j + 1) * width]
    grads_ref[0:ff, :] = mm(act_ref[...], cot_ref[...], TN)
    grads_ref[ff:2 * ff, :] = mm(gh_ref[...], nt_ref[...], TN)
    grads_ref[2 * ff:2 * ff + width, :] = mm(att_t[...], gml_ref[...])

    gatt_t[...] = mm(wo_ref[...], gml_ref[...], NT).astype(bf16)
    sub = lax.broadcasted_iota(jnp.int32, (16, own), 0)
    for p in range(pairs):
        for h in range(2):
            lanes = slice(h * head_cols, h * head_cols + own)
            g = gatt_t[p * pw + h * hd:p * pw + (h + 1) * hd, :].astype(f32)
            g = (g * rl_ref[p, :, lanes]).astype(bf16)
            gaug[p, h * hd:(h + 1) * hd, lanes] = g
            delta = -colsum(g.astype(f32) * ot_ref[p, h * hd:(h + 1) * hd, lanes])
            coarse = delta.astype(bf16).astype(f32)
            fine = delta - coarse
            gaug[p, pw:pw + 16, lanes] = jnp.where(sub == 0, coarse, jnp.where(sub == 1, fine, 0.0)).astype(bf16)

    for p in range(pairs):
        dv_ref[:, p * pw:(p + 1) * pw] = mm(prob[p], gaug[p, 0:pw, :], NT).astype(bf16)

    def backward(i, carry):
        p = i // tiles
        at = pl.ds(pl.multiple_of((i % tiles) * TILE, TILE), TILE)
        ds = prob[p, :, at] * mm(vaug[p], gaug[p, :, at]).astype(bf16)
        prob[p, :, at] = ds
        dq = mm(kt[pl.ds(pl.multiple_of(p * pw, pw), pw), :], ds)
        ot_ref[p, :, at] = dq * scale
        return carry

    lax.fori_loop(0, pairs * tiles, backward, 0)
    for p in range(pairs):
        dk_ref[:, p * pw:(p + 1) * pw] = (mm(prob[p], qaug[p, 0:pw, :], NT) * scale).astype(bf16)

    for p in range(pairs):
        for h in range(2):
            att_t[p * pw + h * hd:p * pw + (h + 1) * hd, :] = ot_ref[
                p, h * hd:(h + 1) * hd, h * head_cols:h * head_cols + own
            ].astype(bf16)
    dq = jnp.transpose(att_t[...])
    base = 2 * ff + width
    grads_ref[base:base + width, :] = mm(n_ref[0:own, :], dq, TN)
    grads_ref[base + width:base + 2 * width, :] = mm(n_ref[...], dk_ref[...], TN)
    grads_ref[base + 2 * width:base + 3 * width, :] = mm(n_ref[...], dv_ref[...], TN)
    esib_ref[...] = (mm(dk_ref[own:rows, :], wk_ref[...], NT) + mm(dv_ref[own:rows, :], wv_ref[...], NT)).astype(bf16)
    eown_ref[...] = (
        mm(dq, wq_ref[...], NT) + mm(dk_ref[0:own, :], wk_ref[...], NT) + mm(dv_ref[0:own, :], wv_ref[...], NT)
    )


def final_kernel(x_ref, eown_ref, esib_ref, dmid_ref, ag_ref, res_ref, small_ref):
    n, rstd = norm_parts(x_ref[...].astype(f32))
    e = eown_ref[...] + esib_ref[...].astype(f32)
    small_ref[0:1, :] = colsum(e * n)
    small_ref[1:2, :] = colsum(e)
    res_ref[...] = (dmid_ref[...] + norm_back(e * ag_ref[...].astype(f32), n, rstd)).astype(bf16)


def reduce_kernel(nbits, seqs, g_ref, small_ref, res_ref, sres_ref, acc, send, recv, gat, ssend, srecv, ssem, rsem):
    c = lax.axis_index("ctx")
    s = lax.axis_index("seq")
    rows = g_ref.shape[0]
    bar = pltpu.get_barrier_semaphore()
    for b in range(nbits):
        pl.semaphore_signal(bar, inc=1, device_id=(c ^ (1 << b), s), device_id_type=MESH)
    for d in range(1, seqs):
        pl.semaphore_signal(bar, inc=1, device_id=(c, lax.rem(s + d, seqs)), device_id_type=MESH)
    pl.semaphore_wait(bar, nbits + seqs - 1)
    off = jnp.int32(0)
    size = rows
    roff = 0
    offs = []
    for b in range(nbits):
        half = size // 2
        mine = lax.rem(c // (1 << b), 2)
        peer = (c ^ (1 << b), s)
        src = acc if b else g_ref
        away = pl.multiple_of(off + (1 - mine) * half, 16)
        keep = pl.multiple_of(off + mine * half, 16)
        send[pl.ds(roff, half), :] = src[pl.ds(away, half), :].astype(bf16)
        ssend[b] = (sres_ref if b else small_ref)[...].astype(bf16)
        cp = pltpu.make_async_remote_copy(
            src_ref=send.at[pl.ds(roff, half)], dst_ref=recv.at[pl.ds(roff, half)],
            send_sem=ssem.at[2 * b], recv_sem=rsem.at[2 * b], device_id=peer, device_id_type=MESH)
        cs = pltpu.make_async_remote_copy(
            src_ref=ssend.at[b], dst_ref=srecv.at[b],
            send_sem=ssem.at[2 * b + 1], recv_sem=rsem.at[2 * b + 1], device_id=peer, device_id_type=MESH)
        cp.start()
        cs.start()
        cp.wait()
        cs.wait()
        acc[pl.ds(keep, half), :] = src[pl.ds(keep, half), :] + recv[pl.ds(roff, half), :].astype(f32)
        sres_ref[...] = ssend[b].astype(f32) + srecv[b].astype(f32)
        offs.append((off, half, mine))
        off = keep
        roff += half
        size = half
    piece = size // seqs
    k = 2 * nbits
    send[pl.ds(roff, size), :] = acc[pl.ds(off, size), :].astype(bf16)
    ssend[nbits] = sres_ref[...].astype(bf16)
    cps = []
    for d in range(1, seqs):
        t = lax.rem(s + d, seqs)
        cps.append(pltpu.make_async_remote_copy(
            src_ref=send.at[pl.ds(pl.multiple_of(roff + t * piece, 16), piece)],
            dst_ref=recv.at[pl.ds(roff + (d - 1) * piece, piece)],
            send_sem=ssem.at[k], recv_sem=rsem.at[k], device_id=(c, t), device_id_type=MESH))
        cps.append(pltpu.make_async_remote_copy(
            src_ref=ssend.at[nbits], dst_ref=srecv.at[nbits + d - 1],
            send_sem=ssem.at[k + 1], recv_sem=rsem.at[k + 1], device_id=(c, t), device_id_type=MESH))
        k += 2
    for cp in cps:
        cp.start()
    for cp in cps:
        cp.wait()
    mine_at = pl.multiple_of(off + s * piece, 16)
    total = acc[pl.ds(mine_at, piece), :]
    for d in range(1, seqs):
        total += recv[pl.ds(roff + (d - 1) * piece, piece), :].astype(f32)
    gat[pl.ds(mine_at, piece), :] = total.astype(bf16)
    shares = [ssend[nbits].astype(f32)] + [srecv[nbits + d - 1].astype(f32) for d in range(1, seqs)]
    stotal = jnp.zeros_like(shares[0])
    for o in range(seqs):
        which = lax.rem(s - o + seqs, seqs)
        for d in range(seqs):
            stotal += jnp.where(which == d, shares[d], 0.0)
    sres_ref[...] = stotal
    cps = []
    for d in range(1, seqs):
        t = lax.rem(s + d, seqs)
        cps.append(pltpu.make_async_remote_copy(
            src_ref=gat.at[pl.ds(mine_at, piece)], dst_ref=gat.at[pl.ds(mine_at, piece)],
            send_sem=ssem.at[k], recv_sem=rsem.at[k], device_id=(c, t), device_id_type=MESH))
        k += 1
    for cp in cps:
        cp.start()
    for cp in cps:
        cp.wait()
    for b in reversed(range(nbits)):
        start, half, mine = offs[b]
        keep = pl.ds(pl.multiple_of(start + mine * half, 16), half)
        cp = pltpu.make_async_remote_copy(
            src_ref=gat.at[keep], dst_ref=gat.at[keep],
            send_sem=ssem.at[k], recv_sem=rsem.at[k], device_id=(c ^ (1 << b), s), device_id_type=MESH)
        cp.start()
        cp.wait()
        k += 1
    res_ref[...] = gat[...].astype(f32)


def all_sum(grads, small, nctx, seqs):
    nbits = nctx.bit_length() - 1
    step = 16 * nctx * seqs
    grads = jnp.pad(grads, ((0, -grads.shape[0] % step), (0, 0)))
    rows, width = grads.shape
    nsem = 2 * nbits + 3 * (seqs - 1) + nbits
    vmem = pl.BlockSpec(memory_space=pltpu.VMEM)
    return pl.pallas_call(
        partial(reduce_kernel, nbits, seqs),
        out_shape=(jax.ShapeDtypeStruct(grads.shape, f32), jax.ShapeDtypeStruct(small.shape, f32)),
        in_specs=[vmem, vmem],
        out_specs=(vmem, vmem),
        scratch_shapes=[
            pltpu.VMEM((rows, width), f32), pltpu.VMEM((rows, width), bf16), pltpu.VMEM((rows, width), bf16),
            pltpu.VMEM((rows, width), bf16), pltpu.VMEM((nbits + 1,) + small.shape, bf16),
            pltpu.VMEM((nbits + seqs,) + small.shape, bf16),
            pltpu.SemaphoreType.DMA((nsem,)), pltpu.SemaphoreType.DMA((nsem,)),
        ],
        compiler_params=pltpu.CompilerParams(collective_id=1, has_side_effects=True, vmem_limit_bytes=40 * 2**20),
        name="sum_grads",
    )(grads, small)


def body(nctx, seqs, layer_input, gene_kept, attn_gain, attn_shift, w_query, w_key, w_value, w_out, out_bias,
         mlp_gain, mlp_shift, w_up, up_bias, w_down, down_bias, cotangent):
    copies, tok, width = layer_input.shape
    own = 2 * tok
    rows = 2 * own
    ff = w_up.shape[1]
    c = lax.axis_index("ctx")
    s = lax.axis_index("seq")
    cc = c % 2

    def go(k):
        return [
            (ci * seqs + si, (ci - ci % 2 + si // 2) * seqs + 2 * (ci % 2) + (si + k) % 2)
            for ci in range(nctx) for si in range(seqs)
        ]

    siblings = [(ci, ci ^ 1) for ci in range(nctx)]

    def scatter(local):
        parts = []
        for k in range(2):
            block = lax.dynamic_index_in_dim(local, (s + k) % 2, 0, keepdims=False)
            parts.append(lax.ppermute(block, ("ctx", "seq"), go(k)))
        return jnp.concatenate(parts)

    def gather(held):
        parts = []
        for k in range(2):
            back = [(b, a) for a, b in go(k)]
            parts.append(lax.ppermute(held[k * tok:(k + 1) * tok], ("ctx", "seq"), back))
        return jnp.where(s % 2 == 0, jnp.stack(parts), jnp.stack(parts[::-1]))

    x_own = scatter(layer_input)
    kept_sib = lax.ppermute(gene_kept, "ctx", siblings)
    x_all = jnp.concatenate([x_own, lax.ppermute(x_own, "ctx", siblings)])
    cot_own = scatter(cotangent.astype(bf16))
    usable = (jnp.stack([gene_kept, kept_sib]) == 1) | (jnp.arange(seqs * tok) < CLS)
    row = jnp.where(s // 2 == cc, usable[0], usable[1])
    row = lax.dynamic_index_in_dim(row, s % 2, 0, keepdims=False).reshape(seqs, tok)
    first = s % 2
    order = jnp.stack([2 * cc + first, 2 * cc + 1 - first, 2 * (1 - cc) + first, 2 * (1 - cc) + 1 - first])
    keep = jnp.where(row[order].reshape(rows, 1), 0.0, MASKED).astype(f32)

    vec = lambda v: v.reshape(1, -1)
    vmem = pl.BlockSpec(memory_space=pltpu.VMEM)
    head_cols = -(-own // 128) * 128
    cols = 2 * head_cols
    pairs = HEADS // 2
    grad_rows = 2 * ff + 4 * width
    out, dmid, esib, eown, grads, small = pl.pallas_call(
        layer_kernel,
        out_shape=(
            jax.ShapeDtypeStruct((own, width), bf16),
            jax.ShapeDtypeStruct((own, width), f32),
            jax.ShapeDtypeStruct((own, width), bf16),
            jax.ShapeDtypeStruct((own, width), f32),
            jax.ShapeDtypeStruct((grad_rows, width), f32),
            jax.ShapeDtypeStruct((8, width), f32),
        ),
        in_specs=[vmem] * 16,
        out_specs=(vmem,) * 6,
        scratch_shapes=[
            pltpu.VMEM((rows, width), bf16),
            pltpu.VMEM((pairs, width, cols), bf16),
            pltpu.VMEM((pairs, rows, width), bf16),
            pltpu.VMEM((pairs, rows, width), bf16),
            pltpu.VMEM((width, rows), bf16),
            pltpu.VMEM((pairs, width // 2 + 16, rows), bf16),
            pltpu.VMEM((pairs, rows, cols), bf16),
            pltpu.VMEM((rows, TILE), f32),
            pltpu.VMEM((pairs, width // 2, cols), f32),
            pltpu.VMEM((pairs, 1, cols), f32),
            pltpu.VMEM((width, own), bf16),
            pltpu.VMEM((own, width), bf16),
            pltpu.VMEM((own, width), bf16),
            pltpu.VMEM((own, ff), bf16),
            pltpu.VMEM((own, ff), bf16),
            pltpu.VMEM((own, width), bf16),
            pltpu.VMEM((pairs, width, cols), bf16),
            pltpu.VMEM((width, own), bf16),
            pltpu.VMEM((rows, width), bf16),
            pltpu.VMEM((rows, width), bf16),
        ],
        compiler_params=pltpu.CompilerParams(vmem_limit_bytes=62 * 2**20),
        name="layer",
    )(x_all, keep, cot_own, vec(attn_gain), vec(attn_shift), w_query, w_key, w_value, w_out, vec(out_bias),
      vec(mlp_gain), vec(mlp_shift), w_up, vec(up_bias), w_down, vec(down_bias))
    result = gather(out)
    esib = lax.ppermute(esib, "ctx", siblings)
    back, gains = pl.pallas_call(
        final_kernel,
        out_shape=(jax.ShapeDtypeStruct((own, width), bf16), jax.ShapeDtypeStruct((8, width), f32)),
        in_specs=[vmem] * 5,
        out_specs=(vmem, vmem),
        compiler_params=pltpu.CompilerParams(vmem_limit_bytes=32 * 2**20),
        name="input_grad",
    )(x_own, eown, esib, dmid, vec(attn_gain))
    input_grad = cotangent + gather(back).astype(f32)
    grads, small = all_sum(grads, jnp.concatenate([small, gains]), nctx, seqs)
    up_rows = ff // width
    return (
        result, input_grad, small[8], small[9],
        grads[2 * ff + width:2 * ff + 2 * width], grads[2 * ff + 2 * width:2 * ff + 3 * width],
        grads[2 * ff + 3 * width:2 * ff + 4 * width], grads[2 * ff:2 * ff + width],
        small[1], small[2], small[3], grads[ff:2 * ff].T, small[4:4 + up_rows].reshape(ff),
        grads[0:ff], small[0],
    )


def solution(mesh):
    tokens = P("ctx", "seq", None)
    return jax.shard_map(
        partial(body, mesh.shape["ctx"], mesh.shape["seq"]),
        mesh=mesh,
        in_specs=(tokens, P("ctx", None)) + (P(),) * 13 + (tokens,),
        out_specs=(tokens, tokens) + (P(),) * 13,
        check_vma=False,
    )
```

```python
import math
from functools import partial

import jax
import jax.numpy as jnp
from jax import lax
from jax.experimental import pallas as pl
from jax.experimental.pallas import tpu as pltpu
from jax.sharding import PartitionSpec as P

bf16 = jnp.bfloat16
f32 = jnp.float32
HEADS = 4
CLS = 8
TILE = 256
MASKED = -8.0e9
NN = (((1,), (0,)), ((), ()))
NT = (((1,), (1,)), ((), ()))
TN = (((0,), (0,)), ((), ()))
TT = (((0,), (1,)), ((), ()))
MESH = pl.DeviceIdType.MESH


def mm(a, b, dims=NN):
    return lax.dot_general(a, b, dims, preferred_element_type=f32)


def norm_parts(z):
    average = jnp.mean(z, axis=-1, keepdims=True)
    centred = z - average
    spread = jnp.mean(centred * centred, axis=-1, keepdims=True)
    rstd = lax.rsqrt(spread + 1e-05)
    return centred * rstd, rstd


def norm_back(f, n, rstd):
    mean_f = jnp.mean(f, axis=-1, keepdims=True)
    mean_fn = jnp.mean(f * n, axis=-1, keepdims=True)
    return rstd * (f - mean_f - n * mean_fn)


def normal_parts(u):
    bell = jnp.exp2(u * u * (-0.5 * math.log2(math.e)))
    t = 1.0 / (1.0 + (0.3275911 / math.sqrt(2.0)) * jnp.abs(u))
    poly = 1.061405429 * t - 1.453152027
    poly = poly * t + 1.421413741
    poly = poly * t - 0.284496736
    poly = (poly * t + 0.254829592) * t
    tail = 0.5 * poly * bell
    return jnp.where(u < 0, tail, 1.0 - tail), bell * (1.0 / math.sqrt(2.0 * math.pi))


def colsum(z):
    return jnp.sum(z, axis=0, keepdims=True)


def layer_kernel(
    x_ref, keep_ref, cot_ref,
    ag_ref, as_ref, wq_ref, wk_ref, wv_ref, wo_ref, ob_ref,
    mg_ref, ms_ref, wu_ref, ub_ref, wd_ref, db_ref,
    out_ref, back_ref, grads_ref, small_ref,
    erecv_ref, esend_sem, erecv_sem,
    n_ref, qaug, kaug, vaug, kt, vtaug, prob, s_ref, ot_ref, rl_ref,
    att_t, att, act_ref, gh_ref, gml_ref, gaug,
):
    rows, width = x_ref.shape
    own = rows // 2
    ctx = lax.axis_index("ctx")
    sibling = (ctx + 1 - 2 * lax.rem(ctx, 2), lax.axis_index("seq"))
    barrier = pltpu.get_barrier_semaphore()
    pl.semaphore_signal(barrier, inc=1, device_id=sibling, device_id_type=MESH)
    pl.semaphore_wait(barrier, 1)
    hd = width // HEADS
    pairs = HEADS // 2
    pw = 2 * hd
    head_cols = qaug.shape[2] // 2
    cols = 2 * head_cols
    tiles = cols // TILE
    scale = 1.0 / math.sqrt(hd)
    expo = scale * math.log2(math.e)
    ff = wu_ref.shape[1]
    chunk = own // 3

    gain = ag_ref[...].astype(f32).reshape(1, -1)
    shift = as_ref[...].astype(f32).reshape(1, -1)

    def norm_rows(i, carry):
        at = pl.ds(pl.multiple_of(i * chunk, 16), chunk)
        n, _ = norm_parts(x_ref[at, :].astype(f32))
        low = (n * gain + shift).astype(bf16)
        n_ref[at, :] = low
        k = mm(low, wk_ref[...]).astype(bf16)
        v = mm(low, wv_ref[...]).astype(bf16)
        for p in range(pairs):
            kaug[p, at, 0:pw] = k[:, p * pw:(p + 1) * pw]
            vaug[p, at, 0:pw] = v[:, p * pw:(p + 1) * pw]
        return carry

    lax.fori_loop(0, rows // chunk, norm_rows, 0)
    lane = lax.broadcasted_iota(jnp.int32, (rows, pw), 1)
    sub = lax.broadcasted_iota(jnp.int32, (16, rows), 0)
    marks = jnp.where(sub == 0, keep_ref[...], 0.0).astype(bf16)
    unit = jnp.where(lax.broadcasted_iota(jnp.int32, (16, pw), 0) == lax.broadcasted_iota(jnp.int32, (16, pw), 1), 1.0, 0.0)
    bias = mm(marks, unit.astype(bf16), TN).astype(bf16)
    ones = jnp.where(lane < 2, 1.0, 0.0).astype(bf16)
    for p in range(pairs):
        kaug[p, :, pw:2 * pw] = bias
        vaug[p, :, pw:2 * pw] = ones
    sub = lax.broadcasted_iota(jnp.int32, (16, rows), 0)
    kt[...] = mm(wk_ref[...], n_ref[...], TT).astype(bf16)
    vt = mm(wv_ref[...], n_ref[...], TT).astype(bf16)
    for p in range(pairs):
        vtaug[p, 0:pw, :] = vt[p * pw:(p + 1) * pw, :]
        vtaug[p, pw:pw + 16, :] = jnp.where(sub == 0, 1.0, 0.0).astype(bf16)
    qt = mm(wq_ref[...], n_ref[0:own, :], TT).astype(bf16)
    qaug[...] = jnp.zeros_like(qaug)
    gaug[...] = jnp.zeros_like(gaug)
    sub = lax.broadcasted_iota(jnp.int32, (16, cols), 0)
    for p in range(pairs):
        for h in range(2):
            qaug[p, h * hd:(h + 1) * hd, h * head_cols:h * head_cols + own] = qt[p * pw + h * hd:p * pw + (h + 1) * hd, :]
        qaug[p, pw:pw + 16, :] = jnp.where(sub == 0, 1.0, 0.0).astype(bf16)

    def forward(i, carry):
        p = i // tiles
        at = pl.ds(pl.multiple_of((i % tiles) * TILE, TILE), TILE)
        s_ref[...] = mm(kaug[p], qaug[p, :, at])
        top = jnp.max(s_ref[...], axis=0, keepdims=True)
        prob[p, :, at] = jnp.exp2((s_ref[...] - top) * expo).astype(bf16)
        o = mm(vtaug[p], prob[p, :, at])
        rl = 1.0 / o[pw:pw + 1]
        ot_ref[p, :, at] = o[0:pw] * rl
        rl_ref[p, :, at] = rl
        return carry

    lax.fori_loop(0, pairs * tiles, forward, 0)
    for p in range(pairs):
        for h in range(2):
            att_t[p * pw + h * hd:p * pw + (h + 1) * hd, :] = ot_ref[
                p, h * hd:(h + 1) * hd, h * head_cols:h * head_cols + own
            ].astype(bf16)
    att[...] = jnp.transpose(att_t[...])

    gain2 = mg_ref[...].astype(f32).reshape(1, -1)
    shift2 = ms_ref[...].astype(f32).reshape(1, -1)
    out_bias = ob_ref[...].astype(f32).reshape(1, -1)
    up_bias = ub_ref[...].astype(f32).reshape(1, -1)
    down_bias = db_ref[...].astype(f32).reshape(1, -1)

    def mlp(i, carry):
        g_up, g_down, g_out, g_gain, g_shift = carry
        at = pl.ds(pl.multiple_of(i * chunk, 16), chunk)
        middle = x_ref[at, :].astype(f32) + (mm(att[at, :], wo_ref[...]) + out_bias)
        n, rstd = norm_parts(middle)
        low = (n * gain2 + shift2).astype(bf16)
        att[at, :] = low
        hidden = mm(low, wu_ref[...]) + up_bias
        dist, dens = normal_parts(hidden)
        act = (hidden * dist).astype(bf16)
        act_ref[at, :] = act
        out_ref[at, :] = (middle + (mm(act, wd_ref[...]) + down_bias)).astype(bf16)
        cot = cot_ref[at, :]
        gh = ((dist + hidden * dens) * mm(cot, wd_ref[...], NT)).astype(bf16)
        gh_ref[at, :] = gh
        e = mm(gh, wu_ref[...], NT)
        back = norm_back(e * gain2, n, rstd)
        s_ref[at, :] = back
        cot = cot.astype(f32)
        gml = (cot + back).astype(bf16)
        gml_ref[at, :] = gml
        return (
            g_up + colsum(gh.astype(f32)), g_down + colsum(cot), g_out + colsum(gml.astype(f32)),
            g_gain + colsum(e * n), g_shift + colsum(e),
        )

    zero = jnp.zeros((1, width), f32)
    sums = lax.fori_loop(0, 3, mlp, (jnp.zeros((1, ff), f32), zero, zero, zero, zero))
    small_ref[0:1, :] = sums[1]
    small_ref[1:2, :] = sums[2]
    small_ref[2:3, :] = sums[3]
    small_ref[3:4, :] = sums[4]
    for j in range(ff // width):
        small_ref[4 + j:5 + j, :] = sums[0][:, j * width:(j + 1) * width]
    grads_ref[0:ff, :] = mm(act_ref[...], cot_ref[...], TN)
    grads_ref[ff:2 * ff, :] = mm(gh_ref[...], att[...], TN)
    grads_ref[2 * ff:2 * ff + width, :] = mm(att_t[...], gml_ref[...])

    sub = lax.broadcasted_iota(jnp.int32, (16, own), 0)
    for p in range(pairs):
        for h in range(2):
            lanes = slice(h * head_cols, h * head_cols + own)
            g = mm(wo_ref[p * pw + h * hd:p * pw + (h + 1) * hd, :], gml_ref[...], NT).astype(bf16).astype(f32)
            g = (g * rl_ref[p, :, lanes]).astype(bf16)
            gaug[p, h * hd:(h + 1) * hd, lanes] = g
            delta = -colsum(g.astype(f32) * ot_ref[p, h * hd:(h + 1) * hd, lanes])
            coarse = delta.astype(bf16).astype(f32)
            fine = delta - coarse
            gaug[p, pw:pw + 16, lanes] = jnp.where(sub == 0, coarse, jnp.where(sub == 1, fine, 0.0)).astype(bf16)

    for p in range(pairs):
        for half in range(2):
            lanes = slice(half * width + p * pw, half * width + (p + 1) * pw)
            act_ref[:, lanes] = mm(prob[p, half * own:(half + 1) * own, :], gaug[p, 0:pw, :], NT).astype(bf16)

    def backward(i, carry):
        p = i // tiles
        at = pl.ds(pl.multiple_of((i % tiles) * TILE, TILE), TILE)
        ds = prob[p, :, at] * mm(vaug[p], gaug[p, :, at]).astype(bf16)
        prob[p, :, at] = ds
        dq = mm(kt[pl.ds(pl.multiple_of(p * pw, pw), pw), :], ds)
        ot_ref[p, :, at] = dq * scale
        return carry

    lax.fori_loop(0, pairs * tiles, backward, 0)
    for p in range(pairs):
        for half in range(2):
            lanes = slice(half * width + p * pw, half * width + (p + 1) * pw)
            gh_ref[:, lanes] = (mm(prob[p, half * own:(half + 1) * own, :], qaug[p, 0:pw, :], NT) * scale).astype(bf16)

    dv_own, dv_sib = act_ref.at[:, 0:width], act_ref.at[:, width:2 * width]
    dk_own, dk_sib = gh_ref.at[:, 0:width], gh_ref.at[:, width:2 * width]

    def other_rows(i, carry):
        at = pl.ds(pl.multiple_of(i * chunk, 16), chunk)
        gml_ref[at, :] = (mm(dk_sib[at, :], wk_ref[...], NT) + mm(dv_sib[at, :], wv_ref[...], NT)).astype(bf16)
        return carry

    lax.fori_loop(0, 3, other_rows, 0)
    copy = pltpu.make_async_remote_copy(
        src_ref=gml_ref, dst_ref=erecv_ref, send_sem=esend_sem, recv_sem=erecv_sem,
        device_id=sibling, device_id_type=MESH)
    copy.start()
    for p in range(pairs):
        for h in range(2):
            att_t[p * pw + h * hd:p * pw + (h + 1) * hd, :] = ot_ref[
                p, h * hd:(h + 1) * hd, h * head_cols:h * head_cols + own
            ].astype(bf16)
    att[...] = jnp.transpose(att_t[...])
    base = 2 * ff + width
    grads_ref[base:base + width, :] = mm(n_ref[0:own, :], att[...], TN)
    grads_ref[base + width:base + 2 * width, :] = mm(n_ref[0:own, :], dk_own[...], TN) + mm(n_ref[own:rows, :], dk_sib[...], TN)
    grads_ref[base + 2 * width:base + 3 * width, :] = mm(n_ref[0:own, :], dv_own[...], TN) + mm(n_ref[own:rows, :], dv_sib[...], TN)

    def own_rows(i, carry):
        at = pl.ds(pl.multiple_of(i * chunk, 16), chunk)
        s_ref[pl.ds(pl.multiple_of(own + i * chunk, 16), chunk), :] = (
            mm(att[at, :], wq_ref[...], NT) + mm(dk_own[at, :], wk_ref[...], NT) + mm(dv_own[at, :], wv_ref[...], NT)
        )
        return carry

    lax.fori_loop(0, 3, own_rows, 0)
    copy.wait()

    def last_rows(i, carry):
        at = pl.ds(pl.multiple_of(i * chunk, 16), chunk)
        n, rstd = norm_parts(x_ref[at, :].astype(f32))
        e = s_ref[pl.ds(pl.multiple_of(own + i * chunk, 16), chunk), :] + erecv_ref[at, :].astype(f32)
        back_ref[at, :] = (s_ref[at, :] + norm_back(e * gain, n, rstd)).astype(bf16)
        return carry[0] + colsum(e * n), carry[1] + colsum(e)

    sums = lax.fori_loop(0, 3, last_rows, (zero, zero))
    ups = 4 + ff // width
    small_ref[ups:ups + 1, :] = sums[0]
    small_ref[ups + 1:ups + 2, :] = sums[1]


def reduce_kernel(nbits, seqs, g_ref, small_ref, res_ref, sres_ref, acc, send, recv, gat, ssend, srecv, ssem, rsem):
    c = lax.axis_index("ctx")
    s = lax.axis_index("seq")
    rows = g_ref.shape[0]
    bar = pltpu.get_barrier_semaphore()
    for b in range(nbits):
        pl.semaphore_signal(bar, inc=1, device_id=(c ^ (1 << b), s), device_id_type=MESH)
    for d in range(1, seqs):
        pl.semaphore_signal(bar, inc=1, device_id=(c, lax.rem(s + d, seqs)), device_id_type=MESH)
    pl.semaphore_wait(bar, nbits + seqs - 1)
    off = jnp.int32(0)
    size = rows
    roff = 0
    offs = []
    for b in range(nbits):
        half = size // 2
        mine = lax.rem(c // (1 << b), 2)
        peer = (c ^ (1 << b), s)
        src = acc if b else g_ref
        away = pl.multiple_of(off + (1 - mine) * half, 16)
        keep = pl.multiple_of(off + mine * half, 16)
        send[pl.ds(roff, half), :] = src[pl.ds(away, half), :].astype(bf16)
        ssend[b] = (sres_ref if b else small_ref)[...].astype(bf16)
        cp = pltpu.make_async_remote_copy(
            src_ref=send.at[pl.ds(roff, half)], dst_ref=recv.at[pl.ds(roff, half)],
            send_sem=ssem.at[2 * b], recv_sem=rsem.at[2 * b], device_id=peer, device_id_type=MESH)
        cs = pltpu.make_async_remote_copy(
            src_ref=ssend.at[b], dst_ref=srecv.at[b],
            send_sem=ssem.at[2 * b + 1], recv_sem=rsem.at[2 * b + 1], device_id=peer, device_id_type=MESH)
        cp.start()
        cs.start()
        cp.wait()
        cs.wait()
        acc[pl.ds(keep, half), :] = src[pl.ds(keep, half), :] + recv[pl.ds(roff, half), :].astype(f32)
        sres_ref[...] = ssend[b].astype(f32) + srecv[b].astype(f32)
        offs.append((off, half, mine))
        off = keep
        roff += half
        size = half
    piece = size // seqs
    k = 2 * nbits
    send[pl.ds(roff, size), :] = acc[pl.ds(off, size), :].astype(bf16)
    ssend[nbits] = sres_ref[...].astype(bf16)
    cps = []
    for d in range(1, seqs):
        t = lax.rem(s + d, seqs)
        cps.append(pltpu.make_async_remote_copy(
            src_ref=send.at[pl.ds(pl.multiple_of(roff + t * piece, 16), piece)],
            dst_ref=recv.at[pl.ds(roff + (d - 1) * piece, piece)],
            send_sem=ssem.at[k], recv_sem=rsem.at[k], device_id=(c, t), device_id_type=MESH))
        cps.append(pltpu.make_async_remote_copy(
            src_ref=ssend.at[nbits], dst_ref=srecv.at[nbits + d - 1],
            send_sem=ssem.at[k + 1], recv_sem=rsem.at[k + 1], device_id=(c, t), device_id_type=MESH))
        k += 2
    for cp in cps:
        cp.start()
    for cp in cps:
        cp.wait()
    mine_at = pl.multiple_of(off + s * piece, 16)
    total = acc[pl.ds(mine_at, piece), :]
    for d in range(1, seqs):
        total += recv[pl.ds(roff + (d - 1) * piece, piece), :].astype(f32)
    gat[pl.ds(mine_at, piece), :] = total.astype(bf16)
    shares = [ssend[nbits].astype(f32)] + [srecv[nbits + d - 1].astype(f32) for d in range(1, seqs)]
    stotal = jnp.zeros_like(shares[0])
    for o in range(seqs):
        which = lax.rem(s - o + seqs, seqs)
        for d in range(seqs):
            stotal += jnp.where(which == d, shares[d], 0.0)
    sres_ref[...] = stotal
    cps = []
    for d in range(1, seqs):
        t = lax.rem(s + d, seqs)
        cps.append(pltpu.make_async_remote_copy(
            src_ref=gat.at[pl.ds(mine_at, piece)], dst_ref=gat.at[pl.ds(mine_at, piece)],
            send_sem=ssem.at[k], recv_sem=rsem.at[k], device_id=(c, t), device_id_type=MESH))
        k += 1
    for cp in cps:
        cp.start()
    for cp in cps:
        cp.wait()
    for b in reversed(range(nbits)):
        start, half, mine = offs[b]
        keep = pl.ds(pl.multiple_of(start + mine * half, 16), half)
        cp = pltpu.make_async_remote_copy(
            src_ref=gat.at[keep], dst_ref=gat.at[keep],
            send_sem=ssem.at[k], recv_sem=rsem.at[k], device_id=(c ^ (1 << b), s), device_id_type=MESH)
        cp.start()
        cp.wait()
        k += 1
    res_ref[...] = gat[...].astype(f32)


def all_sum(grads, small, nctx, seqs):
    nbits = nctx.bit_length() - 1
    step = 16 * nctx * seqs
    grads = jnp.pad(grads, ((0, -grads.shape[0] % step), (0, 0)))
    rows, width = grads.shape
    nsem = 2 * nbits + 3 * (seqs - 1) + nbits
    vmem = pl.BlockSpec(memory_space=pltpu.VMEM)
    return pl.pallas_call(
        partial(reduce_kernel, nbits, seqs),
        out_shape=(jax.ShapeDtypeStruct(grads.shape, f32), jax.ShapeDtypeStruct(small.shape, f32)),
        in_specs=[vmem, vmem],
        out_specs=(vmem, vmem),
        scratch_shapes=[
            pltpu.VMEM((rows, width), f32), pltpu.VMEM((rows, width), bf16), pltpu.VMEM((rows, width), bf16),
            pltpu.VMEM((rows, width), bf16), pltpu.VMEM((nbits + 1,) + small.shape, bf16),
            pltpu.VMEM((nbits + seqs,) + small.shape, bf16),
            pltpu.SemaphoreType.DMA((nsem,)), pltpu.SemaphoreType.DMA((nsem,)),
        ],
        compiler_params=pltpu.CompilerParams(collective_id=1, has_side_effects=True, vmem_limit_bytes=40 * 2**20),
        name="sum_grads",
    )(grads, small)


def body(nctx, seqs, layer_input, gene_kept, attn_gain, attn_shift, w_query, w_key, w_value, w_out, out_bias,
         mlp_gain, mlp_shift, w_up, up_bias, w_down, down_bias, cotangent):
    copies, tok, width = layer_input.shape
    own = 2 * tok
    rows = 2 * own
    ff = w_up.shape[1]
    c = lax.axis_index("ctx")
    s = lax.axis_index("seq")
    cc = c % 2

    def go(k):
        return [
            (ci * seqs + si, (ci - ci % 2 + si // 2) * seqs + 2 * (ci % 2) + (si + k) % 2)
            for ci in range(nctx) for si in range(seqs)
        ]

    siblings = [(ci, ci ^ 1) for ci in range(nctx)]

    def scatter(local):
        parts = []
        for k in range(2):
            block = lax.dynamic_index_in_dim(local, (s + k) % 2, 0, keepdims=False)
            parts.append(lax.ppermute(block, ("ctx", "seq"), go(k)))
        return jnp.concatenate(parts)

    def gather(held):
        parts = []
        for k in range(2):
            back = [(b, a) for a, b in go(k)]
            parts.append(lax.ppermute(held[k * tok:(k + 1) * tok], ("ctx", "seq"), back))
        return jnp.where(s % 2 == 0, jnp.stack(parts), jnp.stack(parts[::-1]))

    x_own = scatter(layer_input)
    kept_sib = lax.ppermute(gene_kept, "ctx", siblings)
    x_all = jnp.concatenate([x_own, lax.ppermute(x_own, "ctx", siblings)])
    cot_own = scatter(cotangent.astype(bf16))
    usable = (jnp.stack([gene_kept, kept_sib]) == 1) | (jnp.arange(seqs * tok) < CLS)
    row = jnp.where(s // 2 == cc, usable[0], usable[1])
    row = lax.dynamic_index_in_dim(row, s % 2, 0, keepdims=False).reshape(seqs, tok)
    first = s % 2
    order = jnp.stack([2 * cc + first, 2 * cc + 1 - first, 2 * (1 - cc) + first, 2 * (1 - cc) + 1 - first])
    keep = jnp.where(row[order].reshape(1, rows), 0.0, MASKED).astype(f32)

    vmem = pl.BlockSpec(memory_space=pltpu.VMEM)
    head_cols = -(-own // 128) * 128
    cols = 2 * head_cols
    pairs = HEADS // 2
    grad_rows = 2 * ff + 4 * width
    out, back, grads, small = pl.pallas_call(
        layer_kernel,
        out_shape=(
            jax.ShapeDtypeStruct((own, width), bf16),
            jax.ShapeDtypeStruct((own, width), bf16),
            jax.ShapeDtypeStruct((grad_rows, width), f32),
            jax.ShapeDtypeStruct((16, width), f32),
        ),
        in_specs=[vmem] * 16,
        out_specs=(vmem,) * 4,
        scratch_shapes=[
            pltpu.VMEM((own, width), bf16),
            pltpu.SemaphoreType.DMA,
            pltpu.SemaphoreType.DMA,
            pltpu.VMEM((rows, width), bf16),
            pltpu.VMEM((pairs, width, cols), bf16),
            pltpu.VMEM((pairs, rows, width), bf16),
            pltpu.VMEM((pairs, rows, width), bf16),
            pltpu.VMEM((width, rows), bf16),
            pltpu.VMEM((pairs, width // 2 + 16, rows), bf16),
            pltpu.VMEM((pairs, rows, cols), bf16),
            pltpu.VMEM((rows, TILE), f32),
            pltpu.VMEM((pairs, width // 2, cols), f32),
            pltpu.VMEM((pairs, 1, cols), f32),
            pltpu.VMEM((width, own), bf16),
            pltpu.VMEM((own, width), bf16),
            pltpu.VMEM((own, ff), bf16),
            pltpu.VMEM((own, ff), bf16),
            pltpu.VMEM((own, width), bf16),
            pltpu.VMEM((pairs, width, cols), bf16),
        ],
        compiler_params=pltpu.CompilerParams(collective_id=2, has_side_effects=True, vmem_limit_bytes=62 * 2**20),
        name="layer",
    )(x_all, keep, cot_own, attn_gain, attn_shift, w_query, w_key, w_value, w_out, out_bias,
      mlp_gain, mlp_shift, w_up, up_bias, w_down, down_bias)
    result = gather(out)
    input_grad = cotangent + gather(back).astype(f32)
    grads, small = all_sum(grads, small, nctx, seqs)
    up_rows = ff // width
    return (
        result, input_grad, small[8], small[9],
        grads[2 * ff + width:2 * ff + 2 * width], grads[2 * ff + 2 * width:2 * ff + 3 * width],
        grads[2 * ff + 3 * width:2 * ff + 4 * width], grads[2 * ff:2 * ff + width],
        small[1], small[2], small[3], grads[ff:2 * ff].T, small[4:4 + up_rows].reshape(ff),
        grads[0:ff], small[0],
    )


def solution(mesh):
    tokens = P("ctx", "seq", None)
    return jax.shard_map(
        partial(body, mesh.shape["ctx"], mesh.shape["seq"]),
        mesh=mesh,
        in_specs=(tokens, P("ctx", None)) + (P(),) * 13 + (tokens,),
        out_specs=(tokens, tokens) + (P(),) * 13,
        check_vma=False,
    )
```

```python
import math
from functools import partial

import jax
import jax.numpy as jnp
from jax import lax
from jax.experimental import pallas as pl
from jax.experimental.pallas import tpu as pltpu
from jax.sharding import PartitionSpec as P

bf16 = jnp.bfloat16
f32 = jnp.float32
HEADS = 4
CLS = 8
TILE = 256
MASKED = -8.0e9
NN = (((1,), (0,)), ((), ()))
NT = (((1,), (1,)), ((), ()))
TN = (((0,), (0,)), ((), ()))
TT = (((0,), (1,)), ((), ()))
MESH = pl.DeviceIdType.MESH


def mm(a, b, dims=NN):
    return lax.dot_general(a, b, dims, preferred_element_type=f32)


def norm_parts(z):
    average = jnp.mean(z, axis=-1, keepdims=True)
    centred = z - average
    spread = jnp.mean(centred * centred, axis=-1, keepdims=True)
    rstd = lax.rsqrt(spread + 1e-05)
    return centred * rstd, rstd


def norm_back(f, n, rstd):
    mean_f = jnp.mean(f, axis=-1, keepdims=True)
    mean_fn = jnp.mean(f * n, axis=-1, keepdims=True)
    return rstd * (f - mean_f - n * mean_fn)


def normal_parts(u):
    bell = jnp.exp2(u * u * (-0.5 * math.log2(math.e)))
    t = 1.0 / (1.0 + (0.3275911 / math.sqrt(2.0)) * jnp.abs(u))
    poly = 1.061405429 * t - 1.453152027
    poly = poly * t + 1.421413741
    poly = poly * t - 0.284496736
    poly = (poly * t + 0.254829592) * t
    tail = 0.5 * poly * bell
    return jnp.where(u < 0, tail, 1.0 - tail), bell * (1.0 / math.sqrt(2.0 * math.pi))


def colsum(z):
    return jnp.sum(z, axis=0, keepdims=True)


def row_vec(ref):
    return ref[...].astype(f32).reshape(1, -1)


def up16(n):
    return -(-n // 16) * 16


class Sems:
    def __init__(self, send, recv):
        self.send, self.recv, self.used = send, recv, 0

    def copy(self, src, dst, device):
        k = self.used
        self.used += 1
        return pltpu.make_async_remote_copy(
            src_ref=src, dst_ref=dst, send_sem=self.send.at[k], recv_sem=self.recv.at[k],
            device_id=device, device_id_type=MESH)


def reduce_steps(sems, ctx, seq, order, seqs, rows, acc, acc0, send, send0, recv, recv0, gat, gat0):
    half = rows // 2
    mine = lax.rem(ctx, 2)
    base = mine * half
    off = base
    size = half
    into = recv0
    out = send0
    path = []
    for step, bit in enumerate(order):
        peer = (ctx + (1 - 2 * lax.rem(ctx // (1 << bit), 2)) * (1 << bit), seq)
        if step == 0:
            path.append((peer, off, size))
            cp = sems.copy(send.at[pl.ds(out, size)], recv.at[pl.ds(into, size)], peer)
            kept = off
        elif size % (32 * seqs) == 0:
            size = size // 2
            mine = lax.rem(ctx // (1 << bit), 2)
            kept = off + mine * size
            away = off + (1 - mine) * size
            send[pl.ds(out, size), :] = acc[pl.ds(pl.multiple_of(acc0 + away - base, 16), size), :].astype(bf16)
            path.append((peer, kept, size))
            cp = sems.copy(send.at[pl.ds(out, size)], recv.at[pl.ds(into, size)], peer)
        else:
            send[pl.ds(out, size), :] = acc[pl.ds(pl.multiple_of(acc0 + off - base, 16), size), :].astype(bf16)
            cp = sems.copy(send.at[pl.ds(out, size)], recv.at[pl.ds(into, size)], peer)
            kept = off
        cp.start()
        yield
        cp.wait()
        at = pl.ds(pl.multiple_of(acc0 + kept - base, 16), size)
        acc[at, :] = acc[at, :] + recv[pl.ds(into, size), :].astype(f32)
        off = kept
        into += size
    piece = size // seqs
    send[pl.ds(out, size), :] = acc[pl.ds(pl.multiple_of(acc0 + off - base, 16), size), :].astype(bf16)
    cps = []
    for d in range(1, seqs):
        t = lax.rem(seq + d, seqs)
        cps.append(sems.copy(
            send.at[pl.ds(pl.multiple_of(out + t * piece, 16), piece)],
            recv.at[pl.ds(into + (d - 1) * piece, piece)], (ctx, t)))
    for cp in cps:
        cp.start()
    yield
    for cp in cps:
        cp.wait()
    total = acc[pl.ds(pl.multiple_of(acc0 + off - base + seq * piece, 16), piece), :]
    for d in range(1, seqs):
        total += recv[pl.ds(into + (d - 1) * piece, piece), :].astype(f32)
    at = pl.ds(pl.multiple_of(gat0 + off + seq * piece, 16), piece)
    gat[at, :] = total.astype(bf16)
    cps = []
    for d in range(1, seqs):
        cps.append(sems.copy(gat.at[at], gat.at[at], (ctx, lax.rem(seq + d, seqs))))
    for cp in cps:
        cp.start()
    yield
    for cp in cps:
        cp.wait()
    for peer, kept, size in reversed(path):
        at = pl.ds(pl.multiple_of(gat0 + kept, 16), size)
        cp = sems.copy(gat.at[at], gat.at[at], peer)
        cp.start()
        yield
        cp.wait()


def landing_rows(rows, nbits, seqs):
    size = rows // 2
    count = size
    for _ in range(nbits - 1):
        if size % (32 * seqs) == 0:
            size //= 2
        count += size
    return count + size // seqs * (seqs - 1)


def landing_rows(rows, nbits, seqs):
    size = rows // 2
    count = size
    for _ in range(nbits - 1):
        if size % (32 * seqs) == 0:
            size //= 2
        count += size
    return count + size // seqs * (seqs - 1)


def small_steps(sems, ctx, seq, nbits, seqs, small, send, recv):
    for b in range(nbits):
        send[b] = small[...].astype(bf16)
        peer = (ctx + (1 - 2 * lax.rem(ctx // (1 << b), 2)) * (1 << b), seq)
        cp = sems.copy(send.at[b], recv.at[b], peer)
        cp.start()
        yield
        cp.wait()
        small[...] = send[b].astype(f32) + recv[b].astype(f32)
    send[nbits] = small[...].astype(bf16)
    cps = []
    for d in range(1, seqs):
        cps.append(sems.copy(send.at[nbits], recv.at[nbits + d - 1], (ctx, lax.rem(seq + d, seqs))))
    for cp in cps:
        cp.start()
    yield
    for cp in cps:
        cp.wait()
    shares = [send[nbits].astype(f32)] + [recv[nbits + d - 1].astype(f32) for d in range(1, seqs)]
    total = jnp.zeros_like(shares[0])
    for o in range(seqs):
        which = lax.rem(seq - o + seqs, seqs)
        for d in range(seqs):
            total += jnp.where(which == d, shares[d], 0.0)
    small[...] = total


def layer_kernel(
    nbits, seqs,
    xin, kept_ref, cot_hbm,
    ag_ref, as_ref, wq_ref, wk_ref, wv_ref, wo_ref, ob_ref,
    mg_ref, ms_ref, wu_ref, ub_ref, wd_ref, db_ref,
    outr, backr, gat, small_ref,
    stage, xall, cotr, marks, n_ref, qaug, kaug, vaug, kt, vtaug, prob, s_ref, ot_ref, rl_ref,
    att_t, att, act_ref, gh_ref, gml_ref, gaug, dext, erecv, acc, recv, ssend, srecv,
    local_sem, send_sems, recv_sems, ret_send, ret_recv,
):
    copies, tok, width = xin.shape
    tokp = xall.shape[1]
    own = 2 * tokp
    rows = 2 * own
    ctx = lax.axis_index("ctx")
    seq = lax.axis_index("seq")
    cc = lax.rem(ctx, 2)
    group = ctx - cc
    sems = Sems(send_sems, recv_sems)
    hd = width // HEADS
    pairs = HEADS // 2
    pw = 2 * hd
    head_cols = qaug.shape[2] // 2
    cols = 2 * head_cols
    tiles = cols // TILE
    scale = 1.0 / math.sqrt(hd)
    expo = scale * math.log2(math.e)
    ff = wu_ref.shape[1]
    chunk = tokp
    nchunk = own // chunk
    sibling = (group + 1 - cc, seq)
    stay = seq // 2 == cc

    cot_in = pltpu.make_async_copy(cot_hbm, s_ref.at[pl.ds(0, 2 * tok)], local_sem)
    cot_in.start()

    barrier = pltpu.get_barrier_semaphore()
    for dc in range(2):
        for d in range(seqs):
            if dc or d:
                pl.semaphore_signal(
                    barrier, inc=1, device_id=(group + lax.rem(cc + dc, 2), lax.rem(seq + d, seqs)), device_id_type=MESH)
    for b in range(1, nbits):
        pl.semaphore_signal(
            barrier, inc=1, device_id=(ctx + (1 - 2 * lax.rem(ctx // (1 << b), 2)) * (1 << b), seq), device_id_type=MESH)

    lane = lax.broadcasted_iota(jnp.int32, (1, seqs * tok), 1)
    usable = jnp.where(jnp.logical_or(kept_ref[...] == 1, lane < CLS), 0.0, MASKED)
    usable = jnp.where(lax.rem(seq, 2) == 0, usable[0:1, :], usable[1:2, :])
    wide = marks.shape[3]
    sub = lax.broadcasted_iota(jnp.int32, (16, wide), 0)
    for sh in range(seqs):
        piece = jnp.concatenate(
            [usable[:, sh * tok:(sh + 1) * tok], jnp.full((1, wide - tok), MASKED, f32)], axis=1)
        marks[0, sh] = jnp.where(sub == 0, piece, 0.0).astype(bf16)
    stage[:, tokp - 16:tokp, :] = jnp.zeros((copies, 16, width), bf16)
    stage[:, 0:tok, :] = xin[...]

    def out_copy(k, dst):
        b = lax.rem(seq + k, 2)
        return sems.copy(stage.at[b], dst.at[k], (group + seq // 2, 2 * cc + b))

    def scatter(dst):
        moves = [out_copy(0, dst), out_copy(1, dst)]
        moves[1].start()

        @pl.when(jnp.logical_not(stay))
        def _():
            moves[0].start()

        @pl.when(stay)
        def _():
            dst[0] = stage[lax.rem(seq, 2)]

        return moves

    def arrived(moves, k):
        if k:
            moves[k].wait_recv()
        else:
            @pl.when(jnp.logical_not(stay))
            def _():
                moves[0].wait_recv()

    def left(moves):
        moves[1].wait_send()

        @pl.when(jnp.logical_not(stay))
        def _():
            moves[0].wait_send()

    pl.semaphore_wait(barrier, 2 * seqs - 1 + nbits - 1)
    moves = scatter(xall)
    marks_copy = sems.copy(marks.at[0], marks.at[1], sibling)
    marks_copy.start()

    gain = row_vec(ag_ref)
    shift = row_vec(as_ref)

    def project(pos):
        at = slice(pos * tokp, (pos + 1) * tokp)
        n, _ = norm_parts(xall[pos].astype(f32))
        low = (n * gain + shift).astype(bf16)
        n_ref[at, :] = low
        k = mm(low, wk_ref[...]).astype(bf16)
        v = mm(low, wv_ref[...]).astype(bf16)
        for p in range(pairs):
            kaug[p, at, 0:pw] = k[:, p * pw:(p + 1) * pw]
            vaug[p, at, 0:pw] = v[:, p * pw:(p + 1) * pw]

    forwards = []
    for k in range(2):
        arrived(moves, k)
        forwards.append(sems.copy(xall.at[k], xall.at[2 + k], sibling))
        forwards[k].start()
    for k in range(2):
        project(k)
    left(moves)
    cot_in.wait()
    for b in range(2):
        stage[b, 0:tok, :] = s_ref[b * tok:(b + 1) * tok, :].astype(bf16)
    cot_moves = scatter(cotr)
    marks_copy.wait()
    held = jnp.where(stay, 0, 1)
    unit = jnp.where(
        lax.broadcasted_iota(jnp.int32, (16, pw), 0) == lax.broadcasted_iota(jnp.int32, (16, pw), 1), 1.0, 0.0
    ).astype(bf16)
    lane = lax.broadcasted_iota(jnp.int32, (rows, pw), 1)
    ones = jnp.where(lane < 2, 1.0, 0.0).astype(bf16)
    for p in range(pairs):
        vaug[p, :, pw:2 * pw] = ones
    for pos in range(4):
        side = cc if pos < 2 else 1 - cc
        mark = marks[held, 2 * side + lax.rem(seq + pos, 2)]
        bias = mm(mark, unit, TN).astype(bf16)[0:tokp, :]
        for p in range(pairs):
            kaug[p, pos * tokp:(pos + 1) * tokp, pw:2 * pw] = bias
    qt = mm(wq_ref[...], n_ref[0:own, :], TT).astype(bf16)
    qaug[...] = jnp.zeros_like(qaug)
    gaug[...] = jnp.zeros_like(gaug)
    dext[...] = jnp.zeros_like(dext)
    for p in range(pairs):
        for h in range(2):
            qaug[p, h * hd:(h + 1) * hd, h * head_cols:h * head_cols + own] = qt[p * pw + h * hd:p * pw + (h + 1) * hd, :]
    for k in range(2):
        forwards[k].wait()
        project(2 + k)
    kt[...] = mm(wk_ref[...], n_ref[...], TT).astype(bf16)
    vt = mm(wv_ref[...], n_ref[...], TT).astype(bf16)
    sub = lax.broadcasted_iota(jnp.int32, (16, rows), 0)
    for p in range(pairs):
        vtaug[p, 0:pw, :] = vt[p * pw:(p + 1) * pw, :]
        vtaug[p, pw:pw + 16, :] = jnp.where(sub == 0, 1.0, 0.0).astype(bf16)

    first = jnp.where(lax.broadcasted_iota(jnp.int32, (pw, TILE), 0) == 0, 1.0, 0.0).astype(bf16)

    def forward(i, carry):
        p = i // tiles
        at = pl.ds(pl.multiple_of((i % tiles) * TILE, TILE), TILE)
        s_ref[...] = mm(kaug[p], jnp.concatenate([qaug[p, :, at], first], axis=0))
        top = jnp.max(s_ref[...], axis=0, keepdims=True)
        prob[p, :, at] = jnp.exp2((s_ref[...] - top) * expo).astype(bf16)
        o = mm(vtaug[p], prob[p, :, at])
        rl = 1.0 / o[pw:pw + 1]
        ot_ref[p, :, at] = o[0:pw] * rl
        rl_ref[p, :, at] = rl
        return carry

    lax.fori_loop(0, pairs * tiles, forward, 0)
    for p in range(pairs):
        for h in range(2):
            att_t[p * pw + h * hd:p * pw + (h + 1) * hd, :] = ot_ref[
                p, h * hd:(h + 1) * hd, h * head_cols:h * head_cols + own
            ].astype(bf16)
    att[...] = jnp.transpose(att_t[...])

    gain2 = row_vec(mg_ref)
    shift2 = row_vec(ms_ref)
    out_bias = row_vec(ob_ref)
    up_bias = row_vec(ub_ref)
    down_bias = row_vec(db_ref)
    arrived(cot_moves, 0)
    arrived(cot_moves, 1)
    left(cot_moves)

    def mlp(i, carry):
        g_up, g_down, g_out, g_gain, g_shift = carry
        at = pl.ds(pl.multiple_of(i * chunk, 16), chunk)
        middle = xall[i].astype(f32) + (mm(att[at, :], wo_ref[...]) + out_bias)
        n, rstd = norm_parts(middle)
        low = (n * gain2 + shift2).astype(bf16)
        att[at, :] = low
        hidden = mm(low, wu_ref[...]) + up_bias
        dist, dens = normal_parts(hidden)
        act = (hidden * dist).astype(bf16)
        act_ref[at, :] = act
        stage[i] = (middle + (mm(act, wd_ref[...]) + down_bias)).astype(bf16)
        cot = cotr[i]
        gh = ((dist + hidden * dens) * mm(cot, wd_ref[...], NT)).astype(bf16)
        gh_ref[at, :] = gh
        e = mm(gh, wu_ref[...], NT)
        back = norm_back(e * gain2, n, rstd)
        s_ref[at, :] = back
        cot = cot.astype(f32)
        gml = (cot + back).astype(bf16)
        gml_ref[at, :] = gml
        return (
            g_up + colsum(gh.astype(f32)), g_down + colsum(cot), g_out + colsum(gml.astype(f32)),
            g_gain + colsum(e * n), g_shift + colsum(e),
        )

    zero = jnp.zeros((1, width), f32)
    sums = lax.fori_loop(0, nchunk, mlp, (jnp.zeros((1, ff), f32), zero, zero, zero, zero))
    small_ref[0:1, :] = sums[1]
    small_ref[1:2, :] = sums[2]
    small_ref[2:3, :] = sums[3]
    small_ref[3:4, :] = sums[4]
    ups = 4 + ff // width
    for j in range(ff // width):
        small_ref[4 + j:5 + j, :] = sums[0][:, j * width:(j + 1) * width]

    def back_copy(k, dst, sem):
        b = lax.rem(seq, 2)
        return pltpu.make_async_remote_copy(
            src_ref=stage.at[k], dst_ref=dst.at[b], send_sem=ret_send.at[2 * sem + k], recv_sem=ret_recv.at[2 * sem + b],
            device_id=(group + seq // 2, 2 * cc + lax.rem(seq + k, 2)), device_id_type=MESH)

    def send_home(dst, sem):
        moves = [back_copy(0, dst, sem), back_copy(1, dst, sem)]
        moves[1].start()

        @pl.when(jnp.logical_not(stay))
        def _():
            moves[0].start()

        @pl.when(stay)
        def _():
            dst[lax.rem(seq, 2)] = stage[0]

        return moves

    def home_again(dst, sem):
        for b in range(2):
            here = jnp.logical_and(stay, lax.rem(seq, 2) == b)

            @pl.when(jnp.logical_not(here))
            def _():
                pltpu.make_async_remote_copy(
                    src_ref=stage.at[b], dst_ref=dst.at[b], send_sem=ret_send.at[2 * sem + b],
                    recv_sem=ret_recv.at[2 * sem + b], device_id=sibling, device_id_type=MESH).wait_recv()

    out_moves = send_home(outr, 0)

    spare = own

    def split(value, count, acc0, send, send0, at=0):
        s_ref[spare:spare + count, :] = value
        half = count // 2
        acc[acc0:acc0 + half, :] = s_ref[pl.ds(pl.multiple_of(spare + cc * half, 16), half), :]
        send[pl.ds(send0, half), :] = s_ref[pl.ds(pl.multiple_of(spare + (1 - cc) * half, 16), half), :].astype(bf16)

    sets = (ff, ff, 2 * width, 2 * width)
    starts = [sum(sets[:j]) for j in range(4)]
    lands = [landing_rows(sets[j], nbits, seqs) for j in range(4)]
    lands = [sum(lands[:j]) for j in range(4)]
    lands = [landing_rows(sets[j], nbits, seqs) for j in range(4)]
    lands = [sum(lands[:j]) for j in range(4)]
    send_a = act_ref.at[:, 2 * width:3 * width]
    send_b = act_ref.at[:, 3 * width:4 * width]
    send_c = gh_ref.at[:, 2 * width:3 * width]
    send_d = gh_ref.at[:, 3 * width:4 * width]
    sends = (send_a, send_b, send_c, send_d)
    bits = list(range(nbits))
    turned = bits[:1] + bits[:0:-1]
    orders = (bits, turned, turned, bits)
    steps = [
        reduce_steps(sems, ctx, seq, orders[j], seqs, sets[j], acc, starts[j] // 2, sends[j], 0, recv, lands[j], gat, starts[j])
        for j in range(4)
    ]
    running = []

    def turn():
        for g in list(running):
            if next(g, "done") == "done":
                running.remove(g)

    split(mm(act_ref[...], cotr[...].reshape(own, width), TN), ff, starts[0] // 2, send_a, 0)
    up = mm(att[...], gh_ref[...], TN)
    up = jnp.concatenate([up[:, j * width:(j + 1) * width] for j in range(ff // width)], axis=0)
    split(up, ff, starts[1] // 2, send_b, 0)
    running += [steps[0], steps[1]]
    turn()
    split(mm(att_t[...], gml_ref[...]), width, starts[2] // 2, send_c, 0)

    sub = lax.broadcasted_iota(jnp.int32, (16, own), 0)
    for p in range(pairs):
        for h in range(2):
            lanes = slice(h * head_cols, h * head_cols + own)
            g = mm(wo_ref[p * pw + h * hd:p * pw + (h + 1) * hd, :], gml_ref[...], NT).astype(bf16).astype(f32)
            g = (g * rl_ref[p, :, lanes]).astype(bf16)
            gaug[p, h * hd:(h + 1) * hd, lanes] = g
            delta = -colsum(g.astype(f32) * ot_ref[p, h * hd:(h + 1) * hd, lanes])
            coarse = delta.astype(bf16).astype(f32)
            dext[p, :, lanes] = jnp.where(sub == 0, coarse, jnp.where(sub == 1, delta - coarse, 0.0)).astype(bf16)

    for p in range(pairs):
        for half in range(2):
            lanes = slice(half * width + p * pw, half * width + (p + 1) * pw)
            act_ref[:, lanes] = mm(prob[p, half * own:(half + 1) * own, :], gaug[p], NT).astype(bf16)
        turn()
    dv_own, dv_sib = act_ref.at[:, 0:width], act_ref.at[:, width:2 * width]
    dk_own, dk_sib = gh_ref.at[:, 0:width], gh_ref.at[:, width:2 * width]
    split(mm(n_ref[0:own, :], dv_own[...], TN) + mm(n_ref[own:rows, :], dv_sib[...], TN),
          width, (starts[2] + width) // 2, send_c, width // 2)
    running.append(steps[2])
    turn()
    nothing = jnp.zeros((pw - 16, TILE), bf16)

    def backward(i, carry):
        p = i // tiles
        at = pl.ds(pl.multiple_of((i % tiles) * TILE, TILE), TILE)
        right = jnp.concatenate([gaug[p, :, at], dext[p, :, at], nothing], axis=0)
        ds = prob[p, :, at] * mm(vaug[p], right).astype(bf16)
        prob[p, :, at] = ds
        dq = mm(kt[pl.ds(pl.multiple_of(p * pw, pw), pw), :], ds)
        ot_ref[p, :, at] = dq * scale
        return carry

    for p in range(pairs):
        for part in range(3):
            lax.fori_loop(p * tiles + part * tiles // 3, p * tiles + (part + 1) * tiles // 3, backward, 0)
            turn()
    for p in range(pairs):
        for half in range(2):
            lanes = slice(half * width + p * pw, half * width + (p + 1) * pw)
            gh_ref[:, lanes] = (mm(prob[p, half * own:(half + 1) * own, :], qaug[p], NT) * scale).astype(bf16)
        turn()
    left(out_moves)

    def other_rows(i, carry):
        at = pl.ds(pl.multiple_of(i * chunk, 16), chunk)
        gml_ref[at, :] = (mm(dk_sib[at, :], wk_ref[...], NT) + mm(dv_sib[at, :], wv_ref[...], NT)).astype(bf16)
        return carry

    lax.fori_loop(0, nchunk, other_rows, 0)
    e_copy = sems.copy(gml_ref, erecv, sibling)
    e_copy.start()
    turn()
    for p in range(pairs):
        for h in range(2):
            att_t[p * pw + h * hd:p * pw + (h + 1) * hd, :] = ot_ref[
                p, h * hd:(h + 1) * hd, h * head_cols:h * head_cols + own
            ].astype(bf16)
    att[...] = jnp.transpose(att_t[...])
    split(mm(n_ref[0:own, :], att[...], TN), width, starts[3] // 2, send_d, 0)
    split(mm(n_ref[0:own, :], dk_own[...], TN) + mm(n_ref[own:rows, :], dk_sib[...], TN),
          width, (starts[3] + width) // 2, send_d, width // 2)
    running.append(steps[3])
    turn()

    def own_rows(i, carry):
        at = pl.ds(pl.multiple_of(i * chunk, 16), chunk)
        s_ref[pl.ds(pl.multiple_of(own + i * chunk, 16), chunk), :] = (
            mm(att[at, :], wq_ref[...], NT) + mm(dk_own[at, :], wk_ref[...], NT) + mm(dv_own[at, :], wv_ref[...], NT)
        )
        return carry

    lax.fori_loop(0, nchunk, own_rows, 0)
    turn()
    e_copy.wait()

    def last_rows(i, carry):
        at = pl.ds(pl.multiple_of(i * chunk, 16), chunk)
        n, rstd = norm_parts(xall[i].astype(f32))
        e = s_ref[pl.ds(pl.multiple_of(own + i * chunk, 16), chunk), :] + erecv[at, :].astype(f32)
        stage[i] = (s_ref[at, :] + norm_back(e * gain, n, rstd)).astype(bf16)
        return carry[0] + colsum(e * n), carry[1] + colsum(e)

    sums = lax.fori_loop(0, nchunk, last_rows, (zero, zero))
    small_ref[ups:ups + 1, :] = sums[0]
    small_ref[ups + 1:ups + 2, :] = sums[1]
    small_ref[ups + 2:, :] = jnp.zeros((small_ref.shape[0] - ups - 2, width), f32)
    back_moves = send_home(backr, 1)
    running.append(small_steps(sems, ctx, seq, nbits, seqs, small_ref, ssend, srecv))
    while running:
        turn()
    left(back_moves)
    home_again(outr, 0)
    home_again(backr, 1)


def unpack_kernel(cot_ref, outr, backr, gat, small, *outs):
    copies, tok, width = cot_ref.shape
    (out, xg, ag, as_, wq, wk, wv, wo, ob, mg, ms, wu, ub, wd, db) = outs
    ff = wd.shape[0]
    out[...] = outr[:, 0:tok, :]
    xg[...] = cot_ref[...] + backr[:, 0:tok, :].astype(f32)
    wd[...] = gat[0:ff, :].astype(f32)
    for j in range(ff // width):
        wu[:, j * width:(j + 1) * width] = gat[ff + j * width:ff + (j + 1) * width, :].astype(f32)
        ub[0:1, j * width:(j + 1) * width] = small[4 + j:5 + j, :]
    half = width // 2
    for j, ref in enumerate((wo, wv, wq, wk)):
        at = 2 * ff + j // 2 * 2 * width + j % 2 * half
        ref[0:half, :] = gat[at:at + half, :].astype(f32)
        ref[half:width, :] = gat[at + width:at + width + half, :].astype(f32)
    ups = 4 + ff // width
    for j, ref in ((0, db), (1, ob), (2, mg), (3, ms), (ups, ag), (ups + 1, as_)):
        ref[...] = small[j:j + 1, :]


def body(nctx, seqs, layer_input, gene_kept, attn_gain, attn_shift, w_query, w_key, w_value, w_out, out_bias,
         mlp_gain, mlp_shift, w_up, up_bias, w_down, down_bias, cotangent):
    copies, tok, width = layer_input.shape
    tokp = up16(tok)
    own = 2 * tokp
    rows = 2 * own
    ff = w_up.shape[1]
    nbits = nctx.bit_length() - 1
    vmem = pl.BlockSpec(memory_space=pltpu.VMEM)
    hbm = pl.BlockSpec(memory_space=pl.ANY)
    head_cols = -(-own // 128) * 128
    cols = 2 * head_cols
    pairs = HEADS // 2
    pw = width // 2
    grad_rows = 2 * ff + 4 * width
    landing = 2 * landing_rows(ff, nbits, seqs) + 2 * landing_rows(2 * width, nbits, seqs)
    landing = 2 * landing_rows(ff, nbits, seqs) + 2 * landing_rows(2 * width, nbits, seqs)
    ncopy = 2 + 1 + 2 + 2 + 1 + 4 * (2 * nbits + 2 * (seqs - 1)) + nbits + seqs - 1
    home = jax.ShapeDtypeStruct((copies, tokp, width), bf16)
    outr, backr, gat, small = pl.pallas_call(
        partial(layer_kernel, nbits, seqs),
        out_shape=(
            home, home,
            jax.ShapeDtypeStruct((grad_rows, width), bf16),
            jax.ShapeDtypeStruct((16, width), f32),
        ),
        in_specs=[vmem, vmem, hbm] + [vmem] * 13,
        out_specs=(vmem,) * 4,
        scratch_shapes=[
            pltpu.VMEM((copies, tokp, width), bf16),
            pltpu.VMEM((4, tokp, width), bf16),
            pltpu.VMEM((copies, tokp, width), bf16),
            pltpu.VMEM((2, seqs, 16, -(-tokp // 128) * 128), bf16),
            pltpu.VMEM((rows, width), bf16),
            pltpu.VMEM((pairs, pw, cols), bf16),
            pltpu.VMEM((pairs, rows, width), bf16),
            pltpu.VMEM((pairs, rows, width), bf16),
            pltpu.VMEM((width, rows), bf16),
            pltpu.VMEM((pairs, pw + 16, rows), bf16),
            pltpu.VMEM((pairs, rows, cols), bf16),
            pltpu.VMEM((rows, TILE), f32),
            pltpu.VMEM((pairs, pw, cols), f32),
            pltpu.VMEM((pairs, 1, cols), f32),
            pltpu.VMEM((width, own), bf16),
            pltpu.VMEM((own, width), bf16),
            pltpu.VMEM((own, ff), bf16),
            pltpu.VMEM((own, ff), bf16),
            pltpu.VMEM((own, width), bf16),
            pltpu.VMEM((pairs, pw, cols), bf16),
            pltpu.VMEM((pairs, 16, cols), bf16),
            pltpu.VMEM((own, width), bf16),
            pltpu.VMEM((grad_rows // 2, width), f32),
            pltpu.VMEM((landing, width), bf16),
            pltpu.VMEM((nbits + 1, 16, width), bf16),
            pltpu.VMEM((nbits + seqs, 16, width), bf16),
            pltpu.SemaphoreType.DMA,
            pltpu.SemaphoreType.DMA((ncopy,)),
            pltpu.SemaphoreType.DMA((ncopy,)),
            pltpu.SemaphoreType.DMA((4,)),
            pltpu.SemaphoreType.DMA((4,)),
        ],
        compiler_params=pltpu.CompilerParams(collective_id=1, has_side_effects=True, vmem_limit_bytes=63 * 2**20),
        name="layer",
    )(layer_input, gene_kept, cotangent.reshape(copies * tok, width), attn_gain, attn_shift, w_query, w_key, w_value,
      w_out, out_bias, mlp_gain, mlp_shift, w_up, up_bias, w_down, down_bias)
    line = jax.ShapeDtypeStruct((1, width), f32)
    square = jax.ShapeDtypeStruct((width, width), f32)
    outs = pl.pallas_call(
        unpack_kernel,
        out_shape=(
            jax.ShapeDtypeStruct((copies, tok, width), bf16), jax.ShapeDtypeStruct((copies, tok, width), f32),
            line, line, square, square, square, square, line, line, line,
            jax.ShapeDtypeStruct((width, ff), f32), jax.ShapeDtypeStruct((1, ff), f32),
            jax.ShapeDtypeStruct((ff, width), f32), line,
        ),
        in_specs=[vmem] * 5,
        out_specs=(vmem,) * 15,
        compiler_params=pltpu.CompilerParams(vmem_limit_bytes=32 * 2**20),
        name="unpack",
    )(cotangent, outr, backr, gat, small)
    return tuple(o.reshape(-1) if o.shape[0] == 1 else o for o in outs)


def solution(mesh):
    tokens = P("ctx", "seq", None)
    return jax.shard_map(
        partial(body, mesh.shape["ctx"], mesh.shape["seq"]),
        mesh=mesh,
        in_specs=(tokens, P("ctx", None)) + (P(),) * 13 + (tokens,),
        out_specs=(tokens, tokens) + (P(),) * 13,
        check_vma=False,
    )
```

```python
import math
from functools import partial

import jax
import jax.numpy as jnp
from jax import lax
from jax.experimental import pallas as pl
from jax.experimental.pallas import tpu as pltpu
from jax.sharding import PartitionSpec as P

bf16 = jnp.bfloat16
f32 = jnp.float32
HEADS = 4
CLS = 8
TILE = 256
MASKED = -8.0e9
NN = (((1,), (0,)), ((), ()))
NT = (((1,), (1,)), ((), ()))
TN = (((0,), (0,)), ((), ()))
TT = (((0,), (1,)), ((), ()))
MESH = pl.DeviceIdType.MESH


def mm(a, b, dims=NN):
    return lax.dot_general(a, b, dims, preferred_element_type=f32)


def norm_parts(z):
    average = jnp.mean(z, axis=-1, keepdims=True)
    centred = z - average
    spread = jnp.mean(centred * centred, axis=-1, keepdims=True)
    rstd = lax.rsqrt(spread + 1e-05)
    return centred * rstd, rstd


def norm_back(f, n, rstd):
    mean_f = jnp.mean(f, axis=-1, keepdims=True)
    mean_fn = jnp.mean(f * n, axis=-1, keepdims=True)
    return rstd * (f - mean_f - n * mean_fn)


def normal_parts(u):
    bell = jnp.exp2(u * u * (-0.5 * math.log2(math.e)))
    t = 1.0 / (1.0 + (0.3275911 / math.sqrt(2.0)) * jnp.abs(u))
    poly = 1.061405429 * t - 1.453152027
    poly = poly * t + 1.421413741
    poly = poly * t - 0.284496736
    poly = (poly * t + 0.254829592) * t
    tail = 0.5 * poly * bell
    return jnp.where(u < 0, tail, 1.0 - tail), bell * (1.0 / math.sqrt(2.0 * math.pi))


def colsum(z):
    return jnp.sum(z, axis=0, keepdims=True)


def row_vec(ref):
    return ref[...].astype(f32).reshape(1, -1)


def up16(n):
    return -(-n // 16) * 16


class Sems:
    def __init__(self, send, recv):
        self.send, self.recv, self.used = send, recv, 0

    def copy(self, src, dst, device):
        k = self.used
        self.used += 1
        return pltpu.make_async_remote_copy(
            src_ref=src, dst_ref=dst, send_sem=self.send.at[k], recv_sem=self.recv.at[k],
            device_id=device, device_id_type=MESH)


def spread(ctx, seq, nbits, seqs):
    stages = []
    groups = [(0,)] + [tuple(range(b, min(b + 2, nbits))) for b in range(1, nbits, 2)]
    for bits in groups:
        place = [lax.rem(ctx // (1 << b), 2) for b in bits]
        others = []
        for r in range(1, 1 << len(bits)):
            device, index = ctx, 0
            for k, b in enumerate(bits):
                there = lax.rem(place[k] + (r >> k) % 2, 2)
                device = device + (there - place[k]) * (1 << b)
                index = index + there * (1 << k)
            others.append(((device, seq), index))
        mine = sum(p * (1 << k) for k, p in enumerate(place))
        stages.append((mine, others, 0))
    stages.append((seq, [((ctx, lax.rem(seq + d, seqs)), lax.rem(seq + d, seqs)) for d in range(1, seqs)], seqs // 2 - 1))
    return stages


def add_in_pairs(own, got, pair):
    if len(got) == 1:
        return own + got[0]
    rest = [g for n, g in enumerate(got) if n != pair]
    return (own + got[pair]) + (rest[0] + rest[1])


def reduce_steps(sems, stages, rows, acc, acc0, send, recv, recv0, gat, gat0):
    size = rows // 2
    mine, others, _ = stages[0]
    base = mine * size
    off = base
    into = recv0

    def held(at, count):
        return pl.ds(pl.multiple_of(acc0 + at - base, 16), count)

    cp = sems.copy(send.at[pl.ds(0, size)], recv.at[pl.ds(into, size)], others[0][0])
    cp.start()
    yield
    cp.wait()
    acc[held(off, size), :] = acc[held(off, size), :] + recv[pl.ds(into, size), :].astype(f32)
    into += size
    path = [(others, off, size)]
    for mine, others, pair in stages[1:]:
        ways = len(others) + 1
        split = size % (16 * ways) == 0
        piece = size // ways if split else size
        send[pl.ds(0, size), :] = acc[held(off, size), :].astype(bf16)
        cps = []
        for n, (device, index) in enumerate(others):
            start = pl.multiple_of(index * piece, 16) if split else 0
            cps.append(sems.copy(send.at[pl.ds(start, piece)], recv.at[pl.ds(into + n * piece, piece)], device))
        for cp in cps:
            cp.start()
        yield
        for cp in cps:
            cp.wait()
        got = [recv[pl.ds(into + n * piece, piece), :].astype(f32) for n in range(ways - 1)]
        into += (ways - 1) * piece
        if split:
            off = off + mine * piece
            size = piece
            acc[held(off, size), :] = acc[held(off, size), :] + sum(got[1:], got[0])
            path.append((others, off, size))
        else:
            acc[held(off, size), :] = add_in_pairs(send[pl.ds(0, size), :].astype(f32), got, pair)
    gat[pl.ds(pl.multiple_of(gat0 + off, 16), size), :] = acc[held(off, size), :].astype(bf16)
    for others, off, size in reversed(path):
        at = pl.ds(pl.multiple_of(gat0 + off, 16), size)
        cps = [sems.copy(gat.at[at], gat.at[at], device) for device, _ in others]
        for cp in cps:
            cp.start()
        yield
        for cp in cps:
            cp.wait()


def landing_rows(rows, nbits, seqs):
    size = rows // 2
    count = size
    for ways in [1 << len(range(b, min(b + 2, nbits))) for b in range(1, nbits, 2)] + [seqs]:
        if size % (16 * ways) == 0:
            size //= ways
        count += (ways - 1) * size
    return count


def small_steps(sems, stages, small, send, recv):
    into = 0
    for k, (_, others, pair) in enumerate(stages):
        send[k] = small[...].astype(bf16)
        cps = [sems.copy(send.at[k], recv.at[into + n], device) for n, (device, _) in enumerate(others)]
        for cp in cps:
            cp.start()
        yield
        for cp in cps:
            cp.wait()
        got = [recv[into + n].astype(f32) for n in range(len(others))]
        into += len(others)
        small[...] = add_in_pairs(send[k].astype(f32), got, pair)


def layer_kernel(
    nbits, seqs,
    xin, kept_ref, cot_hbm,
    ag_ref, as_ref, wq_ref, wk_ref, wv_ref, wo_ref, ob_ref,
    mg_ref, ms_ref, wu_ref, ub_ref, wd_ref, db_ref,
    outr, backr, gat, small_ref,
    stage, xall, cotr, marks, n_ref, qaug, kaug, vaug, kt, vtaug, prob, s_ref, ot_ref, rl_ref,
    att_t, att, act_ref, gh_ref, gml_ref, gaug, dext, erecv, s_more, acc, recv, ssend, srecv,
    local_sem, send_sems, recv_sems, ret_send, ret_recv,
):
    copies, tok, width = xin.shape
    tokp = xall.shape[1]
    own = 2 * tokp
    rows = 2 * own
    ctx = lax.axis_index("ctx")
    seq = lax.axis_index("seq")
    cc = lax.rem(ctx, 2)
    group = ctx - cc
    sems = Sems(send_sems, recv_sems)
    hd = width // HEADS
    pairs = HEADS // 2
    pw = 2 * hd
    head_cols = qaug.shape[2] // 2
    cols = 2 * head_cols
    tiles = cols // TILE
    scale = 1.0 / math.sqrt(hd)
    expo = scale * math.log2(math.e)
    ff = wu_ref.shape[1]
    chunk = tokp
    nchunk = own // chunk
    sibling = (group + 1 - cc, seq)
    stay = seq // 2 == cc

    cot_in = pltpu.make_async_copy(cot_hbm, s_ref.at[pl.ds(0, 2 * tok)], local_sem)
    cot_in.start()

    barrier = pltpu.get_barrier_semaphore()
    for dc in range(2):
        for d in range(seqs):
            if dc or d:
                pl.semaphore_signal(
                    barrier, inc=1, device_id=(group + lax.rem(cc + dc, 2), lax.rem(seq + d, seqs)), device_id_type=MESH)
    stages = spread(ctx, seq, nbits, seqs)
    greeted = 2 * seqs - 1
    for _, others, _ in stages[1:-1]:
        greeted += len(others)
        for device, _ in others:
            pl.semaphore_signal(barrier, inc=1, device_id=device, device_id_type=MESH)

    lane = lax.broadcasted_iota(jnp.int32, (1, seqs * tok), 1)
    usable = jnp.where(jnp.logical_or(kept_ref[...] == 1, lane < CLS), 0.0, MASKED)
    usable = jnp.where(lax.rem(seq, 2) == 0, usable[0:1, :], usable[1:2, :])
    wide = marks.shape[3]
    sub = lax.broadcasted_iota(jnp.int32, (16, wide), 0)
    for sh in range(seqs):
        piece = jnp.concatenate(
            [usable[:, sh * tok:(sh + 1) * tok], jnp.full((1, wide - tok), MASKED, f32)], axis=1)
        marks[0, sh] = jnp.where(sub == 0, piece, 0.0).astype(bf16)
    stage[:, tokp - 16:tokp, :] = jnp.zeros((copies, 16, width), bf16)
    stage[:, 0:tok, :] = xin[...]

    def out_copy(k, dst):
        b = lax.rem(seq + k, 2)
        return sems.copy(stage.at[b], dst.at[k], (group + seq // 2, 2 * cc + b))

    def scatter(dst):
        moves = [out_copy(0, dst), out_copy(1, dst)]
        moves[1].start()

        @pl.when(jnp.logical_not(stay))
        def _():
            moves[0].start()

        @pl.when(stay)
        def _():
            dst[0] = stage[lax.rem(seq, 2)]

        return moves

    def arrived(moves, k):
        if k:
            moves[k].wait_recv()
        else:
            @pl.when(jnp.logical_not(stay))
            def _():
                moves[0].wait_recv()

    def left(moves):
        moves[1].wait_send()

        @pl.when(jnp.logical_not(stay))
        def _():
            moves[0].wait_send()

    pl.semaphore_wait(barrier, greeted)
    moves = scatter(xall)
    marks_copy = sems.copy(marks.at[0], marks.at[1], sibling)
    marks_copy.start()

    gain = row_vec(ag_ref)
    shift = row_vec(as_ref)

    def project(pos):
        at = slice(pos * tokp, (pos + 1) * tokp)
        n, _ = norm_parts(xall[pos].astype(f32))
        low = (n * gain + shift).astype(bf16)
        n_ref[at, :] = low
        k = mm(low, wk_ref[...]).astype(bf16)
        v = mm(low, wv_ref[...]).astype(bf16)
        for p in range(pairs):
            kaug[p, at, 0:pw] = k[:, p * pw:(p + 1) * pw]
            vaug[p, at, 0:pw] = v[:, p * pw:(p + 1) * pw]

    forwards = []
    for k in range(2):
        arrived(moves, k)
        forwards.append(sems.copy(xall.at[k], xall.at[2 + k], sibling))
        forwards[k].start()
    for k in range(2):
        project(k)
    left(moves)
    cot_in.wait()
    for b in range(2):
        stage[b, 0:tok, :] = s_ref[b * tok:(b + 1) * tok, :].astype(bf16)
    cot_moves = scatter(cotr)
    marks_copy.wait()
    held = jnp.where(stay, 0, 1)
    unit = jnp.where(
        lax.broadcasted_iota(jnp.int32, (16, pw), 0) == lax.broadcasted_iota(jnp.int32, (16, pw), 1), 1.0, 0.0
    ).astype(bf16)
    lane = lax.broadcasted_iota(jnp.int32, (rows, pw), 1)
    ones = jnp.where(lane < 2, 1.0, 0.0).astype(bf16)
    for p in range(pairs):
        vaug[p, :, pw:2 * pw] = ones
    for pos in range(4):
        side = cc if pos < 2 else 1 - cc
        mark = marks[held, 2 * side + lax.rem(seq + pos, 2)]
        bias = mm(mark, unit, TN).astype(bf16)[0:tokp, :]
        for p in range(pairs):
            kaug[p, pos * tokp:(pos + 1) * tokp, pw:2 * pw] = bias
    qt = mm(wq_ref[...], n_ref[0:own, :], TT).astype(bf16)
    qaug[...] = jnp.zeros_like(qaug)
    gaug[...] = jnp.zeros_like(gaug)
    dext[...] = jnp.zeros_like(dext)
    for p in range(pairs):
        for h in range(2):
            qaug[p, h * hd:(h + 1) * hd, h * head_cols:h * head_cols + own] = qt[p * pw + h * hd:p * pw + (h + 1) * hd, :]
    for k in range(2):
        forwards[k].wait()
        project(2 + k)
    kt[...] = mm(wk_ref[...], n_ref[...], TT).astype(bf16)
    vt = mm(wv_ref[...], n_ref[...], TT).astype(bf16)
    sub = lax.broadcasted_iota(jnp.int32, (16, rows), 0)
    for p in range(pairs):
        vtaug[p, 0:pw, :] = vt[p * pw:(p + 1) * pw, :]
        vtaug[p, pw:pw + 16, :] = jnp.where(sub == 0, 1.0, 0.0).astype(bf16)

    first = jnp.where(lax.broadcasted_iota(jnp.int32, (pw, TILE), 0) == 0, 1.0, 0.0).astype(bf16)

    cut = acc.shape[0] // 2
    bounds = ((0, cut), (cut, 2 * cut), (2 * cut, rows))
    even = [s_ref.at[a:b] for a, b in bounds]
    odd = [acc.at[0:cut], acc.at[cut:2 * cut], s_more]
    count = pairs * tiles

    def place(t):
        return t // tiles, pl.ds(pl.multiple_of((t % tiles) * TILE, TILE), TILE)

    def score(t, into, c):
        p, at = place(t)
        a, b = bounds[c]
        value = mm(kaug[p, a:b, :], jnp.concatenate([qaug[p, :, at], first], axis=0))
        into[c][...] = value
        return jnp.max(value.reshape((b - a) // 8, 8, TILE), axis=0)

    def weigh(t, scores, top, ahead):
        p, at = place(t)
        top = jnp.max(top, axis=0, keepdims=True)
        tops = []
        total = None
        for c, (a, b) in enumerate(bounds):
            if ahead is not None:
                tops.append(score(lax.rem(t + 1, count), ahead, c))
            weights = jnp.exp2((scores[c][...] - top) * expo).astype(bf16)
            prob[p, a:b, at] = weights
            part = mm(vtaug[p, :, a:b], weights)
            total = part if total is None else total + part
        rl = 1.0 / total[pw:pw + 1]
        ot_ref[p, :, at] = total[0:pw] * rl
        rl_ref[p, :, at] = rl
        return jnp.maximum(jnp.maximum(tops[0], tops[1]), tops[2])

    def forward(i, top):
        return weigh(2 * i + 1, odd, weigh(2 * i, even, top, odd), even)

    tops = [score(0, even, c) for c in range(3)]
    lax.fori_loop(0, count // 2, forward, jnp.maximum(jnp.maximum(tops[0], tops[1]), tops[2]))
    for p in range(pairs):
        for h in range(2):
            att_t[p * pw + h * hd:p * pw + (h + 1) * hd, :] = ot_ref[
                p, h * hd:(h + 1) * hd, h * head_cols:h * head_cols + own
            ].astype(bf16)
    att[...] = jnp.transpose(att_t[...])

    gain2 = row_vec(mg_ref)
    shift2 = row_vec(ms_ref)
    out_bias = row_vec(ob_ref)
    up_bias = row_vec(ub_ref)
    down_bias = row_vec(db_ref)
    arrived(cot_moves, 0)
    arrived(cot_moves, 1)
    left(cot_moves)

    def mlp(i, carry):
        g_up, g_down, g_out, g_gain, g_shift = carry
        at = pl.ds(pl.multiple_of(i * chunk, 16), chunk)
        middle = xall[i].astype(f32) + (mm(att[at, :], wo_ref[...]) + out_bias)
        n, rstd = norm_parts(middle)
        low = (n * gain2 + shift2).astype(bf16)
        att[at, :] = low
        hidden = mm(low, wu_ref[...]) + up_bias
        dist, dens = normal_parts(hidden)
        act = (hidden * dist).astype(bf16)
        act_ref[at, :] = act
        stage[i] = (middle + (mm(act, wd_ref[...]) + down_bias)).astype(bf16)
        cot = cotr[i]
        gh = ((dist + hidden * dens) * mm(cot, wd_ref[...], NT)).astype(bf16)
        gh_ref[at, :] = gh
        e = mm(gh, wu_ref[...], NT)
        back = norm_back(e * gain2, n, rstd)
        s_ref[at, :] = back
        cot = cot.astype(f32)
        gml = (cot + back).astype(bf16)
        gml_ref[at, :] = gml
        return (
            g_up + colsum(gh.astype(f32)), g_down + colsum(cot), g_out + colsum(gml.astype(f32)),
            g_gain + colsum(e * n), g_shift + colsum(e),
        )

    zero = jnp.zeros((1, width), f32)
    sums = lax.fori_loop(0, nchunk, mlp, (jnp.zeros((1, ff), f32), zero, zero, zero, zero))
    small_ref[0:1, :] = sums[1]
    small_ref[1:2, :] = sums[2]
    small_ref[2:3, :] = sums[3]
    small_ref[3:4, :] = sums[4]
    ups = 4 + ff // width
    for j in range(ff // width):
        small_ref[4 + j:5 + j, :] = sums[0][:, j * width:(j + 1) * width]

    def back_copy(k, dst, sem):
        b = lax.rem(seq, 2)
        return pltpu.make_async_remote_copy(
            src_ref=stage.at[k], dst_ref=dst.at[b], send_sem=ret_send.at[2 * sem + k], recv_sem=ret_recv.at[2 * sem + b],
            device_id=(group + seq // 2, 2 * cc + lax.rem(seq + k, 2)), device_id_type=MESH)

    def send_home(dst, sem):
        moves = [back_copy(0, dst, sem), back_copy(1, dst, sem)]
        moves[1].start()

        @pl.when(jnp.logical_not(stay))
        def _():
            moves[0].start()

        @pl.when(stay)
        def _():
            dst[lax.rem(seq, 2)] = stage[0]

        return moves

    def home_again(dst, sem):
        for b in range(2):
            here = jnp.logical_and(stay, lax.rem(seq, 2) == b)

            @pl.when(jnp.logical_not(here))
            def _():
                pltpu.make_async_remote_copy(
                    src_ref=stage.at[b], dst_ref=dst.at[b], send_sem=ret_send.at[2 * sem + b],
                    recv_sem=ret_recv.at[2 * sem + b], device_id=sibling, device_id_type=MESH).wait_recv()

    out_moves = send_home(outr, 0)

    spare = own

    def split(value, count, acc0, send, send0, at=0):
        s_ref[spare:spare + count, :] = value
        half = count // 2
        acc[acc0:acc0 + half, :] = s_ref[pl.ds(pl.multiple_of(spare + cc * half, 16), half), :]
        send[pl.ds(send0, half), :] = s_ref[pl.ds(pl.multiple_of(spare + (1 - cc) * half, 16), half), :].astype(bf16)

    sets = (ff, ff, 2 * width, width, width)
    starts = [sum(sets[:j]) for j in range(5)]
    lands = [landing_rows(rows_of, nbits, seqs) for rows_of in sets]
    lands = [sum(lands[:j]) for j in range(5)]
    sends = (
        act_ref.at[:, 2 * width:3 * width], act_ref.at[:, 3 * width:4 * width],
        gh_ref.at[:, 2 * width:3 * width], gh_ref.at[0:own // 2, 3 * width:4 * width], gh_ref.at[own // 2:own, 3 * width:4 * width])
    steps = [
        reduce_steps(sems, stages, sets[j], acc, starts[j] // 2, sends[j], recv, lands[j], gat, starts[j])
        for j in range(5)
    ]

    def turn(*which):
        for j in which:
            next(steps[j], None)

    split(mm(act_ref[...], cotr[...].reshape(own, width), TN), ff, starts[0] // 2, sends[0], 0)
    turn(0)
    up = mm(att[...], gh_ref[...], TN)
    up = jnp.concatenate([up[:, j * width:(j + 1) * width] for j in range(ff // width)], axis=0)
    split(up, ff, starts[1] // 2, sends[1], 0)
    turn(1)
    split(mm(att_t[...], gml_ref[...]), width, starts[2] // 2, sends[2], 0)

    sub = lax.broadcasted_iota(jnp.int32, (16, own), 0)
    for p in range(pairs):
        for h in range(2):
            lanes = slice(h * head_cols, h * head_cols + own)
            g = mm(wo_ref[p * pw + h * hd:p * pw + (h + 1) * hd, :], gml_ref[...], NT).astype(bf16).astype(f32)
            g = (g * rl_ref[p, :, lanes]).astype(bf16)
            gaug[p, h * hd:(h + 1) * hd, lanes] = g
            delta = -colsum(g.astype(f32) * ot_ref[p, h * hd:(h + 1) * hd, lanes])
            coarse = delta.astype(bf16).astype(f32)
            dext[p, :, lanes] = jnp.where(sub == 0, coarse, jnp.where(sub == 1, delta - coarse, 0.0)).astype(bf16)

    turn(0, 1)
    for p in range(pairs):
        for half in range(2):
            lanes = slice(half * width + p * pw, half * width + (p + 1) * pw)
            act_ref[:, lanes] = mm(prob[p, half * own:(half + 1) * own, :], gaug[p], NT).astype(bf16)
    dv_own, dv_sib = act_ref.at[:, 0:width], act_ref.at[:, width:2 * width]
    dk_own, dk_sib = gh_ref.at[:, 0:width], gh_ref.at[:, width:2 * width]
    split(mm(n_ref[0:own, :], dv_own[...], TN) + mm(n_ref[own:rows, :], dv_sib[...], TN),
          width, (starts[2] + width) // 2, sends[2], width // 2)
    turn(0, 1, 2)
    wide = 3 * TILE
    nothing = jnp.zeros((pw - 16, wide), bf16)

    def backward(i, carry):
        p = i // 3
        at = pl.ds(pl.multiple_of((i % 3) * wide, TILE), wide)
        right = jnp.concatenate([gaug[p, :, at], dext[p, :, at], nothing], axis=0)
        total = None
        for a, b in bounds:
            ds = prob[p, a:b, at] * mm(vaug[p, a:b, :], right).astype(bf16)
            prob[p, a:b, at] = ds
            part = mm(kt[pl.ds(pl.multiple_of(p * pw, pw), pw), a:b], ds)
            total = part if total is None else total + part
        ot_ref[p, :, at] = total * scale
        return carry

    lax.fori_loop(0, 3, backward, 0)
    turn(0, 1, 2)
    lax.fori_loop(3, 6, backward, 0)
    turn(0, 1, 2)
    for p in range(pairs):
        for h in range(2):
            att_t[p * pw + h * hd:p * pw + (h + 1) * hd, :] = ot_ref[
                p, h * hd:(h + 1) * hd, h * head_cols:h * head_cols + own
            ].astype(bf16)
    att[...] = jnp.transpose(att_t[...])
    split(mm(n_ref[0:own, :], att[...], TN), width, starts[3] // 2, sends[3], 0)
    turn(3)

    def key_grads(half):
        for p in range(pairs):
            lanes = slice(half * width + p * pw, half * width + (p + 1) * pw)
            gh_ref[:, lanes] = (mm(prob[p, half * own:(half + 1) * own, :], qaug[p], NT) * scale).astype(bf16)

    key_grads(1)
    left(out_moves)

    def other_rows(i, carry):
        at = pl.ds(pl.multiple_of(i * chunk, 16), chunk)
        gml_ref[at, :] = (mm(dk_sib[at, :], wk_ref[...], NT) + mm(dv_sib[at, :], wv_ref[...], NT)).astype(bf16)
        return carry

    lax.fori_loop(0, nchunk, other_rows, 0)
    e_copy = sems.copy(gml_ref, erecv, sibling)
    e_copy.start()
    turn(2, 3)
    key_grads(0)
    turn(0, 1, 2, 3)
    split(mm(n_ref[0:own, :], dk_own[...], TN) + mm(n_ref[own:rows, :], dk_sib[...], TN),
          width, starts[4] // 2, sends[4], 0)
    turn(4)

    def own_rows(i, carry):
        at = pl.ds(pl.multiple_of(i * chunk, 16), chunk)
        s_ref[pl.ds(pl.multiple_of(own + i * chunk, 16), chunk), :] = (
            mm(att[at, :], wq_ref[...], NT) + mm(dk_own[at, :], wk_ref[...], NT) + mm(dv_own[at, :], wv_ref[...], NT)
        )
        return carry

    lax.fori_loop(0, nchunk, own_rows, 0)
    turn(4)
    e_copy.wait()

    moves = [back_copy(0, backr, 1), back_copy(1, backr, 1)]
    sums = (zero, zero)
    for k in range(2):
        at = slice(k * chunk, (k + 1) * chunk)
        n, rstd = norm_parts(xall[k].astype(f32))
        e = s_ref[own + k * chunk:own + (k + 1) * chunk, :] + erecv[at, :].astype(f32)
        stage[k] = (s_ref[at, :] + norm_back(e * gain, n, rstd)).astype(bf16)
        sums = (sums[0] + colsum(e * n), sums[1] + colsum(e))
        if k:
            moves[1].start()
        else:
            @pl.when(jnp.logical_not(stay))
            def _():
                moves[0].start()

            @pl.when(stay)
            def _():
                backr[lax.rem(seq, 2)] = stage[0]
    small_ref[ups:ups + 1, :] = sums[0]
    small_ref[ups + 1:ups + 2, :] = sums[1]
    small_ref[ups + 2:, :] = jnp.zeros((small_ref.shape[0] - ups - 2, width), f32)
    steps.append(small_steps(sems, stages, small_ref, ssend, srecv))
    for _ in range(len(stages) * 2):
        turn(5, 0, 1, 2, 3, 4)
    left(moves)
    home_again(outr, 0)
    home_again(backr, 1)


def unpack_kernel(cot_hbm, outr_hbm, backr_hbm, gat_hbm, small_hbm, *refs):
    outs, (cot_ref, outr, backr, gat, small, sems) = refs[:15], refs[15:]
    (out, xg, ag, as_, wq, wk, wv, wo, ob, mg, ms, wu, ub, wd, db) = outs
    copies = [
        pltpu.make_async_copy(src, dst, sems.at[k])
        for k, (src, dst) in enumerate(
            ((gat_hbm, gat), (outr_hbm, outr), (backr_hbm, backr), (cot_hbm, cot_ref), (small_hbm, small)))
    ]
    for cp in copies:
        cp.start()
    _, tok, width = cot_ref.shape
    ff = wd.shape[0]
    half = width // 2
    copies[0].wait()
    wd[...] = gat[0:ff, :].astype(f32)
    for j in range(ff // width):
        wu[:, j * width:(j + 1) * width] = gat[ff + j * width:ff + (j + 1) * width, :].astype(f32)
    for j, ref in enumerate((wo, wv)):
        at = 2 * ff + j * half
        ref[0:half, :] = gat[at:at + half, :].astype(f32)
        ref[half:width, :] = gat[at + width:at + width + half, :].astype(f32)
    for j, ref in enumerate((wq, wk)):
        at = 2 * ff + (2 + j) * width
        ref[...] = gat[at:at + width, :].astype(f32)
    copies[1].wait()
    out[...] = outr[:, 0:tok, :]
    copies[2].wait()
    copies[3].wait()
    xg[...] = cot_ref[...] + backr[:, 0:tok, :].astype(f32)
    copies[4].wait()
    for j in range(ff // width):
        ub[0:1, j * width:(j + 1) * width] = small[4 + j:5 + j, :]
    ups = 4 + ff // width
    for j, ref in ((0, db), (1, ob), (2, mg), (3, ms), (ups, ag), (ups + 1, as_)):
        ref[...] = small[j:j + 1, :]


def body(nctx, seqs, layer_input, gene_kept, attn_gain, attn_shift, w_query, w_key, w_value, w_out, out_bias,
         mlp_gain, mlp_shift, w_up, up_bias, w_down, down_bias, cotangent):
    copies, tok, width = layer_input.shape
    tokp = up16(tok)
    own = 2 * tokp
    rows = 2 * own
    ff = w_up.shape[1]
    nbits = nctx.bit_length() - 1
    vmem = pl.BlockSpec(memory_space=pltpu.VMEM)
    hbm = pl.BlockSpec(memory_space=pl.ANY)
    head_cols = -(-own // 128) * 128
    cols = 2 * head_cols
    pairs = HEADS // 2
    pw = width // 2
    grad_rows = 2 * ff + 4 * width
    sets = (ff, ff, 2 * width, width, width)
    landing = sum(landing_rows(r, nbits, seqs) for r in sets)
    peers = 1 + sum((1 << len(range(b, min(b + 2, nbits)))) - 1 for b in range(1, nbits, 2)) + seqs - 1
    sets = (ff, ff, 2 * width, width, width)
    landing = sum(landing_rows(r, nbits, seqs) for r in sets)
    peers = 1 + sum((1 << len(range(b, min(b + 2, nbits)))) - 1 for b in range(1, nbits, 2)) + seqs - 1
    ncopy = 8 + (2 * len(sets) + 1) * peers
    home = jax.ShapeDtypeStruct((copies, tokp, width), bf16)
    outr, backr, gat, small = pl.pallas_call(
        partial(layer_kernel, nbits, seqs),
        out_shape=(
            home, home,
            jax.ShapeDtypeStruct((grad_rows, width), bf16),
            jax.ShapeDtypeStruct((16, width), f32),
        ),
        in_specs=[vmem, vmem, hbm] + [vmem] * 13,
        out_specs=(vmem,) * 4,
        scratch_shapes=[
            pltpu.VMEM((copies, tokp, width), bf16),
            pltpu.VMEM((4, tokp, width), bf16),
            pltpu.VMEM((copies, tokp, width), bf16),
            pltpu.VMEM((2, seqs, 16, -(-tokp // 128) * 128), bf16),
            pltpu.VMEM((rows, width), bf16),
            pltpu.VMEM((pairs, pw, cols), bf16),
            pltpu.VMEM((pairs, rows, width), bf16),
            pltpu.VMEM((pairs, rows, width), bf16),
            pltpu.VMEM((width, rows), bf16),
            pltpu.VMEM((pairs, pw + 16, rows), bf16),
            pltpu.VMEM((pairs, rows, cols), bf16),
            pltpu.VMEM((rows, TILE), f32),
            pltpu.VMEM((pairs, pw, cols), f32),
            pltpu.VMEM((pairs, 1, cols), f32),
            pltpu.VMEM((width, own), bf16),
            pltpu.VMEM((own, width), bf16),
            pltpu.VMEM((own, ff), bf16),
            pltpu.VMEM((own, ff), bf16),
            pltpu.VMEM((own, width), bf16),
            pltpu.VMEM((pairs, pw, cols), bf16),
            pltpu.VMEM((pairs, 16, cols), bf16),
            pltpu.VMEM((own, width), bf16),
            pltpu.VMEM((rows - grad_rows // 2, TILE), f32),
            pltpu.VMEM((grad_rows // 2, width), f32),
            pltpu.VMEM((landing, width), bf16),
            pltpu.VMEM((nbits + 1, 16, width), bf16),
            pltpu.VMEM((peers, 16, width), bf16),
            pltpu.SemaphoreType.DMA,
            pltpu.SemaphoreType.DMA((ncopy,)),
            pltpu.SemaphoreType.DMA((ncopy,)),
            pltpu.SemaphoreType.DMA((4,)),
            pltpu.SemaphoreType.DMA((4,)),
        ],
        compiler_params=pltpu.CompilerParams(collective_id=1, has_side_effects=True, vmem_limit_bytes=63 * 2**20),
        name="layer",
    )(layer_input, gene_kept, cotangent.reshape(copies * tok, width), attn_gain, attn_shift, w_query, w_key, w_value,
      w_out, out_bias, mlp_gain, mlp_shift, w_up, up_bias, w_down, down_bias)
    line = jax.ShapeDtypeStruct((1, width), f32)
    square = jax.ShapeDtypeStruct((width, width), f32)
    outs = pl.pallas_call(
        unpack_kernel,
        out_shape=(
            jax.ShapeDtypeStruct((copies, tok, width), bf16), jax.ShapeDtypeStruct((copies, tok, width), f32),
            line, line, square, square, square, square, line, line, line,
            jax.ShapeDtypeStruct((width, ff), f32), jax.ShapeDtypeStruct((1, ff), f32),
            jax.ShapeDtypeStruct((ff, width), f32), line,
        ),
        in_specs=[hbm] * 5,
        out_specs=(vmem,) * 15,
        scratch_shapes=[
            pltpu.VMEM(cotangent.shape, f32), pltpu.VMEM(home.shape, bf16), pltpu.VMEM(home.shape, bf16),
            pltpu.VMEM((grad_rows, width), bf16), pltpu.VMEM((16, width), f32), pltpu.SemaphoreType.DMA((5,)),
        ],
        compiler_params=pltpu.CompilerParams(vmem_limit_bytes=63 * 2**20),
        name="unpack",
    )(cotangent, outr, backr, gat, small)
    return tuple(o.reshape(-1) if o.shape[0] == 1 else o for o in outs)


def solution(mesh):
    tokens = P("ctx", "seq", None)
    return jax.shard_map(
        partial(body, mesh.shape["ctx"], mesh.shape["seq"]),
        mesh=mesh,
        in_specs=(tokens, P("ctx", None)) + (P(),) * 13 + (tokens,),
        out_specs=(tokens, tokens) + (P(),) * 13,
        check_vma=False,
    )
```

```python
import math
from functools import partial

import jax
import jax.numpy as jnp
from jax import lax
from jax.experimental import pallas as pl
from jax.experimental.pallas import tpu as pltpu
from jax.sharding import PartitionSpec as P

bf16 = jnp.bfloat16
f32 = jnp.float32
HEADS = 4
CLS = 8
TILE = 256
MASKED = -8.0e9
NN = (((1,), (0,)), ((), ()))
NT = (((1,), (1,)), ((), ()))
TN = (((0,), (0,)), ((), ()))
TT = (((0,), (1,)), ((), ()))
MESH = pl.DeviceIdType.MESH


def mm(a, b, dims=NN):
    return lax.dot_general(a, b, dims, preferred_element_type=f32)


def norm_parts(z):
    average = jnp.mean(z, axis=-1, keepdims=True)
    centred = z - average
    spread = jnp.mean(centred * centred, axis=-1, keepdims=True)
    rstd = lax.rsqrt(spread + 1e-05)
    return centred * rstd, rstd


def norm_back(f, n, rstd):
    mean_f = jnp.mean(f, axis=-1, keepdims=True)
    mean_fn = jnp.mean(f * n, axis=-1, keepdims=True)
    return rstd * (f - mean_f - n * mean_fn)


def normal_parts(u):
    bell = jnp.exp2(u * u * (-0.5 * math.log2(math.e)))
    t = 1.0 / (1.0 + (0.3275911 / math.sqrt(2.0)) * jnp.abs(u))
    poly = 1.061405429 * t - 1.453152027
    poly = poly * t + 1.421413741
    poly = poly * t - 0.284496736
    poly = (poly * t + 0.254829592) * t
    tail = 0.5 * poly * bell
    return jnp.where(u < 0, tail, 1.0 - tail), bell * (1.0 / math.sqrt(2.0 * math.pi))


def colsum(z):
    return jnp.sum(z, axis=0, keepdims=True)


def row_vec(ref):
    return ref[...].astype(f32).reshape(1, -1)


def up16(n):
    return -(-n // 16) * 16


class Sems:
    def __init__(self, send, recv):
        self.send, self.recv, self.used = send, recv, 0

    def copy(self, src, dst, device):
        k = self.used
        self.used += 1
        return pltpu.make_async_remote_copy(
            src_ref=src, dst_ref=dst, send_sem=self.send.at[k], recv_sem=self.recv.at[k],
            device_id=device, device_id_type=MESH)


def bit_groups(nbits, first):
    return [tuple(range(first))] + [tuple(range(b, min(b + 2, nbits))) for b in range(first, nbits, 2)]


def spread(ctx, seq, nbits, seqs, first):
    stages = []
    for bits in bit_groups(nbits, first):
        place = [lax.rem(ctx // (1 << b), 2) for b in bits]
        others = []
        for r in range(1, 1 << len(bits)):
            device, index = ctx, 0
            for k, b in enumerate(bits):
                there = lax.rem(place[k] + (r >> k) % 2, 2)
                device = device + (there - place[k]) * (1 << b)
                index = index + there * (1 << k)
            others.append(((device, seq), index))
        mine = sum(p * (1 << k) for k, p in enumerate(place))
        stages.append((mine, others, list(range(len(others) + 1))))
    half = seqs // 2
    stages.append((
        seq, [((ctx, lax.rem(seq + d, seqs)), lax.rem(seq + d, seqs)) for d in range(1, seqs)],
        [n // 2 + n % 2 * half for n in range(seqs)]))
    return stages


def add_in_pairs(values, order):
    values = [values[n] for n in order]
    while len(values) > 1:
        values = [a + b for a, b in zip(values[::2], values[1::2])]
    return values[0]


def reduce_steps(sems, stages, rows, acc, acc0, send, recv, recv0, gat, gat0, split_first, done):
    into = recv0
    path = []
    if split_first:
        size = rows // 2
        mine, others, _ = stages[0]
        off = mine * size
    else:
        size = rows
        off = 0
    base = off

    def held(at, count):
        return pl.ds(pl.multiple_of(acc0 + at - base, 16), count)

    if split_first:
        cp = sems.copy(send.at[pl.ds(0, size)], recv.at[pl.ds(into, size)], others[0][0])
        cp.start()
        yield
        cp.wait()
        acc[held(off, size), :] = acc[held(off, size), :] + recv[pl.ds(into, size), :].astype(f32)
        into += size
        path.append((others, off, size))
        stages = stages[1:]
    for mine, others, order in stages:
        ways = len(others) + 1
        split = size % (16 * ways) == 0
        piece = size // ways if split else size
        send[pl.ds(0, size), :] = acc[held(off, size), :].astype(bf16)
        cps = []
        for n, (device, index) in enumerate(others):
            start = pl.multiple_of(index * piece, 16) if split else 0
            cps.append(sems.copy(send.at[pl.ds(start, piece)], recv.at[pl.ds(into + n * piece, piece)], device))
        for cp in cps:
            cp.start()
        yield
        for cp in cps:
            cp.wait()
        got = [recv[pl.ds(into + n * piece, piece), :].astype(f32) for n in range(ways - 1)]
        into += (ways - 1) * piece
        if split:
            off = off + mine * piece
            size = piece
            acc[held(off, size), :] = acc[held(off, size), :] + sum(got[1:], got[0])
            path.append((others, off, size))
        else:
            acc[held(off, size), :] = add_in_pairs([send[pl.ds(0, size), :].astype(f32)] + got, order)
    gat[pl.ds(pl.multiple_of(gat0 + off, 16), size), :] = acc[held(off, size), :].astype(bf16)
    for others, off, size in reversed(path):
        at = pl.ds(pl.multiple_of(gat0 + off, 16), size)
        cps = [sems.copy(gat.at[at], gat.at[at], device) for device, _ in others]
        for cp in cps:
            cp.start()
        yield
        for cp in cps:
            cp.wait()
    done()


def landing_rows(rows, nbits, seqs, split_first):
    ways_of = [1 << len(bits) for bits in bit_groups(nbits, 1 if split_first else 3)] + [seqs]
    count = 0
    size = rows
    if split_first:
        size = count = rows // 2
        ways_of = ways_of[1:]
    for ways in ways_of:
        if size % (16 * ways) == 0:
            size //= ways
        count += (ways - 1) * size
    return count


def small_steps(sems, stages, small, send, recv, done):
    into = 0
    for k, (_, others, order) in enumerate(stages):
        send[k] = small[...].astype(bf16)
        cps = [sems.copy(send.at[k], recv.at[into + n], device) for n, (device, _) in enumerate(others)]
        for cp in cps:
            cp.start()
        yield
        for cp in cps:
            cp.wait()
        got = [recv[into + n].astype(f32) for n in range(len(others))]
        into += len(others)
        small[...] = add_in_pairs([send[k].astype(f32)] + got, order)
    done()


def layer_kernel(
    nbits, seqs,
    xin_hbm, kept_ref, cot_hbm,
    ag_ref, as_ref, wq_ref, wk_ref, wv_ref, wo_ref, ob_ref,
    mg_ref, ms_ref, wu_ref, ub_ref, wd_ref, db_ref,
    outr, backr, gat_hbm, small_hbm,
    gat, small_ref, xin, stage, xall, cotr, marks, n_ref, qaug, kaug, vaug, kt, vtaug, prob, s_ref, ot_ref, rl_ref,
    att_t, att, act_ref, gh_ref, gml_ref, gaug, dext, erecv, s_more, acc, recv, ssend, srecv,
    local_sems, send_sems, recv_sems, ret_send, ret_recv,
):
    copies, tok, width = xin_hbm.shape
    tokp = xall.shape[1]
    own = 2 * tokp
    rows = 2 * own
    ctx = lax.axis_index("ctx")
    seq = lax.axis_index("seq")
    cc = lax.rem(ctx, 2)
    group = ctx - cc
    sems = Sems(send_sems, recv_sems)
    hd = width // HEADS
    pairs = HEADS // 2
    pw = 2 * hd
    head_cols = qaug.shape[2] // 2
    cols = 2 * head_cols
    tiles = cols // TILE
    scale = 1.0 / math.sqrt(hd)
    expo = scale * math.log2(math.e)
    ff = wu_ref.shape[1]
    chunk = tokp
    nchunk = own // chunk
    sibling = (group + 1 - cc, seq)
    stay = seq // 2 == cc

    keep_in = pltpu.make_async_copy(xin_hbm, xin, local_sems.at[0])
    keep_in.start()
    cot_in = pltpu.make_async_copy(cot_hbm, s_ref.at[pl.ds(0, 2 * tok)], local_sems.at[1])
    cot_in.start()

    barrier = pltpu.get_barrier_semaphore()
    for dc in range(2):
        for d in range(seqs):
            if dc or d:
                pl.semaphore_signal(
                    barrier, inc=1, device_id=(group + lax.rem(cc + dc, 2), lax.rem(seq + d, seqs)), device_id_type=MESH)
    stages = spread(ctx, seq, nbits, seqs, 1)
    stages_flat = spread(ctx, seq, nbits, seqs, min(nbits, 3))
    met = [device for device, _ in stages_flat[0][1][1:]]
    met += [device for _, others, _ in stages_flat[1:-1] for device, _ in others]
    for device in met:
        pl.semaphore_signal(barrier, inc=1, device_id=device, device_id_type=MESH)
    greeted = 2 * seqs - 1 + len(met)

    lane = lax.broadcasted_iota(jnp.int32, (1, seqs * tok), 1)
    usable = jnp.where(jnp.logical_or(kept_ref[...] == 1, lane < CLS), 0.0, MASKED)
    usable = jnp.where(lax.rem(seq, 2) == 0, usable[0:1, :], usable[1:2, :])
    wide = marks.shape[3]
    sub = lax.broadcasted_iota(jnp.int32, (16, wide), 0)
    for sh in range(seqs):
        piece = jnp.concatenate(
            [usable[:, sh * tok:(sh + 1) * tok], jnp.full((1, wide - tok), MASKED, f32)], axis=1)
        marks[0, sh] = jnp.where(sub == 0, piece, 0.0).astype(bf16)
    stage[:, tokp - 16:tokp, :] = jnp.zeros((copies, 16, width), bf16)
    keep_in.wait()
    stage[:, 0:tok, :] = xin[...]

    def out_copy(k, dst):
        b = lax.rem(seq + k, 2)
        return sems.copy(stage.at[b], dst.at[k], (group + seq // 2, 2 * cc + b))

    def scatter(dst):
        moves = [out_copy(0, dst), out_copy(1, dst)]
        moves[1].start()

        @pl.when(jnp.logical_not(stay))
        def _():
            moves[0].start()

        @pl.when(stay)
        def _():
            dst[0] = stage[lax.rem(seq, 2)]

        return moves

    def arrived(moves, k):
        if k:
            moves[k].wait_recv()
        else:
            @pl.when(jnp.logical_not(stay))
            def _():
                moves[0].wait_recv()

    def left(moves):
        moves[1].wait_send()

        @pl.when(jnp.logical_not(stay))
        def _():
            moves[0].wait_send()

    qaug[...] = jnp.zeros_like(qaug)
    gaug[...] = jnp.zeros_like(gaug)
    dext[...] = jnp.zeros_like(dext)
    lane = lax.broadcasted_iota(jnp.int32, (rows, pw), 1)
    sub = lax.broadcasted_iota(jnp.int32, (16, rows), 0)
    for p in range(pairs):
        vaug[p, :, pw:2 * pw] = jnp.where(lane < 2, 1.0, 0.0).astype(bf16)
        vtaug[p, pw:pw + 16, :] = jnp.where(sub == 0, 1.0, 0.0).astype(bf16)
    pl.semaphore_wait(barrier, greeted)
    moves = scatter(xall)
    marks_copy = sems.copy(marks.at[0], marks.at[1], sibling)
    marks_copy.start()

    gain = row_vec(ag_ref)
    shift = row_vec(as_ref)

    def project(pos):
        at = slice(pos * tokp, (pos + 1) * tokp)
        n, _ = norm_parts(xall[pos].astype(f32))
        low = (n * gain + shift).astype(bf16)
        n_ref[at, :] = low
        k = mm(low, wk_ref[...]).astype(bf16)
        v = mm(low, wv_ref[...]).astype(bf16)
        for p in range(pairs):
            kaug[p, at, 0:pw] = k[:, p * pw:(p + 1) * pw]
            vaug[p, at, 0:pw] = v[:, p * pw:(p + 1) * pw]

    forwards = []
    for k in range(2):
        arrived(moves, k)
        forwards.append(sems.copy(xall.at[k], xall.at[2 + k], sibling))
        forwards[k].start()
    for k in range(2):
        project(k)
    left(moves)
    cot_in.wait()
    for b in range(2):
        stage[b, 0:tok, :] = s_ref[b * tok:(b + 1) * tok, :].astype(bf16)
    cot_moves = scatter(cotr)
    marks_copy.wait()
    held = jnp.where(stay, 0, 1)
    unit = jnp.where(
        lax.broadcasted_iota(jnp.int32, (16, pw), 0) == lax.broadcasted_iota(jnp.int32, (16, pw), 1), 1.0, 0.0
    ).astype(bf16)
    for pos in range(4):
        side = cc if pos < 2 else 1 - cc
        mark = marks[held, 2 * side + lax.rem(seq + pos, 2)]
        bias = mm(mark, unit, TN).astype(bf16)[0:tokp, :]
        for p in range(pairs):
            kaug[p, pos * tokp:(pos + 1) * tokp, pw:2 * pw] = bias
    qt = mm(wq_ref[...], n_ref[0:own, :], TT).astype(bf16)
    for p in range(pairs):
        for h in range(2):
            qaug[p, h * hd:(h + 1) * hd, h * head_cols:h * head_cols + own] = qt[p * pw + h * hd:p * pw + (h + 1) * hd, :]
    for k in range(2):
        forwards[k].wait()
        project(2 + k)
    kt[...] = mm(wk_ref[...], n_ref[...], TT).astype(bf16)
    vt = mm(wv_ref[...], n_ref[...], TT).astype(bf16)
    for p in range(pairs):
        vtaug[p, 0:pw, :] = vt[p * pw:(p + 1) * pw, :]

    first = jnp.where(lax.broadcasted_iota(jnp.int32, (pw, TILE), 0) == 0, 1.0, 0.0).astype(bf16)

    cut = (rows - s_more.shape[0]) // 2
    bounds = ((0, cut), (cut, 2 * cut), (2 * cut, rows))
    even = [s_ref.at[a:b] for a, b in bounds]
    odd = [acc.at[0:cut], acc.at[cut:2 * cut], s_more]
    count = pairs * tiles

    def place(t):
        return t // tiles, pl.ds(pl.multiple_of((t % tiles) * TILE, TILE), TILE)

    def score(t, into, c):
        p, at = place(t)
        a, b = bounds[c]
        value = mm(kaug[p, a:b, :], jnp.concatenate([qaug[p, :, at], first], axis=0))
        into[c][...] = value
        return jnp.max(value.reshape((b - a) // 8, 8, TILE), axis=0)

    def weigh(t, scores, top, ahead):
        p, at = place(t)
        top = jnp.max(top, axis=0, keepdims=True)
        tops = []
        total = None
        for c, (a, b) in enumerate(bounds):
            if ahead is not None:
                tops.append(score(lax.rem(t + 1, count), ahead, c))
            weights = jnp.exp2((scores[c][...] - top) * expo).astype(bf16)
            prob[p, a:b, at] = weights
            part = mm(vtaug[p, :, a:b], weights)
            total = part if total is None else total + part
        rl = 1.0 / total[pw:pw + 1]
        ot_ref[p, :, at] = total[0:pw] * rl
        rl_ref[p, :, at] = rl
        return jnp.maximum(jnp.maximum(tops[0], tops[1]), tops[2])

    def forward(i, top):
        return weigh(2 * i + 1, odd, weigh(2 * i, even, top, odd), even)

    tops = [score(0, even, c) for c in range(3)]
    lax.fori_loop(0, count // 2, forward, jnp.maximum(jnp.maximum(tops[0], tops[1]), tops[2]))
    for p in range(pairs):
        for h in range(2):
            att_t[p * pw + h * hd:p * pw + (h + 1) * hd, :] = ot_ref[
                p, h * hd:(h + 1) * hd, h * head_cols:h * head_cols + own
            ].astype(bf16)
    att[...] = jnp.transpose(att_t[...])

    gain2 = row_vec(mg_ref)
    shift2 = row_vec(ms_ref)
    out_bias = row_vec(ob_ref)
    up_bias = row_vec(ub_ref)
    down_bias = row_vec(db_ref)
    arrived(cot_moves, 0)
    arrived(cot_moves, 1)
    left(cot_moves)

    def mlp(i, carry):
        g_up, g_down, g_out, g_gain, g_shift = carry
        at = pl.ds(pl.multiple_of(i * chunk, 16), chunk)
        middle = xall[i].astype(f32) + (mm(att[at, :], wo_ref[...]) + out_bias)
        n, rstd = norm_parts(middle)
        low = (n * gain2 + shift2).astype(bf16)
        att[at, :] = low
        hidden = mm(low, wu_ref[...]) + up_bias
        dist, dens = normal_parts(hidden)
        act = (hidden * dist).astype(bf16)
        act_ref[at, :] = act
        stage[i] = (middle + (mm(act, wd_ref[...]) + down_bias)).astype(bf16)
        cot = cotr[i]
        gh = ((dist + hidden * dens) * mm(cot, wd_ref[...], NT)).astype(bf16)
        gh_ref[at, :] = gh
        e = mm(gh, wu_ref[...], NT)
        back = norm_back(e * gain2, n, rstd)
        s_ref[at, :] = back
        cot = cot.astype(f32)
        gml = (cot + back).astype(bf16)
        gml_ref[at, :] = gml
        return (
            g_up + colsum(gh.astype(f32)), g_down + colsum(cot), g_out + colsum(gml.astype(f32)),
            g_gain + colsum(e * n), g_shift + colsum(e),
        )

    zero = jnp.zeros((1, width), f32)
    sums = lax.fori_loop(0, nchunk, mlp, (jnp.zeros((1, ff), f32), zero, zero, zero, zero))
    small_ref[0:1, :] = sums[1]
    small_ref[1:2, :] = sums[2]
    small_ref[2:3, :] = sums[3]
    small_ref[3:4, :] = sums[4]
    ups = 4 + ff // width
    for j in range(ff // width):
        small_ref[4 + j:5 + j, :] = sums[0][:, j * width:(j + 1) * width]

    def back_copy(k, dst, sem):
        b = lax.rem(seq, 2)
        return pltpu.make_async_remote_copy(
            src_ref=stage.at[k], dst_ref=dst.at[b], send_sem=ret_send.at[2 * sem + k], recv_sem=ret_recv.at[2 * sem + b],
            device_id=(group + seq // 2, 2 * cc + lax.rem(seq + k, 2)), device_id_type=MESH)

    def send_block(move, k, dst, sem):
        if k:
            move.start()
            return

        @pl.when(jnp.logical_not(stay))
        def _():
            move.start()

        @pl.when(stay)
        def _():
            pltpu.make_async_copy(stage.at[0], dst.at[lax.rem(seq, 2)], local_sems.at[2 + sem]).start()

    def left_home(moves, dst, sem):
        moves[1].wait_send()

        @pl.when(jnp.logical_not(stay))
        def _():
            moves[0].wait_send()

        @pl.when(stay)
        def _():
            pltpu.make_async_copy(stage.at[0], dst.at[lax.rem(seq, 2)], local_sems.at[2 + sem]).wait()

    def home_again(dst, sem):
        for b in range(2):
            here = jnp.logical_and(stay, lax.rem(seq, 2) == b)

            @pl.when(jnp.logical_not(here))
            def _():
                pltpu.make_async_remote_copy(
                    src_ref=stage.at[b], dst_ref=dst.at[b], send_sem=ret_send.at[2 * sem + b],
                    recv_sem=ret_recv.at[2 * sem + b], device_id=sibling, device_id_type=MESH).wait_recv()

    out_moves = [back_copy(0, outr, 0), back_copy(1, outr, 0)]
    for k in range(2):
        send_block(out_moves[k], k, outr, 0)

    sets = (ff, ff, 2 * width, width, width)
    halved = (True, True, False, False, False)
    starts = [sum(sets[:j]) for j in range(5)]
    lands = [landing_rows(sets[j], nbits, seqs, halved[j]) for j in range(5)]
    lands = [sum(lands[:j]) for j in range(5)]
    kept = [sets[j] // 2 if halved[j] else sets[j] for j in range(5)]
    kept = [sum(kept[:j]) for j in range(5)]
    sends = (
        act_ref.at[:, 2 * width:3 * width], act_ref.at[:, 3 * width:4 * width],
        gh_ref.at[:, 2 * width:3 * width], gh_ref.at[0:own // 2, 3 * width:4 * width], gh_ref.at[own // 2:own, 3 * width:4 * width])
    written = []

    def write_out(j):
        at = pl.ds(starts[j], sets[j])
        copy = pltpu.make_async_copy(gat.at[at], gat_hbm.at[at], local_sems.at[4 + j])
        copy.start()
        written.append(copy)

    def write_small():
        copy = pltpu.make_async_copy(small_ref, small_hbm, local_sems.at[9])
        copy.start()
        written.append(copy)

    steps = [
        reduce_steps(
            sems, stages if halved[j] else stages_flat, sets[j], acc, kept[j], sends[j], recv, lands[j], gat, starts[j],
            halved[j], partial(write_out, j))
        for j in range(5)
    ]

    def turn(*which):
        for j in which:
            next(steps[j], None)

    def split(j, make, half):
        acc[kept[j]:kept[j] + half, :] = make(cc)
        sends[j][0:half, :] = make(1 - cc).astype(bf16)

    def part(w, count):
        return pl.ds(pl.multiple_of(w * count, 128), count)

    def up_half(w):
        value = mm(att[...], gh_ref[:, part(w, ff // 2)], TN)
        return jnp.concatenate([value[:, j * width:(j + 1) * width] for j in range(ff // width // 2)], axis=0)

    split(0, lambda w: mm(act_ref[:, part(w, ff // 2)], cotr[...].reshape(own, width), TN), ff // 2)
    turn(0)
    split(1, up_half, ff // 2)
    turn(1)
    acc[kept[2]:kept[2] + width, :] = mm(att_t[...], gml_ref[...])

    sub = lax.broadcasted_iota(jnp.int32, (16, own), 0)
    for p in range(pairs):
        for h in range(2):
            lanes = slice(h * head_cols, h * head_cols + own)
            g = mm(wo_ref[p * pw + h * hd:p * pw + (h + 1) * hd, :], gml_ref[...], NT).astype(bf16).astype(f32)
            g = (g * rl_ref[p, :, lanes]).astype(bf16)
            gaug[p, h * hd:(h + 1) * hd, lanes] = g
            delta = -colsum(g.astype(f32) * ot_ref[p, h * hd:(h + 1) * hd, lanes])
            coarse = delta.astype(bf16).astype(f32)
            dext[p, :, lanes] = jnp.where(sub == 0, coarse, jnp.where(sub == 1, delta - coarse, 0.0)).astype(bf16)

    turn(0, 1)
    for p in range(pairs):
        for half in range(2):
            lanes = slice(half * width + p * pw, half * width + (p + 1) * pw)
            act_ref[:, lanes] = mm(prob[p, half * own:(half + 1) * own, :], gaug[p], NT).astype(bf16)
    dv_own, dv_sib = act_ref.at[:, 0:width], act_ref.at[:, width:2 * width]
    dk_own, dk_sib = gh_ref.at[:, 0:width], gh_ref.at[:, width:2 * width]
    acc[kept[2] + width:kept[2] + 2 * width, :] = mm(n_ref[0:own, :], dv_own[...], TN) + mm(n_ref[own:rows, :], dv_sib[...], TN)
    turn(2)
    wide = 3 * TILE
    nothing = jnp.zeros((pw - 16, wide), bf16)

    def backward(i, carry):
        p = i // 3
        at = pl.ds(pl.multiple_of((i % 3) * wide, TILE), wide)
        right = jnp.concatenate([gaug[p, :, at], dext[p, :, at], nothing], axis=0)
        total = None
        for a, b in bounds:
            ds = prob[p, a:b, at] * mm(vaug[p, a:b, :], right).astype(bf16)
            prob[p, a:b, at] = ds
            part = mm(kt[pl.ds(pl.multiple_of(p * pw, pw), pw), a:b], ds)
            total = part if total is None else total + part
        ot_ref[p, :, at] = total * scale
        return carry

    lax.fori_loop(0, 1, backward, 0)
    turn(0, 1)
    lax.fori_loop(1, 4, backward, 0)
    turn(2)
    lax.fori_loop(4, 5, backward, 0)
    turn(0, 1)
    lax.fori_loop(5, 6, backward, 0)
    for p in range(pairs):
        for h in range(2):
            att_t[p * pw + h * hd:p * pw + (h + 1) * hd, :] = ot_ref[
                p, h * hd:(h + 1) * hd, h * head_cols:h * head_cols + own
            ].astype(bf16)
    att[...] = jnp.transpose(att_t[...])
    acc[kept[3]:kept[3] + width, :] = mm(n_ref[0:own, :], att[...], TN)
    turn(2, 3)
    left_home(out_moves, outr, 0)

    def key_grads(pos):
        half, k = pos // 2, pos % 2
        for p in range(pairs):
            lanes = slice(half * width + p * pw, half * width + (p + 1) * pw)
            gh_ref[k * chunk:(k + 1) * chunk, lanes] = (
                mm(prob[p, pos * chunk:(pos + 1) * chunk, :], qaug[p], NT) * scale).astype(bf16)

    e_copies = []
    back_moves = [back_copy(0, backr, 1), back_copy(1, backr, 1)]
    sums = (zero, zero)
    for k in range(2):
        at = slice(k * chunk, (k + 1) * chunk)
        key_grads(2 + k)
        gml_ref[at, :] = (mm(dk_sib[at, :], wk_ref[...], NT) + mm(dv_sib[at, :], wv_ref[...], NT)).astype(bf16)
        e_copies.append(sems.copy(gml_ref.at[at], erecv.at[at], sibling))
        e_copies[k].start()
        key_grads(k)
        if k == 0:
            turn(2, 3)
        else:
            acc[kept[4]:kept[4] + width, :] = mm(n_ref[0:own, :], dk_own[...], TN) + mm(n_ref[own:rows, :], dk_sib[...], TN)
            turn(4, 0, 1, 3)
        e = mm(att[at, :], wq_ref[...], NT) + mm(dk_own[at, :], wk_ref[...], NT) + mm(dv_own[at, :], wv_ref[...], NT)
        n, rstd = norm_parts(xall[k].astype(f32))
        e_copies[k].wait()
        e = e + erecv[at, :].astype(f32)
        stage[k] = (s_ref[at, :] + norm_back(e * gain, n, rstd)).astype(bf16)
        sums = (sums[0] + colsum(e * n), sums[1] + colsum(e))
        send_block(back_moves[k], k, backr, 1)
    small_ref[ups:ups + 1, :] = sums[0]
    small_ref[ups + 1:ups + 2, :] = sums[1]
    small_ref[ups + 2:, :] = jnp.zeros((small_ref.shape[0] - ups - 2, width), f32)
    steps.append(small_steps(sems, stages_flat, small_ref, ssend, srecv, write_small))
    turn(5)
    turn(4, 5, 3, 2)
    turn(4, 5, 0, 1)
    turn(4, 0, 1)
    for _ in range(len(stages) * 2):
        turn(5, 4, 0, 1, 2, 3)
    left_home(back_moves, backr, 1)
    home_again(outr, 0)
    home_again(backr, 1)
    for copy in written:
        copy.wait()


def unpack_kernel(cot_hbm, outr_hbm, backr_hbm, gat_hbm, small_hbm, *refs):
    hbm, vec_hbm, vec = refs[:8], refs[8:15], refs[15:22]
    cot_ref, outr, backr, gat, small, out, xg, wide, up, sq, in_sems, out_sems = refs[22:]
    out_hbm, xg_hbm, wq_hbm, wk_hbm, wv_hbm, wo_hbm, wu_hbm, wd_hbm = hbm
    ag, as_, ob, mg, ms, ub, db = vec
    _, tok, width = cot_ref.shape
    ff = wide.shape[0]
    cuts = ((0, ff), (ff, 2 * ff), (2 * ff, 2 * ff + 4 * width))
    ins = [
        pltpu.make_async_copy(src, dst, in_sems.at[k])
        for k, (src, dst) in enumerate(
            [(gat_hbm.at[a:b], gat.at[a:b]) for a, b in cuts]
            + [(outr_hbm, outr), (backr_hbm, backr), (cot_hbm, cot_ref), (small_hbm, small)])
    ]
    for cp in ins:
        cp.start()
    outs = []

    def put(src, dst):
        cp = pltpu.make_async_copy(src, dst, out_sems.at[len(outs)])
        cp.start()
        outs.append(cp)

    ins[0].wait()
    wide[...] = gat[0:ff, :].astype(f32)
    put(wide, wd_hbm)
    ins[1].wait()
    for j in range(ff // width):
        up[:, j * width:(j + 1) * width] = gat[ff + j * width:ff + (j + 1) * width, :].astype(f32)
    put(up, wu_hbm)
    ins[4].wait()
    ins[5].wait()
    xg[...] = cot_ref[...] + backr[:, 0:tok, :].astype(f32)
    put(xg, xg_hbm)
    ins[2].wait()
    for j, dst in enumerate((wo_hbm, wv_hbm, wq_hbm, wk_hbm)):
        at = 2 * ff + j * width
        sq[j] = gat[at:at + width, :].astype(f32)
        put(sq.at[j], dst)
    ins[3].wait()
    out[...] = outr[:, 0:tok, :]
    put(out, out_hbm)
    ins[6].wait()
    for j in range(ff // width):
        ub[0:1, j * width:(j + 1) * width] = small[4 + j:5 + j, :]
    ups = 4 + ff // width
    for j, ref in ((0, db), (1, ob), (2, mg), (3, ms), (ups, ag), (ups + 1, as_)):
        ref[...] = small[j:j + 1, :]
    for src, dst in zip(vec, vec_hbm):
        put(src, dst)
    for cp in outs:
        cp.wait()


def body(nctx, seqs, layer_input, gene_kept, attn_gain, attn_shift, w_query, w_key, w_value, w_out, out_bias,
         mlp_gain, mlp_shift, w_up, up_bias, w_down, down_bias, cotangent):
    copies, tok, width = layer_input.shape
    tokp = up16(tok)
    own = 2 * tokp
    rows = 2 * own
    ff = w_up.shape[1]
    nbits = nctx.bit_length() - 1
    vmem = pl.BlockSpec(memory_space=pltpu.VMEM)
    hbm = pl.BlockSpec(memory_space=pl.ANY)
    head_cols = -(-own // 128) * 128
    cols = 2 * head_cols
    pairs = HEADS // 2
    pw = width // 2
    grad_rows = 2 * ff + 4 * width
    sets = (ff, ff, 2 * width, width, width)
    halved = (True, True, False, False, False)
    landing = sum(landing_rows(r, nbits, seqs, h) for r, h in zip(sets, halved))
    peers = sum((1 << len(bits)) - 1 for bits in bit_groups(nbits, min(nbits, 3))) + seqs - 1
    ncopy = 8 + (2 * len(sets) + 1) * peers
    home = jax.ShapeDtypeStruct((copies, tokp, width), bf16)
    outr, backr, gat, small = pl.pallas_call(
        partial(layer_kernel, nbits, seqs),
        out_shape=(
            home, home,
            jax.ShapeDtypeStruct((grad_rows, width), bf16),
            jax.ShapeDtypeStruct((16, width), f32),
        ),
        in_specs=[hbm, vmem, hbm] + [vmem] * 13,
        out_specs=(hbm,) * 4,
        scratch_shapes=[
            pltpu.VMEM((grad_rows, width), bf16),
            pltpu.VMEM((16, width), f32),
            pltpu.VMEM(layer_input.shape, bf16),
            pltpu.VMEM((copies, tokp, width), bf16),
            pltpu.VMEM((4, tokp, width), bf16),
            pltpu.VMEM((copies, tokp, width), bf16),
            pltpu.VMEM((2, seqs, 16, -(-tokp // 128) * 128), bf16),
            pltpu.VMEM((rows, width), bf16),
            pltpu.VMEM((pairs, pw, cols), bf16),
            pltpu.VMEM((pairs, rows, width), bf16),
            pltpu.VMEM((pairs, rows, width), bf16),
            pltpu.VMEM((width, rows), bf16),
            pltpu.VMEM((pairs, pw + 16, rows), bf16),
            pltpu.VMEM((pairs, rows, cols), bf16),
            pltpu.VMEM((rows, TILE), f32),
            pltpu.VMEM((pairs, pw, cols), f32),
            pltpu.VMEM((pairs, 1, cols), f32),
            pltpu.VMEM((width, own), bf16),
            pltpu.VMEM((own, width), bf16),
            pltpu.VMEM((own, ff), bf16),
            pltpu.VMEM((own, ff), bf16),
            pltpu.VMEM((own, width), bf16),
            pltpu.VMEM((pairs, pw, cols), bf16),
            pltpu.VMEM((pairs, 16, cols), bf16),
            pltpu.VMEM((own, width), bf16),
            pltpu.VMEM((rows - grad_rows // 2, TILE), f32),
            pltpu.VMEM((grad_rows - ff, width), f32),
            pltpu.VMEM((landing, width), bf16),
            pltpu.VMEM((nbits + 1, 16, width), bf16),
            pltpu.VMEM((peers, 16, width), bf16),
            pltpu.SemaphoreType.DMA((10,)),
            pltpu.SemaphoreType.DMA((ncopy,)),
            pltpu.SemaphoreType.DMA((ncopy,)),
            pltpu.SemaphoreType.DMA((4,)),
            pltpu.SemaphoreType.DMA((4,)),
        ],
        compiler_params=pltpu.CompilerParams(collective_id=1, has_side_effects=True, vmem_limit_bytes=63 * 2**20),
        name="layer",
    )(layer_input, gene_kept, cotangent.reshape(copies * tok, width), attn_gain, attn_shift, w_query, w_key, w_value,
      w_out, out_bias, mlp_gain, mlp_shift, w_up, up_bias, w_down, down_bias)
    line = jax.ShapeDtypeStruct((1, width), f32)
    square = jax.ShapeDtypeStruct((width, width), f32)
    whole = [
        jax.ShapeDtypeStruct((copies, tok, width), bf16), jax.ShapeDtypeStruct((copies, tok, width), f32),
        square, square, square, square, jax.ShapeDtypeStruct((width, ff), f32), jax.ShapeDtypeStruct((ff, width), f32),
    ]
    rows_out = [line, line, line, line, line, jax.ShapeDtypeStruct((1, ff), f32), line]
    out, xg, wq, wk, wv, wo, wu, wd, ag, as_, ob, mg, ms, ub, db = pl.pallas_call(
        unpack_kernel,
        out_shape=tuple(whole + rows_out),
        in_specs=[hbm] * 5,
        out_specs=(hbm,) * 15,
        scratch_shapes=[pltpu.VMEM(v.shape, f32) for v in rows_out] + [
            pltpu.VMEM(cotangent.shape, f32), pltpu.VMEM(home.shape, bf16), pltpu.VMEM(home.shape, bf16),
            pltpu.VMEM((grad_rows, width), bf16), pltpu.VMEM((16, width), f32),
            pltpu.VMEM(layer_input.shape, bf16), pltpu.VMEM(cotangent.shape, f32), pltpu.VMEM((ff, width), f32),
            pltpu.VMEM((width, ff), f32), pltpu.VMEM((4, width, width), f32),
            pltpu.SemaphoreType.DMA((7,)), pltpu.SemaphoreType.DMA((15,)),
        ],
        compiler_params=pltpu.CompilerParams(vmem_limit_bytes=63 * 2**20),
        name="unpack",
    )(cotangent, outr, backr, gat, small)
    ag, as_, ob, mg, ms, ub, db = (v.reshape(-1) for v in (ag, as_, ob, mg, ms, ub, db))
    return out, xg, ag, as_, wq, wk, wv, wo, ob, mg, ms, wu, ub, wd, db


def solution(mesh):
    tokens = P("ctx", "seq", None)
    return jax.shard_map(
        partial(body, mesh.shape["ctx"], mesh.shape["seq"]),
        mesh=mesh,
        in_specs=(tokens, P("ctx", None)) + (P(),) * 13 + (tokens,),
        out_specs=(tokens, tokens) + (P(),) * 13,
        check_vma=False,
    )
```

```python
import math
from functools import partial

import jax
import jax.numpy as jnp
from jax import lax
from jax.experimental import pallas as pl
from jax.experimental.pallas import tpu as pltpu
from jax.sharding import PartitionSpec as P

bf16 = jnp.bfloat16
f32 = jnp.float32
HEADS = 4
CLS = 8
TILE = 256
MASKED = -8.0e9
NN = (((1,), (0,)), ((), ()))
NT = (((1,), (1,)), ((), ()))
TN = (((0,), (0,)), ((), ()))
TT = (((0,), (1,)), ((), ()))
MESH = pl.DeviceIdType.MESH


def mm(a, b, dims=NN):
    return lax.dot_general(a, b, dims, preferred_element_type=f32)


def norm_parts(z):
    average = jnp.mean(z, axis=-1, keepdims=True)
    centred = z - average
    spread = jnp.mean(centred * centred, axis=-1, keepdims=True)
    rstd = lax.rsqrt(spread + 1e-05)
    return centred * rstd, rstd


def norm_back(f, n, rstd):
    mean_f = jnp.mean(f, axis=-1, keepdims=True)
    mean_fn = jnp.mean(f * n, axis=-1, keepdims=True)
    return rstd * (f - mean_f - n * mean_fn)


def normal_parts(u):
    bell = jnp.exp2(u * u * (-0.5 * math.log2(math.e)))
    t = 1.0 / (1.0 + (0.3275911 / math.sqrt(2.0)) * jnp.abs(u))
    poly = 1.061405429 * t - 1.453152027
    poly = poly * t + 1.421413741
    poly = poly * t - 0.284496736
    poly = (poly * t + 0.254829592) * t
    tail = 0.5 * poly * bell
    return jnp.where(u < 0, tail, 1.0 - tail), bell * (1.0 / math.sqrt(2.0 * math.pi))


def colsum(z):
    return jnp.sum(z, axis=0, keepdims=True)


def row_vec(ref):
    return ref[...].astype(f32).reshape(1, -1)


def up16(n):
    return -(-n // 16) * 16


class Sems:
    def __init__(self, send, recv):
        self.send, self.recv, self.used = send, recv, 0

    def copy(self, src, dst, device):
        k = self.used
        self.used += 1
        return pltpu.make_async_remote_copy(
            src_ref=src, dst_ref=dst, send_sem=self.send.at[k], recv_sem=self.recv.at[k],
            device_id=device, device_id_type=MESH)


def bit_groups(nbits, first):
    return [tuple(range(first))] + [tuple(range(b, min(b + 2, nbits))) for b in range(first, nbits, 2)]


def spread(ctx, seq, nbits, seqs, first):
    stages = []
    for bits in bit_groups(nbits, first):
        place = [lax.rem(ctx // (1 << b), 2) for b in bits]
        others = []
        for r in range(1, 1 << len(bits)):
            device, index = ctx, 0
            for k, b in enumerate(bits):
                there = lax.rem(place[k] + (r >> k) % 2, 2)
                device = device + (there - place[k]) * (1 << b)
                index = index + there * (1 << k)
            others.append(((device, seq), index))
        mine = sum(p * (1 << k) for k, p in enumerate(place))
        stages.append((mine, others, list(range(len(others) + 1))))
    half = seqs // 2
    stages.append((
        seq, [((ctx, lax.rem(seq + d, seqs)), lax.rem(seq + d, seqs)) for d in range(1, seqs)],
        [n // 2 + n % 2 * half for n in range(seqs)]))
    return stages


def add_in_pairs(values, order):
    values = [values[n] for n in order]
    while len(values) > 1:
        values = [a + b for a, b in zip(values[::2], values[1::2])]
    return values[0]


def reduce_steps(sems, stages, rows, acc, acc0, send, recv, recv0, gat, gat_hbm, gat0, split_first, write):
    into = recv0
    path = []
    if split_first:
        size = rows // 2
        mine, others, _ = stages[0]
        off = mine * size
    else:
        size = rows
        off = 0
    base = off

    def held(at, count):
        return pl.ds(pl.multiple_of(acc0 + at - base, 16), count)

    if split_first:
        cp = sems.copy(send.at[pl.ds(0, size)], recv.at[pl.ds(into, size)], others[0][0])
        cp.start()
        yield
        cp.wait()
        acc[held(off, size), :] = acc[held(off, size), :] + recv[pl.ds(into, size), :].astype(f32)
        into += size
        path.append((others, off, size))
        stages = stages[1:]
    for mine, others, order in stages:
        ways = len(others) + 1
        split = size % (16 * ways) == 0
        piece = size // ways if split else size
        send[pl.ds(0, size), :] = acc[held(off, size), :].astype(bf16)
        cps = []
        for n, (device, index) in enumerate(others):
            start = pl.multiple_of(index * piece, 16) if split else 0
            cps.append(sems.copy(send.at[pl.ds(start, piece)], recv.at[pl.ds(into + n * piece, piece)], device))
        for cp in cps:
            cp.start()
        yield
        for cp in cps:
            cp.wait()
        got = [recv[pl.ds(into + n * piece, piece), :].astype(f32) for n in range(ways - 1)]
        into += (ways - 1) * piece
        if split:
            off = off + mine * piece
            size = piece
            acc[held(off, size), :] = acc[held(off, size), :] + sum(got[1:], got[0])
            path.append((others, off, size))
        else:
            acc[held(off, size), :] = add_in_pairs([send[pl.ds(0, size), :].astype(f32)] + got, order)
    gat[pl.ds(pl.multiple_of(gat0 + off, 16), size), :] = acc[held(off, size), :].astype(bf16)
    for k, (others, off, size) in reversed(list(enumerate(path))):
        at = pl.ds(pl.multiple_of(gat0 + off, 16), size)
        into = gat if k else gat_hbm
        cps = [sems.copy(gat.at[at], into.at[at], device) for device, _ in others]
        for cp in cps:
            cp.start()
        if k == 0:
            write(gat.at[at], gat_hbm.at[at])
        yield
        for cp in cps:
            cp.wait()


def landing_rows(rows, nbits, seqs, split_first):
    ways_of = [1 << len(bits) for bits in bit_groups(nbits, 1 if split_first else 3)] + [seqs]
    count = 0
    size = rows
    if split_first:
        size = count = rows // 2
        ways_of = ways_of[1:]
    for ways in ways_of:
        if size % (16 * ways) == 0:
            size //= ways
        count += (ways - 1) * size
    return count


def small_steps(sems, stages, small, send, recv, done):
    into = 0
    for k, (_, others, order) in enumerate(stages):
        send[k] = small[...].astype(bf16)
        cps = [sems.copy(send.at[k], recv.at[into + n], device) for n, (device, _) in enumerate(others)]
        for cp in cps:
            cp.start()
        yield
        for cp in cps:
            cp.wait()
        got = [recv[into + n].astype(f32) for n in range(len(others))]
        into += len(others)
        small[...] = add_in_pairs([send[k].astype(f32)] + got, order)
    done()


def layer_kernel(
    nbits, seqs,
    xin_hbm, kept_ref, cot_hbm,
    ag_ref, as_ref, wq_ref, wk_ref, wv_ref, wo_ref, ob_ref,
    mg_ref, ms_ref, wu_ref, ub_ref, wd_ref, db_ref,
    outr, backr, gat_hbm, small_hbm,
    gat, small_ref, xin, stage, xall, cotr, marks, n_ref, qaug, kaug, vaug, kt, vtaug, prob, s_ref, ot_ref, rl_ref,
    att_t, att, act_ref, gh_ref, gml_ref, gaug, dext, erecv, s_more, acc, recv, ssend, srecv,
    local_sems, send_sems, recv_sems, ret_send, ret_recv,
):
    copies, tok, width = xin_hbm.shape
    tokp = xall.shape[1]
    own = 2 * tokp
    rows = 2 * own
    ctx = lax.axis_index("ctx")
    seq = lax.axis_index("seq")
    cc = lax.rem(ctx, 2)
    group = ctx - cc
    sems = Sems(send_sems, recv_sems)
    hd = width // HEADS
    pairs = HEADS // 2
    pw = 2 * hd
    head_cols = qaug.shape[2] // 2
    cols = 2 * head_cols
    tiles = cols // TILE
    scale = 1.0 / math.sqrt(hd)
    expo = scale * math.log2(math.e)
    ff = wu_ref.shape[1]
    chunk = tokp
    nchunk = own // chunk
    sibling = (group + 1 - cc, seq)
    stay = seq // 2 == cc

    keep_in = pltpu.make_async_copy(xin_hbm, xin, local_sems.at[0])
    keep_in.start()
    cot_in = pltpu.make_async_copy(cot_hbm, s_ref.at[pl.ds(0, 2 * tok)], local_sems.at[1])
    cot_in.start()

    barrier = pltpu.get_barrier_semaphore()
    for dc in range(2):
        for d in range(seqs):
            if dc or d:
                pl.semaphore_signal(
                    barrier, inc=1, device_id=(group + lax.rem(cc + dc, 2), lax.rem(seq + d, seqs)), device_id_type=MESH)
    stages = spread(ctx, seq, nbits, seqs, 1)
    stages_flat = spread(ctx, seq, nbits, seqs, min(nbits, 3))
    met = [device for device, _ in stages_flat[0][1][1:]]
    met += [device for _, others, _ in stages_flat[1:-1] for device, _ in others]
    for device in met:
        pl.semaphore_signal(barrier, inc=1, device_id=device, device_id_type=MESH)
    greeted = 2 * seqs - 1 + len(met)

    lane = lax.broadcasted_iota(jnp.int32, (1, seqs * tok), 1)
    usable = jnp.where(jnp.logical_or(kept_ref[...] == 1, lane < CLS), 0.0, MASKED)
    usable = jnp.where(lax.rem(seq, 2) == 0, usable[0:1, :], usable[1:2, :])
    wide = marks.shape[3]
    sub = lax.broadcasted_iota(jnp.int32, (16, wide), 0)
    for sh in range(seqs):
        piece = jnp.concatenate(
            [usable[:, sh * tok:(sh + 1) * tok], jnp.full((1, wide - tok), MASKED, f32)], axis=1)
        marks[0, sh] = jnp.where(sub == 0, piece, 0.0).astype(bf16)
    stage[:, tokp - 16:tokp, :] = jnp.zeros((copies, 16, width), bf16)
    keep_in.wait()
    stage[:, 0:tok, :] = xin[...]

    def out_copy(k, dst):
        b = lax.rem(seq + k, 2)
        return sems.copy(stage.at[b], dst.at[k], (group + seq // 2, 2 * cc + b))

    def scatter(dst):
        moves = [out_copy(0, dst), out_copy(1, dst)]
        moves[1].start()

        @pl.when(jnp.logical_not(stay))
        def _():
            moves[0].start()

        @pl.when(stay)
        def _():
            dst[0] = stage[lax.rem(seq, 2)]

        return moves

    def arrived(moves, k):
        if k:
            moves[k].wait_recv()
        else:
            @pl.when(jnp.logical_not(stay))
            def _():
                moves[0].wait_recv()

    def left(moves):
        moves[1].wait_send()

        @pl.when(jnp.logical_not(stay))
        def _():
            moves[0].wait_send()

    qaug[...] = jnp.zeros_like(qaug)
    gaug[...] = jnp.zeros_like(gaug)
    dext[...] = jnp.zeros_like(dext)
    lane = lax.broadcasted_iota(jnp.int32, (rows, pw), 1)
    sub = lax.broadcasted_iota(jnp.int32, (16, rows), 0)
    for p in range(pairs):
        vaug[p, :, pw:2 * pw] = jnp.where(lane < 2, 1.0, 0.0).astype(bf16)
        vtaug[p, pw:pw + 16, :] = jnp.where(sub == 0, 1.0, 0.0).astype(bf16)
    pl.semaphore_wait(barrier, greeted)
    moves = scatter(xall)
    marks_copy = sems.copy(marks.at[0], marks.at[1], sibling)
    marks_copy.start()

    gain = row_vec(ag_ref)
    shift = row_vec(as_ref)

    def project(pos):
        at = slice(pos * tokp, (pos + 1) * tokp)
        n, _ = norm_parts(xall[pos].astype(f32))
        low = (n * gain + shift).astype(bf16)
        n_ref[at, :] = low
        k = mm(low, wk_ref[...]).astype(bf16)
        v = mm(low, wv_ref[...]).astype(bf16)
        for p in range(pairs):
            kaug[p, at, 0:pw] = k[:, p * pw:(p + 1) * pw]
            vaug[p, at, 0:pw] = v[:, p * pw:(p + 1) * pw]

    forwards = []
    for k in range(2):
        arrived(moves, k)
        forwards.append(sems.copy(xall.at[k], xall.at[2 + k], sibling))
        forwards[k].start()
    for k in range(2):
        project(k)
    left(moves)
    cot_in.wait()
    for b in range(2):
        stage[b, 0:tok, :] = s_ref[b * tok:(b + 1) * tok, :].astype(bf16)
    cot_moves = scatter(cotr)
    marks_copy.wait()
    held = jnp.where(stay, 0, 1)
    unit = jnp.where(
        lax.broadcasted_iota(jnp.int32, (16, pw), 0) == lax.broadcasted_iota(jnp.int32, (16, pw), 1), 1.0, 0.0
    ).astype(bf16)
    for pos in range(4):
        side = cc if pos < 2 else 1 - cc
        mark = marks[held, 2 * side + lax.rem(seq + pos, 2)]
        bias = mm(mark, unit, TN).astype(bf16)[0:tokp, :]
        for p in range(pairs):
            kaug[p, pos * tokp:(pos + 1) * tokp, pw:2 * pw] = bias
    qt = mm(wq_ref[...], n_ref[0:own, :], TT).astype(bf16)
    for p in range(pairs):
        for h in range(2):
            qaug[p, h * hd:(h + 1) * hd, h * head_cols:h * head_cols + own] = qt[p * pw + h * hd:p * pw + (h + 1) * hd, :]
    for k in range(2):
        forwards[k].wait()
        project(2 + k)
    kt[...] = mm(wk_ref[...], n_ref[...], TT).astype(bf16)
    vt = mm(wv_ref[...], n_ref[...], TT).astype(bf16)
    for p in range(pairs):
        vtaug[p, 0:pw, :] = vt[p * pw:(p + 1) * pw, :]

    first = jnp.where(lax.broadcasted_iota(jnp.int32, (pw, TILE), 0) == 0, 1.0, 0.0).astype(bf16)

    cut = (rows - s_more.shape[0]) // 2
    bounds = ((0, cut), (cut, 2 * cut), (2 * cut, rows))
    even = [s_ref.at[a:b] for a, b in bounds]
    odd = [acc.at[0:cut], acc.at[cut:2 * cut], s_more]
    count = pairs * tiles

    def place(t):
        return t // tiles, pl.ds(pl.multiple_of((t % tiles) * TILE, TILE), TILE)

    def score(t, into, c):
        p, at = place(t)
        a, b = bounds[c]
        value = mm(kaug[p, a:b, :], jnp.concatenate([qaug[p, :, at], first], axis=0))
        into[c][...] = value
        return jnp.max(value.reshape((b - a) // 8, 8, TILE), axis=0)

    def weigh(t, scores, top, ahead):
        p, at = place(t)
        top = jnp.max(top, axis=0, keepdims=True)
        tops = []
        total = None
        for c, (a, b) in enumerate(bounds):
            if ahead is not None:
                tops.append(score(lax.rem(t + 1, count), ahead, c))
            weights = jnp.exp2((scores[c][...] - top) * expo).astype(bf16)
            prob[p, a:b, at] = weights
            part = mm(vtaug[p, :, a:b], weights)
            total = part if total is None else total + part
        rl = 1.0 / total[pw:pw + 1]
        ot_ref[p, :, at] = total[0:pw] * rl
        rl_ref[p, :, at] = rl
        return jnp.maximum(jnp.maximum(tops[0], tops[1]), tops[2])

    def forward(i, top):
        return weigh(2 * i + 1, odd, weigh(2 * i, even, top, odd), even)

    tops = [score(0, even, c) for c in range(3)]
    lax.fori_loop(0, count // 2, forward, jnp.maximum(jnp.maximum(tops[0], tops[1]), tops[2]))
    for p in range(pairs):
        for h in range(2):
            att_t[p * pw + h * hd:p * pw + (h + 1) * hd, :] = ot_ref[
                p, h * hd:(h + 1) * hd, h * head_cols:h * head_cols + own
            ].astype(bf16)
    att[...] = jnp.transpose(att_t[...])

    gain2 = row_vec(mg_ref)
    shift2 = row_vec(ms_ref)
    out_bias = row_vec(ob_ref)
    up_bias = row_vec(ub_ref)
    down_bias = row_vec(db_ref)
    arrived(cot_moves, 0)
    arrived(cot_moves, 1)
    left(cot_moves)

    def mlp(i, carry):
        g_up, g_down, g_out, g_gain, g_shift = carry
        at = pl.ds(pl.multiple_of(i * chunk, 16), chunk)
        middle = xall[i].astype(f32) + (mm(att[at, :], wo_ref[...]) + out_bias)
        n, rstd = norm_parts(middle)
        low = (n * gain2 + shift2).astype(bf16)
        att[at, :] = low
        hidden = mm(low, wu_ref[...]) + up_bias
        dist, dens = normal_parts(hidden)
        act = (hidden * dist).astype(bf16)
        act_ref[at, :] = act
        stage[i] = (middle + (mm(act, wd_ref[...]) + down_bias)).astype(bf16)
        cot = cotr[i]
        gh = ((dist + hidden * dens) * mm(cot, wd_ref[...], NT)).astype(bf16)
        gh_ref[at, :] = gh
        e = mm(gh, wu_ref[...], NT)
        back = norm_back(e * gain2, n, rstd)
        s_ref[at, :] = back
        cot = cot.astype(f32)
        gml = (cot + back).astype(bf16)
        gml_ref[at, :] = gml
        return (
            g_up + colsum(gh.astype(f32)), g_down + colsum(cot), g_out + colsum(gml.astype(f32)),
            g_gain + colsum(e * n), g_shift + colsum(e),
        )

    zero = jnp.zeros((1, width), f32)
    sums = lax.fori_loop(0, nchunk, mlp, (jnp.zeros((1, ff), f32), zero, zero, zero, zero))
    small_ref[0:1, :] = sums[1]
    small_ref[1:2, :] = sums[2]
    small_ref[2:3, :] = sums[3]
    small_ref[3:4, :] = sums[4]
    ups = 4 + ff // width
    for j in range(ff // width):
        small_ref[4 + j:5 + j, :] = sums[0][:, j * width:(j + 1) * width]

    cut_at = up16(chunk // 2)
    spans = ((0, cut_at), (cut_at, chunk - cut_at))

    def back_copy(k, dst, sem, part):
        b = lax.rem(seq, 2)
        at = pl.ds(*spans[part])
        return pltpu.make_async_remote_copy(
            src_ref=stage.at[k, at], dst_ref=dst.at[b, at],
            send_sem=ret_send.at[4 * sem + 2 * part + k], recv_sem=ret_recv.at[4 * sem + 2 * part + b],
            device_id=(group + seq // 2, 2 * cc + lax.rem(seq + k, 2)), device_id_type=MESH)

    def own_copy(dst, sem):
        return pltpu.make_async_copy(stage.at[0], dst.at[lax.rem(seq, 2)], local_sems.at[2 + sem])

    def send_block(moves, k, dst, sem, parts=(0, 1)):
        if k:
            for part in parts:
                moves[k][part].start()
            return

        @pl.when(jnp.logical_not(stay))
        def _():
            for part in parts:
                moves[k][part].start()

        @pl.when(stay)
        def _():
            own_copy(dst, sem).start()

    def left_home(moves, dst, sem):
        for move in moves[1]:
            move.wait_send()

        @pl.when(jnp.logical_not(stay))
        def _():
            for move in moves[0]:
                move.wait_send()

        @pl.when(stay)
        def _():
            own_copy(dst, sem).wait()

    def home_again(dst, sem):
        for b in range(2):
            here = jnp.logical_and(stay, lax.rem(seq, 2) == b)

            @pl.when(jnp.logical_not(here))
            def _():
                for part in range(2):
                    at = pl.ds(*spans[part])
                    pltpu.make_async_remote_copy(
                        src_ref=stage.at[b, at], dst_ref=dst.at[b, at], send_sem=ret_send.at[4 * sem + 2 * part + b],
                        recv_sem=ret_recv.at[4 * sem + 2 * part + b], device_id=sibling, device_id_type=MESH).wait_recv()

    out_moves = [[back_copy(k, outr, 0, part) for part in range(2)] for k in range(2)]
    for k in range(2):
        send_block(out_moves, k, outr, 0)

    sets = (ff, ff, 2 * width, width, width)
    halved = (True, True, False, False, False)
    starts = [sum(sets[:j]) for j in range(5)]
    lands = [landing_rows(sets[j], nbits, seqs, halved[j]) for j in range(5)]
    lands = [sum(lands[:j]) for j in range(5)]
    kept = [sets[j] // 2 if halved[j] else sets[j] for j in range(5)]
    kept = [sum(kept[:j]) for j in range(5)]
    sends = (
        act_ref.at[:, 2 * width:3 * width], act_ref.at[:, 3 * width:4 * width],
        gh_ref.at[:, 2 * width:3 * width], gh_ref.at[0:own // 2, 3 * width:4 * width], gh_ref.at[own // 2:own, 3 * width:4 * width])
    written = []

    def write_out(j, src, dst):
        copy = pltpu.make_async_copy(src, dst, local_sems.at[4 + j])
        copy.start()
        written.append(copy)

    def write_small():
        copy = pltpu.make_async_copy(small_ref, small_hbm, local_sems.at[9])
        copy.start()
        written.append(copy)

    steps = [
        reduce_steps(
            sems, stages if halved[j] else stages_flat, sets[j], acc, kept[j], sends[j], recv, lands[j], gat, gat_hbm, starts[j],
            halved[j], partial(write_out, j))
        for j in range(5)
    ]

    def turn(*which):
        for j in which:
            next(steps[j], None)

    def split(j, make, half):
        acc[kept[j]:kept[j] + half, :] = make(cc)
        sends[j][0:half, :] = make(1 - cc).astype(bf16)

    def part(w, count):
        return pl.ds(pl.multiple_of(w * count, 128), count)

    def up_half(w):
        value = mm(att[...], gh_ref[:, part(w, ff // 2)], TN)
        return jnp.concatenate([value[:, j * width:(j + 1) * width] for j in range(ff // width // 2)], axis=0)

    split(0, lambda w: mm(act_ref[:, part(w, ff // 2)], cotr[...].reshape(own, width), TN), ff // 2)
    turn(0)
    split(1, up_half, ff // 2)
    turn(1)
    acc[kept[2]:kept[2] + width, :] = mm(att_t[...], gml_ref[...])

    sub = lax.broadcasted_iota(jnp.int32, (16, own), 0)
    for p in range(pairs):
        for h in range(2):
            lanes = slice(h * head_cols, h * head_cols + own)
            g = mm(wo_ref[p * pw + h * hd:p * pw + (h + 1) * hd, :], gml_ref[...], NT).astype(bf16).astype(f32)
            g = (g * rl_ref[p, :, lanes]).astype(bf16)
            gaug[p, h * hd:(h + 1) * hd, lanes] = g
            delta = -colsum(g.astype(f32) * ot_ref[p, h * hd:(h + 1) * hd, lanes])
            coarse = delta.astype(bf16).astype(f32)
            dext[p, :, lanes] = jnp.where(sub == 0, coarse, jnp.where(sub == 1, delta - coarse, 0.0)).astype(bf16)

    turn(0, 1)
    for p in range(pairs):
        for half in range(2):
            lanes = slice(half * width + p * pw, half * width + (p + 1) * pw)
            act_ref[:, lanes] = mm(prob[p, half * own:(half + 1) * own, :], gaug[p], NT).astype(bf16)
    dv_own, dv_sib = act_ref.at[:, 0:width], act_ref.at[:, width:2 * width]
    dk_own, dk_sib = gh_ref.at[:, 0:width], gh_ref.at[:, width:2 * width]
    acc[kept[2] + width:kept[2] + 2 * width, :] = mm(n_ref[0:own, :], dv_own[...], TN) + mm(n_ref[own:rows, :], dv_sib[...], TN)
    turn(2)
    nothing = jnp.zeros((pw - 16, cols), bf16)

    def backward(p, c):
        a, b = bounds[c]
        right = jnp.concatenate([gaug[p], dext[p], nothing], axis=0)
        ds = prob[p, a:b, :] * mm(vaug[p, a:b, :], right).astype(bf16)
        prob[p, a:b, :] = ds
        part = mm(kt[p * pw:(p + 1) * pw, a:b], ds) * scale
        ot_ref[p] = ot_ref[p] + part if c else part

    backward(0, 0)
    turn(0, 1)
    backward(0, 1)
    backward(0, 2)
    backward(1, 0)
    turn(2)
    backward(1, 1)
    turn(0, 1)
    backward(1, 2)
    for p in range(pairs):
        for h in range(2):
            att_t[p * pw + h * hd:p * pw + (h + 1) * hd, :] = ot_ref[
                p, h * hd:(h + 1) * hd, h * head_cols:h * head_cols + own
            ].astype(bf16)
    att[...] = jnp.transpose(att_t[...])
    acc[kept[3]:kept[3] + width, :] = mm(n_ref[0:own, :], att[...], TN)
    turn(2, 3)
    left_home(out_moves, outr, 0)

    def key_grads(pos):
        half, k = pos // 2, pos % 2
        for p in range(pairs):
            lanes = slice(half * width + p * pw, half * width + (p + 1) * pw)
            gh_ref[k * chunk:(k + 1) * chunk, lanes] = (
                mm(prob[p, pos * chunk:(pos + 1) * chunk, :], qaug[p], NT) * scale).astype(bf16)

    def key_weight(k):
        at = slice(k * chunk, (k + 1) * chunk)
        beyond = slice(own + k * chunk, own + (k + 1) * chunk)
        return mm(n_ref[at, :], dk_own[at, :], TN) + mm(n_ref[beyond, :], dk_sib[at, :], TN)

    e_copies = []
    back_moves = [[back_copy(k, backr, 1, part) for part in range(2)] for k in range(2)]
    sums = (zero, zero)
    for k in range(2):
        at = slice(k * chunk, (k + 1) * chunk)
        key_grads(2 + k)
        gml_ref[at, :] = (mm(dk_sib[at, :], wk_ref[...], NT) + mm(dv_sib[at, :], wv_ref[...], NT)).astype(bf16)
        e_copies.append(sems.copy(gml_ref.at[at], erecv.at[at], sibling))
        e_copies[k].start()
        key_grads(k)
        if k == 0:
            acc[kept[4]:kept[4] + width, :] = key_weight(k)
            turn(0, 1, 2, 3)
        else:
            acc[kept[4]:kept[4] + width, :] += key_weight(k)
            turn(4, 3)
        e = mm(att[at, :], wq_ref[...], NT) + mm(dk_own[at, :], wk_ref[...], NT) + mm(dv_own[at, :], wv_ref[...], NT)
        n, rstd = norm_parts(xall[k].astype(f32))
        e_copies[k].wait()
        e = e + erecv[at, :].astype(f32)
        stage[k] = (s_ref[at, :] + norm_back(e * gain, n, rstd)).astype(bf16)
        sums = (sums[0] + colsum(e * n), sums[1] + colsum(e))
        send_block(back_moves, k, backr, 1, (0,) if k else (0, 1))
    small_ref[ups:ups + 1, :] = sums[0]
    small_ref[ups + 1:ups + 2, :] = sums[1]
    small_ref[ups + 2:, :] = jnp.zeros((small_ref.shape[0] - ups - 2, width), f32)
    steps.append(small_steps(sems, stages_flat, small_ref, ssend, srecv, write_small))
    turn(5)
    turn(4)
    send_block(back_moves, 1, backr, 1, (1,))
    turn(0, 1, 2, 5, 3)
    turn(4, 0, 1, 5)
    turn(4)
    for _ in range(len(stages) * 2):
        turn(5, 4, 0, 1, 2, 3)
    left_home(back_moves, backr, 1)
    home_again(outr, 0)
    home_again(backr, 1)
    for copy in written:
        copy.wait()


def unpack_kernel(cot_hbm, outr_hbm, backr_hbm, gat_hbm, small_hbm, *refs):
    hbm, vec_hbm, vec = refs[:8], refs[8:15], refs[15:22]
    cot_ref, outr, backr, gat, small, out, xg, wide, up, sq, in_sems, out_sems = refs[22:]
    out_hbm, xg_hbm, wq_hbm, wk_hbm, wv_hbm, wo_hbm, wu_hbm, wd_hbm = hbm
    ag, as_, ob, mg, ms, ub, db = vec
    _, tok, width = cot_ref.shape
    ff = wide.shape[0]
    cuts = ((0, ff), (ff, 2 * ff), (2 * ff, 2 * ff + 4 * width))
    ins = [
        pltpu.make_async_copy(src, dst, in_sems.at[k])
        for k, (src, dst) in enumerate(
            [(gat_hbm.at[a:b], gat.at[a:b]) for a, b in cuts]
            + [(outr_hbm, outr), (backr_hbm, backr), (cot_hbm, cot_ref), (small_hbm, small)])
    ]
    for cp in ins:
        cp.start()
    outs = []

    def put(src, dst):
        cp = pltpu.make_async_copy(src, dst, out_sems.at[len(outs)])
        cp.start()
        outs.append(cp)

    ins[0].wait()
    wide[...] = gat[0:ff, :].astype(f32)
    put(wide, wd_hbm)
    ins[1].wait()
    for j in range(ff // width):
        up[:, j * width:(j + 1) * width] = gat[ff + j * width:ff + (j + 1) * width, :].astype(f32)
    put(up, wu_hbm)
    ins[4].wait()
    ins[5].wait()
    xg[...] = cot_ref[...] + backr[:, 0:tok, :].astype(f32)
    put(xg, xg_hbm)
    ins[2].wait()
    for j, dst in enumerate((wo_hbm, wv_hbm, wq_hbm, wk_hbm)):
        at = 2 * ff + j * width
        sq[j] = gat[at:at + width, :].astype(f32)
        put(sq.at[j], dst)
    ins[3].wait()
    out[...] = outr[:, 0:tok, :]
    put(out, out_hbm)
    ins[6].wait()
    for j in range(ff // width):
        ub[0:1, j * width:(j + 1) * width] = small[4 + j:5 + j, :]
    ups = 4 + ff // width
    for j, ref in ((0, db), (1, ob), (2, mg), (3, ms), (ups, ag), (ups + 1, as_)):
        ref[...] = small[j:j + 1, :]
    for src, dst in zip(vec, vec_hbm):
        put(src, dst)
    for cp in outs:
        cp.wait()


def body(nctx, seqs, layer_input, gene_kept, attn_gain, attn_shift, w_query, w_key, w_value, w_out, out_bias,
         mlp_gain, mlp_shift, w_up, up_bias, w_down, down_bias, cotangent):
    copies, tok, width = layer_input.shape
    tokp = up16(tok)
    own = 2 * tokp
    rows = 2 * own
    ff = w_up.shape[1]
    nbits = nctx.bit_length() - 1
    vmem = pl.BlockSpec(memory_space=pltpu.VMEM)
    hbm = pl.BlockSpec(memory_space=pl.ANY)
    head_cols = -(-own // 128) * 128
    cols = 2 * head_cols
    pairs = HEADS // 2
    pw = width // 2
    grad_rows = 2 * ff + 4 * width
    sets = (ff, ff, 2 * width, width, width)
    halved = (True, True, False, False, False)
    landing = sum(landing_rows(r, nbits, seqs, h) for r, h in zip(sets, halved))
    peers = sum((1 << len(bits)) - 1 for bits in bit_groups(nbits, min(nbits, 3))) + seqs - 1
    ncopy = 8 + (2 * len(sets) + 1) * peers
    home = jax.ShapeDtypeStruct((copies, tokp, width), bf16)
    outr, backr, gat, small = pl.pallas_call(
        partial(layer_kernel, nbits, seqs),
        out_shape=(
            home, home,
            jax.ShapeDtypeStruct((grad_rows, width), bf16),
            jax.ShapeDtypeStruct((16, width), f32),
        ),
        in_specs=[hbm, vmem, hbm] + [vmem] * 13,
        out_specs=(hbm,) * 4,
        scratch_shapes=[
            pltpu.VMEM((grad_rows, width), bf16),
            pltpu.VMEM((16, width), f32),
            pltpu.VMEM(layer_input.shape, bf16),
            pltpu.VMEM((copies, tokp, width), bf16),
            pltpu.VMEM((4, tokp, width), bf16),
            pltpu.VMEM((copies, tokp, width), bf16),
            pltpu.VMEM((2, seqs, 16, -(-tokp // 128) * 128), bf16),
            pltpu.VMEM((rows, width), bf16),
            pltpu.VMEM((pairs, pw, cols), bf16),
            pltpu.VMEM((pairs, rows, width), bf16),
            pltpu.VMEM((pairs, rows, width), bf16),
            pltpu.VMEM((width, rows), bf16),
            pltpu.VMEM((pairs, pw + 16, rows), bf16),
            pltpu.VMEM((pairs, rows, cols), bf16),
            pltpu.VMEM((rows, TILE), f32),
            pltpu.VMEM((pairs, pw, cols), f32),
            pltpu.VMEM((pairs, 1, cols), f32),
            pltpu.VMEM((width, own), bf16),
            pltpu.VMEM((own, width), bf16),
            pltpu.VMEM((own, ff), bf16),
            pltpu.VMEM((own, ff), bf16),
            pltpu.VMEM((own, width), bf16),
            pltpu.VMEM((pairs, pw, cols), bf16),
            pltpu.VMEM((pairs, 16, cols), bf16),
            pltpu.VMEM((own, width), bf16),
            pltpu.VMEM((rows - grad_rows // 2, TILE), f32),
            pltpu.VMEM((grad_rows - ff, width), f32),
            pltpu.VMEM((landing, width), bf16),
            pltpu.VMEM((nbits + 1, 16, width), bf16),
            pltpu.VMEM((peers, 16, width), bf16),
            pltpu.SemaphoreType.DMA((10,)),
            pltpu.SemaphoreType.DMA((ncopy,)),
            pltpu.SemaphoreType.DMA((ncopy,)),
            pltpu.SemaphoreType.DMA((8,)),
            pltpu.SemaphoreType.DMA((8,)),
        ],
        compiler_params=pltpu.CompilerParams(collective_id=1, has_side_effects=True, vmem_limit_bytes=63 * 2**20),
        name="layer",
    )(layer_input, gene_kept, cotangent.reshape(copies * tok, width), attn_gain, attn_shift, w_query, w_key, w_value,
      w_out, out_bias, mlp_gain, mlp_shift, w_up, up_bias, w_down, down_bias)
    line = jax.ShapeDtypeStruct((1, width), f32)
    square = jax.ShapeDtypeStruct((width, width), f32)
    whole = [
        jax.ShapeDtypeStruct((copies, tok, width), bf16), jax.ShapeDtypeStruct((copies, tok, width), f32),
        square, square, square, square, jax.ShapeDtypeStruct((width, ff), f32), jax.ShapeDtypeStruct((ff, width), f32),
    ]
    rows_out = [line, line, line, line, line, jax.ShapeDtypeStruct((1, ff), f32), line]
    out, xg, wq, wk, wv, wo, wu, wd, ag, as_, ob, mg, ms, ub, db = pl.pallas_call(
        unpack_kernel,
        out_shape=tuple(whole + rows_out),
        in_specs=[hbm] * 5,
        out_specs=(hbm,) * 15,
        scratch_shapes=[pltpu.VMEM(v.shape, f32) for v in rows_out] + [
            pltpu.VMEM(cotangent.shape, f32), pltpu.VMEM(home.shape, bf16), pltpu.VMEM(home.shape, bf16),
            pltpu.VMEM((grad_rows, width), bf16), pltpu.VMEM((16, width), f32),
            pltpu.VMEM(layer_input.shape, bf16), pltpu.VMEM(cotangent.shape, f32), pltpu.VMEM((ff, width), f32),
            pltpu.VMEM((width, ff), f32), pltpu.VMEM((4, width, width), f32),
            pltpu.SemaphoreType.DMA((7,)), pltpu.SemaphoreType.DMA((15,)),
        ],
        compiler_params=pltpu.CompilerParams(vmem_limit_bytes=63 * 2**20),
        name="unpack",
    )(cotangent, outr, backr, gat, small)
    ag, as_, ob, mg, ms, ub, db = (v.reshape(-1) for v in (ag, as_, ob, mg, ms, ub, db))
    return out, xg, ag, as_, wq, wk, wv, wo, ob, mg, ms, wu, ub, wd, db


def solution(mesh):
    tokens = P("ctx", "seq", None)
    return jax.shard_map(
        partial(body, mesh.shape["ctx"], mesh.shape["seq"]),
        mesh=mesh,
        in_specs=(tokens, P("ctx", None)) + (P(),) * 13 + (tokens,),
        out_specs=(tokens, tokens) + (P(),) * 13,
        check_vma=False,
    )
```

```python
import math
from functools import partial

import jax
import jax.numpy as jnp
from jax import lax
from jax.experimental import pallas as pl
from jax.experimental.pallas import tpu as pltpu
from jax.sharding import PartitionSpec as P

bf16 = jnp.bfloat16
f32 = jnp.float32
HEADS = 4
CLS = 8
TILE = 256
MASKED = -8.0e9
NN = (((1,), (0,)), ((), ()))
NT = (((1,), (1,)), ((), ()))
TN = (((0,), (0,)), ((), ()))
TT = (((0,), (1,)), ((), ()))
MESH = pl.DeviceIdType.MESH


def mm(a, b, dims=NN):
    return lax.dot_general(a, b, dims, preferred_element_type=f32)


def norm_parts(z):
    average = jnp.mean(z, axis=-1, keepdims=True)
    centred = z - average
    spread = jnp.mean(centred * centred, axis=-1, keepdims=True)
    rstd = lax.rsqrt(spread + 1e-05)
    return centred * rstd, rstd


def norm_back(f, n, rstd):
    mean_f = jnp.mean(f, axis=-1, keepdims=True)
    mean_fn = jnp.mean(f * n, axis=-1, keepdims=True)
    return rstd * (f - mean_f - n * mean_fn)


def normal_parts(u):
    bell = jnp.exp2(u * u * (-0.5 * math.log2(math.e)))
    t = 1.0 / (1.0 + (0.3275911 / math.sqrt(2.0)) * jnp.abs(u))
    poly = 1.061405429 * t - 1.453152027
    poly = poly * t + 1.421413741
    poly = poly * t - 0.284496736
    poly = (poly * t + 0.254829592) * t
    tail = 0.5 * poly * bell
    return jnp.where(u < 0, tail, 1.0 - tail), bell * (1.0 / math.sqrt(2.0 * math.pi))


def colsum(z):
    return jnp.sum(z, axis=0, keepdims=True)


def row_vec(ref):
    return ref[...].astype(f32).reshape(1, -1)


def up16(n):
    return -(-n // 16) * 16


class Sems:
    def __init__(self, send, recv):
        self.send, self.recv, self.used = send, recv, 0

    def copy(self, src, dst, device):
        k = self.used
        self.used += 1
        return pltpu.make_async_remote_copy(
            src_ref=src, dst_ref=dst, send_sem=self.send.at[k], recv_sem=self.recv.at[k],
            device_id=device, device_id_type=MESH)


def bit_groups(nbits, first):
    return [tuple(range(first))] + [tuple(range(b, min(b + 2, nbits))) for b in range(first, nbits, 2)]


def spread(ctx, seq, nbits, seqs, first):
    stages = []
    for bits in bit_groups(nbits, first):
        place = [lax.rem(ctx // (1 << b), 2) for b in bits]
        others = []
        for r in range(1, 1 << len(bits)):
            device, index = ctx, 0
            for k, b in enumerate(bits):
                there = lax.rem(place[k] + (r >> k) % 2, 2)
                device = device + (there - place[k]) * (1 << b)
                index = index + there * (1 << k)
            others.append(((device, seq), index))
        mine = sum(p * (1 << k) for k, p in enumerate(place))
        stages.append((mine, others, list(range(len(others) + 1))))
    half = seqs // 2
    stages.append((
        seq, [((ctx, lax.rem(seq + d, seqs)), lax.rem(seq + d, seqs)) for d in range(1, seqs)],
        [n // 2 + n % 2 * half for n in range(seqs)]))
    return stages


def add_in_pairs(values, order):
    values = [values[n] for n in order]
    while len(values) > 1:
        values = [a + b for a, b in zip(values[::2], values[1::2])]
    return values[0]


def reduce_steps(sems, stages, rows, acc, acc0, send, recv, recv0, gat, gat_hbm, gat0, split_first, write):
    into = recv0
    path = []
    if split_first:
        size = rows // 2
        mine, others, _ = stages[0]
        off = mine * size
    else:
        size = rows
        off = 0
    base = off

    def held(at, count):
        return pl.ds(pl.multiple_of(acc0 + at - base, 16), count)

    if split_first:
        cp = sems.copy(send.at[pl.ds(0, size)], recv.at[pl.ds(into, size)], others[0][0])
        cp.start()
        yield
        cp.wait()
        acc[held(off, size), :] = acc[held(off, size), :] + recv[pl.ds(into, size), :].astype(f32)
        into += size
        path.append((others, off, size))
        stages = stages[1:]
    for mine, others, order in stages:
        ways = len(others) + 1
        split = size % (16 * ways) == 0
        piece = size // ways if split else size
        send[pl.ds(0, size), :] = acc[held(off, size), :].astype(bf16)
        cps = []
        for n, (device, index) in enumerate(others):
            start = pl.multiple_of(index * piece, 16) if split else 0
            cps.append(sems.copy(send.at[pl.ds(start, piece)], recv.at[pl.ds(into + n * piece, piece)], device))
        for cp in cps:
            cp.start()
        yield
        for cp in cps:
            cp.wait()
        got = [recv[pl.ds(into + n * piece, piece), :].astype(f32) for n in range(ways - 1)]
        into += (ways - 1) * piece
        if split:
            off = off + mine * piece
            size = piece
            acc[held(off, size), :] = acc[held(off, size), :] + sum(got[1:], got[0])
            path.append((others, off, size))
        else:
            acc[held(off, size), :] = add_in_pairs([send[pl.ds(0, size), :].astype(f32)] + got, order)
    gat[pl.ds(pl.multiple_of(gat0 + off, 16), size), :] = acc[held(off, size), :].astype(bf16)
    for k, (others, off, size) in reversed(list(enumerate(path))):
        at = pl.ds(pl.multiple_of(gat0 + off, 16), size)
        into = gat if k else gat_hbm
        cps = [sems.copy(gat.at[at], into.at[at], device) for device, _ in others]
        for cp in cps:
            cp.start()
        if k == 0:
            write(gat.at[at], gat_hbm.at[at])
        yield
        for cp in cps:
            cp.wait()


def landing_rows(rows, nbits, seqs, split_first):
    ways_of = [1 << len(bits) for bits in bit_groups(nbits, 1 if split_first else 3)] + [seqs]
    count = 0
    size = rows
    if split_first:
        size = count = rows // 2
        ways_of = ways_of[1:]
    for ways in ways_of:
        if size % (16 * ways) == 0:
            size //= ways
        count += (ways - 1) * size
    return count


def small_steps(sems, stages, small, send, recv, done):
    into = 0
    for k, (_, others, order) in enumerate(stages):
        send[k] = small[...].astype(bf16)
        cps = [sems.copy(send.at[k], recv.at[into + n], device) for n, (device, _) in enumerate(others)]
        for cp in cps:
            cp.start()
        yield
        for cp in cps:
            cp.wait()
        got = [recv[into + n].astype(f32) for n in range(len(others))]
        into += len(others)
        small[...] = add_in_pairs([send[k].astype(f32)] + got, order)
    done()


def layer_kernel(
    nbits, seqs,
    xin, kept_ref, cot_hbm,
    ag_ref, as_ref, wq_ref, wk_ref, wv_ref, wo_ref, ob_ref,
    mg_ref, ms_ref, wu_ref, ub_ref, wd_ref, db_ref,
    outr, backr, gat_hbm, small_hbm,
    gat, small_ref, stage, xall, cotr, marks, n_ref, qaug, kaug, vaug, kt, vtaug, prob, s_ref, ot_ref, rl_ref,
    att_t, att, act_ref, gh_ref, gml_ref, gaug, dext, erecv, s_more, acc, recv, ssend, srecv,
    local_sems, send_sems, recv_sems, ret_send, ret_recv,
):
    copies, tok, width = xin.shape
    tokp = xall.shape[1]
    own = 2 * tokp
    rows = 2 * own
    ctx = lax.axis_index("ctx")
    seq = lax.axis_index("seq")
    cc = lax.rem(ctx, 2)
    group = ctx - cc
    sems = Sems(send_sems, recv_sems)
    hd = width // HEADS
    pairs = HEADS // 2
    pw = 2 * hd
    head_cols = qaug.shape[2] // 2
    cols = 2 * head_cols
    tiles = cols // TILE
    scale = 1.0 / math.sqrt(hd)
    expo = scale * math.log2(math.e)
    ff = wu_ref.shape[1]
    chunk = tokp
    nchunk = own // chunk
    sibling = (group + 1 - cc, seq)
    stay = seq // 2 == cc

    cot_in = pltpu.make_async_copy(cot_hbm, s_ref.at[pl.ds(0, 2 * tok)], local_sems.at[1])
    cot_in.start()

    barrier = pltpu.get_barrier_semaphore()
    for dc in range(2):
        for d in range(seqs):
            if dc or d:
                pl.semaphore_signal(
                    barrier, inc=1, device_id=(group + lax.rem(cc + dc, 2), lax.rem(seq + d, seqs)), device_id_type=MESH)
    stages = spread(ctx, seq, nbits, seqs, 1)
    stages_flat = spread(ctx, seq, nbits, seqs, min(nbits, 3))
    met = [device for device, _ in stages_flat[0][1][1:]]
    met += [device for _, others, _ in stages_flat[1:-1] for device, _ in others]
    for device in met:
        pl.semaphore_signal(barrier, inc=1, device_id=device, device_id_type=MESH)
    greeted = 2 * seqs - 1 + len(met)

    lane = lax.broadcasted_iota(jnp.int32, (1, seqs * tok), 1)
    usable = jnp.where(jnp.logical_or(kept_ref[...] == 1, lane < CLS), 0.0, MASKED)
    usable = jnp.where(lax.rem(seq, 2) == 0, usable[0:1, :], usable[1:2, :])
    wide = marks.shape[3]
    sub = lax.broadcasted_iota(jnp.int32, (16, wide), 0)
    for sh in range(seqs):
        piece = jnp.concatenate(
            [usable[:, sh * tok:(sh + 1) * tok], jnp.full((1, wide - tok), MASKED, f32)], axis=1)
        marks[0, sh] = jnp.where(sub == 0, piece, 0.0).astype(bf16)
    stage[:, tokp - 16:tokp, :] = jnp.zeros((copies, 16, width), bf16)
    stage[:, 0:tok, :] = xin[...]

    def out_copy(k, dst):
        b = lax.rem(seq + k, 2)
        return sems.copy(stage.at[b], dst.at[k], (group + seq // 2, 2 * cc + b))

    def scatter(dst):
        moves = [out_copy(0, dst), out_copy(1, dst)]
        moves[1].start()

        @pl.when(jnp.logical_not(stay))
        def _():
            moves[0].start()

        @pl.when(stay)
        def _():
            dst[0] = stage[lax.rem(seq, 2)]

        return moves

    def arrived(moves, k):
        if k:
            moves[k].wait_recv()
        else:
            @pl.when(jnp.logical_not(stay))
            def _():
                moves[0].wait_recv()

    def left(moves):
        moves[1].wait_send()

        @pl.when(jnp.logical_not(stay))
        def _():
            moves[0].wait_send()

    qaug[...] = jnp.zeros_like(qaug)
    gaug[...] = jnp.zeros_like(gaug)
    dext[...] = jnp.zeros_like(dext)
    lane = lax.broadcasted_iota(jnp.int32, (rows, pw), 1)
    sub = lax.broadcasted_iota(jnp.int32, (16, rows), 0)
    for p in range(pairs):
        vaug[p, :, pw:2 * pw] = jnp.where(lane < 2, 1.0, 0.0).astype(bf16)
        vtaug[p, pw:pw + 16, :] = jnp.where(sub == 0, 1.0, 0.0).astype(bf16)
    pl.semaphore_wait(barrier, greeted)
    moves = scatter(xall)
    marks_copy = sems.copy(marks.at[0], marks.at[1], sibling)
    marks_copy.start()

    gain = row_vec(ag_ref)
    shift = row_vec(as_ref)

    def project(pos):
        at = slice(pos * tokp, (pos + 1) * tokp)
        n, _ = norm_parts(xall[pos].astype(f32))
        low = (n * gain + shift).astype(bf16)
        n_ref[at, :] = low
        k = mm(low, wk_ref[...]).astype(bf16)
        v = mm(low, wv_ref[...]).astype(bf16)
        for p in range(pairs):
            kaug[p, at, 0:pw] = k[:, p * pw:(p + 1) * pw]
            vaug[p, at, 0:pw] = v[:, p * pw:(p + 1) * pw]

    forwards = []
    for k in range(2):
        arrived(moves, k)
        forwards.append(sems.copy(xall.at[k], xall.at[2 + k], sibling))
        forwards[k].start()
    for k in range(2):
        project(k)
    left(moves)
    cot_in.wait()
    for b in range(2):
        stage[b, 0:tok, :] = s_ref[b * tok:(b + 1) * tok, :].astype(bf16)
    cot_moves = scatter(cotr)
    marks_copy.wait()
    held = jnp.where(stay, 0, 1)
    unit = jnp.where(
        lax.broadcasted_iota(jnp.int32, (16, pw), 0) == lax.broadcasted_iota(jnp.int32, (16, pw), 1), 1.0, 0.0
    ).astype(bf16)
    for pos in range(4):
        side = cc if pos < 2 else 1 - cc
        mark = marks[held, 2 * side + lax.rem(seq + pos, 2)]
        bias = mm(mark, unit, TN).astype(bf16)[0:tokp, :]
        for p in range(pairs):
            kaug[p, pos * tokp:(pos + 1) * tokp, pw:2 * pw] = bias
    qt = mm(wq_ref[...], n_ref[0:own, :], TT).astype(bf16)
    for p in range(pairs):
        for h in range(2):
            qaug[p, h * hd:(h + 1) * hd, h * head_cols:h * head_cols + own] = qt[p * pw + h * hd:p * pw + (h + 1) * hd, :]
    for k in range(2):
        forwards[k].wait()
        project(2 + k)
    kt[...] = mm(wk_ref[...], n_ref[...], TT).astype(bf16)
    vt = mm(wv_ref[...], n_ref[...], TT).astype(bf16)
    for p in range(pairs):
        vtaug[p, 0:pw, :] = vt[p * pw:(p + 1) * pw, :]

    first = jnp.where(lax.broadcasted_iota(jnp.int32, (pw, TILE), 0) == 0, 1.0, 0.0).astype(bf16)

    cut = (rows - s_more.shape[0]) // 2
    bounds = ((0, cut), (cut, 2 * cut), (2 * cut, rows))
    even = [s_ref.at[a:b] for a, b in bounds]
    odd = [acc.at[0:cut], acc.at[cut:2 * cut], s_more]
    count = pairs * tiles

    def place(t):
        return t // tiles, pl.ds(pl.multiple_of((t % tiles) * TILE, TILE), TILE)

    def score(t, into, c):
        p, at = place(t)
        a, b = bounds[c]
        value = mm(kaug[p, a:b, :], jnp.concatenate([qaug[p, :, at], first], axis=0))
        into[c][...] = value
        return jnp.max(value.reshape((b - a) // 8, 8, TILE), axis=0)

    def weigh(t, scores, top, ahead):
        p, at = place(t)
        top = jnp.max(top, axis=0, keepdims=True)
        tops = []
        total = None
        for c, (a, b) in enumerate(bounds):
            if ahead is not None:
                tops.append(score(t + 1, ahead, c))
            weights = jnp.exp2((scores[c][...] - top) * expo).astype(bf16)
            prob[p, a:b, at] = weights
            part = mm(vtaug[p, :, a:b], weights)
            total = part if total is None else total + part
        rl = 1.0 / total[pw:pw + 1]
        ot_ref[p, :, at] = total[0:pw] * rl
        rl_ref[p, :, at] = rl
        return jnp.maximum(jnp.maximum(tops[0], tops[1]), tops[2]) if tops else None

    def forward(i, top):
        return weigh(2 * i + 1, odd, weigh(2 * i, even, top, odd), even)

    tops = [score(0, even, c) for c in range(3)]
    top = lax.fori_loop(0, count // 2 - 1, forward, jnp.maximum(jnp.maximum(tops[0], tops[1]), tops[2]))
    top = weigh(count - 2, even, top, odd)
    weigh(count - 1, odd, top, None)
    for p in range(pairs):
        for h in range(2):
            att_t[p * pw + h * hd:p * pw + (h + 1) * hd, :] = ot_ref[
                p, h * hd:(h + 1) * hd, h * head_cols:h * head_cols + own
            ].astype(bf16)
    att[...] = jnp.transpose(att_t[...])

    gain2 = row_vec(mg_ref)
    shift2 = row_vec(ms_ref)
    out_bias = row_vec(ob_ref)
    up_bias = row_vec(ub_ref)
    down_bias = row_vec(db_ref)
    arrived(cot_moves, 0)
    arrived(cot_moves, 1)
    left(cot_moves)

    def mlp(i, carry):
        g_up, g_down, g_out, g_gain, g_shift = carry
        at = pl.ds(pl.multiple_of(i * chunk, 16), chunk)
        middle = xall[i].astype(f32) + (mm(att[at, :], wo_ref[...]) + out_bias)
        n, rstd = norm_parts(middle)
        low = (n * gain2 + shift2).astype(bf16)
        att[at, :] = low
        hidden = mm(low, wu_ref[...]) + up_bias
        dist, dens = normal_parts(hidden)
        act = (hidden * dist).astype(bf16)
        act_ref[at, :] = act
        stage[i] = (middle + (mm(act, wd_ref[...]) + down_bias)).astype(bf16)
        cot = cotr[i]
        gh = ((dist + hidden * dens) * mm(cot, wd_ref[...], NT)).astype(bf16)
        gh_ref[at, :] = gh
        e = mm(gh, wu_ref[...], NT)
        back = norm_back(e * gain2, n, rstd)
        s_ref[at, :] = back
        cot = cot.astype(f32)
        gml = (cot + back).astype(bf16)
        gml_ref[at, :] = gml
        return (
            g_up + colsum(gh.astype(f32)), g_down + colsum(cot), g_out + colsum(gml.astype(f32)),
            g_gain + colsum(e * n), g_shift + colsum(e),
        )

    zero = jnp.zeros((1, width), f32)
    sums = lax.fori_loop(0, nchunk, mlp, (jnp.zeros((1, ff), f32), zero, zero, zero, zero))
    small_ref[0:1, :] = sums[1]
    small_ref[1:2, :] = sums[2]
    small_ref[2:3, :] = sums[3]
    small_ref[3:4, :] = sums[4]
    ups = 4 + ff // width
    for j in range(ff // width):
        small_ref[4 + j:5 + j, :] = sums[0][:, j * width:(j + 1) * width]

    cut_at = up16(chunk // 2)
    spans = ((0, cut_at), (cut_at, chunk - cut_at))

    def back_copy(k, dst, sem, part):
        b = lax.rem(seq, 2)
        at = pl.ds(*spans[part])
        return pltpu.make_async_remote_copy(
            src_ref=stage.at[k, at], dst_ref=dst.at[b, at],
            send_sem=ret_send.at[4 * sem + 2 * part + k], recv_sem=ret_recv.at[4 * sem + 2 * part + b],
            device_id=(group + seq // 2, 2 * cc + lax.rem(seq + k, 2)), device_id_type=MESH)

    def own_copy(dst, sem):
        return pltpu.make_async_copy(stage.at[0], dst.at[lax.rem(seq, 2)], local_sems.at[2 + sem])

    def send_block(moves, k, dst, sem, parts=(0, 1)):
        if k:
            for part in parts:
                moves[k][part].start()
            return

        @pl.when(jnp.logical_not(stay))
        def _():
            for part in parts:
                moves[k][part].start()

        @pl.when(stay)
        def _():
            own_copy(dst, sem).start()

    def left_home(moves, dst, sem):
        for move in moves[1]:
            move.wait_send()

        @pl.when(jnp.logical_not(stay))
        def _():
            for move in moves[0]:
                move.wait_send()

        @pl.when(stay)
        def _():
            own_copy(dst, sem).wait()

    def home_again(dst, sem):
        for b in range(2):
            here = jnp.logical_and(stay, lax.rem(seq, 2) == b)

            @pl.when(jnp.logical_not(here))
            def _():
                for part in range(2):
                    at = pl.ds(*spans[part])
                    pltpu.make_async_remote_copy(
                        src_ref=stage.at[b, at], dst_ref=dst.at[b, at], send_sem=ret_send.at[4 * sem + 2 * part + b],
                        recv_sem=ret_recv.at[4 * sem + 2 * part + b], device_id=sibling, device_id_type=MESH).wait_recv()

    out_moves = [[back_copy(k, outr, 0, part) for part in range(2)] for k in range(2)]
    for k in range(2):
        send_block(out_moves, k, outr, 0)

    sets = (ff, ff, 2 * width, width, width)
    halved = (True, True, False, False, False)
    starts = [sum(sets[:j]) for j in range(5)]
    lands = [landing_rows(sets[j], nbits, seqs, halved[j]) for j in range(5)]
    lands = [sum(lands[:j]) for j in range(5)]
    kept = [sets[j] // 2 if halved[j] else sets[j] for j in range(5)]
    kept = [sum(kept[:j]) for j in range(5)]
    sends = (
        act_ref.at[:, 2 * width:3 * width], act_ref.at[:, 3 * width:4 * width],
        gh_ref.at[:, 2 * width:3 * width], gh_ref.at[0:own // 2, 3 * width:4 * width], gh_ref.at[own // 2:own, 3 * width:4 * width])
    written = []

    def write_out(j, src, dst):
        copy = pltpu.make_async_copy(src, dst, local_sems.at[4 + j])
        copy.start()
        written.append(copy)

    def write_small():
        copy = pltpu.make_async_copy(small_ref, small_hbm, local_sems.at[9])
        copy.start()
        written.append(copy)

    steps = [
        reduce_steps(
            sems, stages if halved[j] else stages_flat, sets[j], acc, kept[j], sends[j], recv, lands[j], gat, gat_hbm, starts[j],
            halved[j], partial(write_out, j))
        for j in range(5)
    ]

    def turn(*which):
        for j in which:
            next(steps[j], None)

    def split(j, make, half):
        acc[kept[j]:kept[j] + half, :] = make(cc)
        sends[j][0:half, :] = make(1 - cc).astype(bf16)

    def part(w, count):
        return pl.ds(pl.multiple_of(w * count, 128), count)

    def up_half(w):
        value = mm(att[...], gh_ref[:, part(w, ff // 2)], TN)
        return jnp.concatenate([value[:, j * width:(j + 1) * width] for j in range(ff // width // 2)], axis=0)

    split(0, lambda w: mm(act_ref[:, part(w, ff // 2)], cotr[...].reshape(own, width), TN), ff // 2)
    turn(0)
    split(1, up_half, ff // 2)
    turn(1)
    acc[kept[2]:kept[2] + width, :] = mm(att_t[...], gml_ref[...])

    sub = lax.broadcasted_iota(jnp.int32, (16, own), 0)
    for p in range(pairs):
        for h in range(2):
            lanes = slice(h * head_cols, h * head_cols + own)
            g = mm(wo_ref[p * pw + h * hd:p * pw + (h + 1) * hd, :], gml_ref[...], NT).astype(bf16).astype(f32)
            g = (g * rl_ref[p, :, lanes]).astype(bf16)
            gaug[p, h * hd:(h + 1) * hd, lanes] = g
            delta = -colsum(g.astype(f32) * ot_ref[p, h * hd:(h + 1) * hd, lanes])
            coarse = delta.astype(bf16).astype(f32)
            dext[p, :, lanes] = jnp.where(sub == 0, coarse, jnp.where(sub == 1, delta - coarse, 0.0)).astype(bf16)

    turn(0, 1)
    for p in range(pairs):
        for half in range(2):
            lanes = slice(half * width + p * pw, half * width + (p + 1) * pw)
            act_ref[:, lanes] = mm(prob[p, half * own:(half + 1) * own, :], gaug[p], NT).astype(bf16)
    dv_own, dv_sib = act_ref.at[:, 0:width], act_ref.at[:, width:2 * width]
    dk_own, dk_sib = gh_ref.at[:, 0:width], gh_ref.at[:, width:2 * width]
    acc[kept[2] + width:kept[2] + 2 * width, :] = mm(n_ref[0:own, :], dv_own[...], TN) + mm(n_ref[own:rows, :], dv_sib[...], TN)
    turn(2)
    nothing = jnp.zeros((pw - 16, cols), bf16)

    def backward(p, c):
        a, b = bounds[c]
        right = jnp.concatenate([gaug[p], dext[p], nothing], axis=0)
        ds = prob[p, a:b, :] * mm(vaug[p, a:b, :], right).astype(bf16)
        prob[p, a:b, :] = ds
        part = mm(kt[p * pw:(p + 1) * pw, a:b], ds) * scale
        ot_ref[p] = ot_ref[p] + part if c else part

    backward(0, 0)
    turn(0, 1)
    backward(0, 1)
    backward(0, 2)
    backward(1, 0)
    turn(2)
    backward(1, 1)
    turn(0, 1)
    backward(1, 2)
    for p in range(pairs):
        for h in range(2):
            att_t[p * pw + h * hd:p * pw + (h + 1) * hd, :] = ot_ref[
                p, h * hd:(h + 1) * hd, h * head_cols:h * head_cols + own
            ].astype(bf16)
    att[...] = jnp.transpose(att_t[...])
    acc[kept[3]:kept[3] + width, :] = mm(n_ref[0:own, :], att[...], TN)
    turn(2, 3)
    left_home(out_moves, outr, 0)

    def key_grads(pos):
        half, k = pos // 2, pos % 2
        for p in range(pairs):
            lanes = slice(half * width + p * pw, half * width + (p + 1) * pw)
            gh_ref[k * chunk:(k + 1) * chunk, lanes] = (
                mm(prob[p, pos * chunk:(pos + 1) * chunk, :], qaug[p], NT) * scale).astype(bf16)

    def key_weight(k):
        at = slice(k * chunk, (k + 1) * chunk)
        beyond = slice(own + k * chunk, own + (k + 1) * chunk)
        return mm(n_ref[at, :], dk_own[at, :], TN) + mm(n_ref[beyond, :], dk_sib[at, :], TN)

    e_copies = []
    back_moves = [[back_copy(k, backr, 1, part) for part in range(2)] for k in range(2)]
    sums = (zero, zero)
    for k in range(2):
        at = slice(k * chunk, (k + 1) * chunk)
        key_grads(2 + k)
        gml_ref[at, :] = (mm(dk_sib[at, :], wk_ref[...], NT) + mm(dv_sib[at, :], wv_ref[...], NT)).astype(bf16)
        e_copies.append(sems.copy(gml_ref.at[at], erecv.at[at], sibling))
        e_copies[k].start()
        key_grads(k)
        if k == 0:
            acc[kept[4]:kept[4] + width, :] = key_weight(k)
            turn(0, 1, 2, 3)
        else:
            acc[kept[4]:kept[4] + width, :] += key_weight(k)
            turn(4, 3)
        e = mm(att[at, :], wq_ref[...], NT) + mm(dk_own[at, :], wk_ref[...], NT) + mm(dv_own[at, :], wv_ref[...], NT)
        n, rstd = norm_parts(xall[k].astype(f32))
        e_copies[k].wait()
        e = e + erecv[at, :].astype(f32)
        stage[k] = (s_ref[at, :] + norm_back(e * gain, n, rstd)).astype(bf16)
        sums = (sums[0] + colsum(e * n), sums[1] + colsum(e))
        send_block(back_moves, k, backr, 1, (0,) if k else (0, 1))
    small_ref[ups:ups + 1, :] = sums[0]
    small_ref[ups + 1:ups + 2, :] = sums[1]
    small_ref[ups + 2:, :] = jnp.zeros((small_ref.shape[0] - ups - 2, width), f32)
    steps.append(small_steps(sems, stages_flat, small_ref, ssend, srecv, write_small))
    turn(5)
    turn(4)
    send_block(back_moves, 1, backr, 1, (1,))
    turn(0, 1, 2, 5, 3)
    turn(4, 0, 1, 5)
    turn(4)
    for _ in range(len(stages) * 2):
        turn(5, 4, 0, 1, 2, 3)
    left_home(back_moves, backr, 1)
    home_again(outr, 0)
    home_again(backr, 1)
    for copy in written:
        copy.wait()


def unpack_kernel(cot_hbm, outr_hbm, backr_hbm, gat_hbm, small_hbm, *refs):
    hbm, vec_hbm, vec = refs[:8], refs[8:15], refs[15:22]
    cot_ref, outr, backr, gat, small, xg, wide, up, sq, in_sems, out_sems = refs[22:]
    out, xg_hbm, wq_hbm, wk_hbm, wv_hbm, wo_hbm, wu_hbm, wd_hbm = hbm
    ag, as_, ob, mg, ms, ub, db = vec
    _, tok, width = cot_ref.shape
    ff = wide.shape[0]
    cuts = ((0, ff), (ff, 2 * ff), (2 * ff, 2 * ff + 4 * width))
    ins = [
        pltpu.make_async_copy(src, dst, in_sems.at[k])
        for k, (src, dst) in enumerate(
            [(gat_hbm.at[a:b], gat.at[a:b]) for a, b in cuts]
            + [(outr_hbm, outr), (backr_hbm, backr), (cot_hbm, cot_ref), (small_hbm, small)])
    ]
    for cp in ins:
        cp.start()
    outs = []

    def put(src, dst):
        cp = pltpu.make_async_copy(src, dst, out_sems.at[len(outs)])
        cp.start()
        outs.append(cp)

    ins[0].wait()
    wide[...] = gat[0:ff, :].astype(f32)
    put(wide, wd_hbm)
    ins[1].wait()
    for j in range(ff // width):
        up[:, j * width:(j + 1) * width] = gat[ff + j * width:ff + (j + 1) * width, :].astype(f32)
    put(up, wu_hbm)
    ins[4].wait()
    ins[5].wait()
    xg[...] = cot_ref[...] + backr[:, 0:tok, :].astype(f32)
    put(xg, xg_hbm)
    ins[2].wait()
    for j, dst in enumerate((wo_hbm, wv_hbm, wq_hbm, wk_hbm)):
        at = 2 * ff + j * width
        sq[j] = gat[at:at + width, :].astype(f32)
        put(sq.at[j], dst)
    ins[3].wait()
    out[...] = outr[:, 0:tok, :]
    ins[6].wait()
    for j in range(ff // width):
        ub[0:1, j * width:(j + 1) * width] = small[4 + j:5 + j, :]
    ups = 4 + ff // width
    for j, ref in ((0, db), (1, ob), (2, mg), (3, ms), (ups, ag), (ups + 1, as_)):
        ref[...] = small[j:j + 1, :]
    for src, dst in zip(vec, vec_hbm):
        put(src, dst)
    for cp in outs:
        cp.wait()


def body(nctx, seqs, layer_input, gene_kept, attn_gain, attn_shift, w_query, w_key, w_value, w_out, out_bias,
         mlp_gain, mlp_shift, w_up, up_bias, w_down, down_bias, cotangent):
    copies, tok, width = layer_input.shape
    tokp = up16(tok)
    own = 2 * tokp
    rows = 2 * own
    ff = w_up.shape[1]
    nbits = nctx.bit_length() - 1
    vmem = pl.BlockSpec(memory_space=pltpu.VMEM)
    hbm = pl.BlockSpec(memory_space=pl.ANY)
    head_cols = -(-own // 128) * 128
    cols = 2 * head_cols
    pairs = HEADS // 2
    pw = width // 2
    grad_rows = 2 * ff + 4 * width
    sets = (ff, ff, 2 * width, width, width)
    halved = (True, True, False, False, False)
    landing = sum(landing_rows(r, nbits, seqs, h) for r, h in zip(sets, halved))
    peers = sum((1 << len(bits)) - 1 for bits in bit_groups(nbits, min(nbits, 3))) + seqs - 1
    ncopy = 8 + (2 * len(sets) + 1) * peers
    home = jax.ShapeDtypeStruct((copies, tokp, width), bf16)
    outr, backr, gat, small = pl.pallas_call(
        partial(layer_kernel, nbits, seqs),
        out_shape=(
            home, home,
            jax.ShapeDtypeStruct((grad_rows, width), bf16),
            jax.ShapeDtypeStruct((16, width), f32),
        ),
        in_specs=[vmem, vmem, hbm] + [vmem] * 13,
        out_specs=(hbm,) * 4,
        scratch_shapes=[
            pltpu.VMEM((grad_rows, width), bf16),
            pltpu.VMEM((16, width), f32),
            pltpu.VMEM((copies, tokp, width), bf16),
            pltpu.VMEM((4, tokp, width), bf16),
            pltpu.VMEM((copies, tokp, width), bf16),
            pltpu.VMEM((2, seqs, 16, -(-tokp // 128) * 128), bf16),
            pltpu.VMEM((rows, width), bf16),
            pltpu.VMEM((pairs, pw, cols), bf16),
            pltpu.VMEM((pairs, rows, width), bf16),
            pltpu.VMEM((pairs, rows, width), bf16),
            pltpu.VMEM((width, rows), bf16),
            pltpu.VMEM((pairs, pw + 16, rows), bf16),
            pltpu.VMEM((pairs, rows, cols), bf16),
            pltpu.VMEM((rows, TILE), f32),
            pltpu.VMEM((pairs, pw, cols), f32),
            pltpu.VMEM((pairs, 1, cols), f32),
            pltpu.VMEM((width, own), bf16),
            pltpu.VMEM((own, width), bf16),
            pltpu.VMEM((own, ff), bf16),
            pltpu.VMEM((own, ff), bf16),
            pltpu.VMEM((own, width), bf16),
            pltpu.VMEM((pairs, pw, cols), bf16),
            pltpu.VMEM((pairs, 16, cols), bf16),
            pltpu.VMEM((own, width), bf16),
            pltpu.VMEM((rows - grad_rows // 2, TILE), f32),
            pltpu.VMEM((grad_rows - ff, width), f32),
            pltpu.VMEM((landing, width), bf16),
            pltpu.VMEM((nbits + 1, 16, width), bf16),
            pltpu.VMEM((peers, 16, width), bf16),
            pltpu.SemaphoreType.DMA((10,)),
            pltpu.SemaphoreType.DMA((ncopy,)),
            pltpu.SemaphoreType.DMA((ncopy,)),
            pltpu.SemaphoreType.DMA((8,)),
            pltpu.SemaphoreType.DMA((8,)),
        ],
        compiler_params=pltpu.CompilerParams(collective_id=1, has_side_effects=True, vmem_limit_bytes=63 * 2**20),
        name="layer",
    )(layer_input, gene_kept, cotangent.reshape(copies * tok, width), attn_gain, attn_shift, w_query, w_key, w_value,
      w_out, out_bias, mlp_gain, mlp_shift, w_up, up_bias, w_down, down_bias)
    line = jax.ShapeDtypeStruct((1, width), f32)
    square = jax.ShapeDtypeStruct((width, width), f32)
    whole = [
        jax.ShapeDtypeStruct((copies, tok, width), bf16), jax.ShapeDtypeStruct((copies, tok, width), f32),
        square, square, square, square, jax.ShapeDtypeStruct((width, ff), f32), jax.ShapeDtypeStruct((ff, width), f32),
    ]
    rows_out = [line, line, line, line, line, jax.ShapeDtypeStruct((1, ff), f32), line]
    out, xg, wq, wk, wv, wo, wu, wd, ag, as_, ob, mg, ms, ub, db = pl.pallas_call(
        unpack_kernel,
        out_shape=tuple(whole + rows_out),
        in_specs=[hbm] * 5,
        out_specs=(vmem,) + (hbm,) * 14,
        scratch_shapes=[pltpu.VMEM(v.shape, f32) for v in rows_out] + [
            pltpu.VMEM(cotangent.shape, f32), pltpu.VMEM(home.shape, bf16), pltpu.VMEM(home.shape, bf16),
            pltpu.VMEM((grad_rows, width), bf16), pltpu.VMEM((16, width), f32),
            pltpu.VMEM(cotangent.shape, f32), pltpu.VMEM((ff, width), f32),
            pltpu.VMEM((width, ff), f32), pltpu.VMEM((4, width, width), f32),
            pltpu.SemaphoreType.DMA((7,)), pltpu.SemaphoreType.DMA((15,)),
        ],
        compiler_params=pltpu.CompilerParams(vmem_limit_bytes=63 * 2**20),
        name="unpack",
    )(cotangent, outr, backr, gat, small)
    ag, as_, ob, mg, ms, ub, db = (v.reshape(-1) for v in (ag, as_, ob, mg, ms, ub, db))
    return out, xg, ag, as_, wq, wk, wv, wo, ob, mg, ms, wu, ub, wd, db


def solution(mesh):
    tokens = P("ctx", "seq", None)
    return jax.shard_map(
        partial(body, mesh.shape["ctx"], mesh.shape["seq"]),
        mesh=mesh,
        in_specs=(tokens, P("ctx", None)) + (P(),) * 13 + (tokens,),
        out_specs=(tokens, tokens) + (P(),) * 13,
        check_vma=False,
    )
```
